128 devices in a mesh: seq: 16 (over x, z), head: 8 (over y, core).
Axes of the slice: x: 4, y: 4, z: 4, core: 2. Of those that a mesh axis runs over, the one named last changes fastest.
Arguments:
- x_in: bfloat16 [16384, 8192], P('seq', 'head'), may hold values from -6 to 6
- z_gate: bfloat16 [16384, 8192], P('seq', 'head'), may hold values from -6 to 6
- b_proj: bfloat16 [16384, 1024], P(('seq', 'head')), may hold values from -0.015625 to 0.015625
- c_proj: bfloat16 [16384, 1024], P(('seq', 'head')), may hold values from -6 to 6
- dt_raw: float32 [128, 16384], P('head', 'seq'), may hold values from -1.25 to 5.25
- dt_bias: float32 [128], P('head'), may hold values from -1 to 1
- a_log: float32 [128], P('head'), may hold values from -10 to -3.5
- skip: float32 [128], P('head'), may hold values from 0.5 to 1.5
- norm_weight: float32 [8192], P('head'), may hold values from 0.25 to 1.75
- doc_starts: int32 [16384], P('seq'), may hold values 0 or 1
- grad_out: bfloat16 [16384, 8192], P('seq', 'head'), may hold values from -16 to 16
Outputs:
- grad_x: bfloat16 [16384, 8192], P('seq', 'head')
- grad_z: bfloat16 [16384, 8192], P('seq', 'head')
- grad_b: bfloat16 [16384, 1024], P(('seq', 'head'))
- grad_c: bfloat16 [16384, 1024], P(('seq', 'head'))
- grad_dt: float32 [128, 16384], P('head', 'seq')
- grad_alog: float32 [128], P('head')
- grad_bias: float32 [128], P('head')
- grad_skip: float32 [128], P('head')
- grad_gain: float32 [8192], P('head')
The draws below stay inside these ranges and needn't reach their ends.
All inputs are finite; a program needn't handle non-finite values. No bound on the sum of `doc_starts` on one device may be relied on, other than what follows from the above.
Results may differ from the reference program's by a relative error of at most 0.00165.
Values may be sent and summed in bfloat16 or wider, within the bound.
No kernel may reach another device: no remote copies, remote signals or barrier semaphores. Data moves between devices by JAX's collectives and lax.ppermute only.
A program may use at most 128 MiB of HBM per device.

```python
import jax
import jax.numpy as jnp
from jax import lax

HEADS = 128
HEAD_DIM = 64
STATE = 128
PROJECTION_SETS = 8
SLICE_POSITIONS = 1024
TOKENS = 16384


def draw_dt_raw(key, part):
    key = jax.random.fold_in(key, 7)
    master_seed, document_span_seed = jax.random.split(key)
    tensor_extent = (HEADS, TOKENS)
    starting_level = 0.5 * jax.random.truncated_normal(master_seed, -2.5, 2.5, tensor_extent, jnp.float32)
    document_spans = jax.random.randint(document_span_seed, tensor_extent, 0, SLICE_POSITIONS) < 2
    return starting_level + 4.0 * document_spans.astype(jnp.float32)


def draw_grad_out(key, part):
    key = jax.random.fold_in(key, 11)
    value_key = jax.random.fold_in(key, 0)
    tensor_extent = (TOKENS, HEADS * HEAD_DIM)
    ramp = 1.0 + 2.0 * jnp.arange(TOKENS, dtype=jnp.float32)[:, None] / TOKENS
    values = jax.random.truncated_normal(value_key, -4.0, 4.0, tensor_extent, jnp.float32)
    return (values * ramp).astype(jnp.bfloat16)


def touch_ends(array, rng, least, largest):
    extent = array.shape
    index_at = [jax.random.randint(jax.random.fold_in(rng, axis), (), 0, extent[axis]) for axis in range(len(extent))]
    array = array.at[tuple(index_at)].set(least)
    longest = extent.index(max(extent))
    index_at[longest] = (index_at[longest] + 1) % extent[longest]
    return array.at[tuple(index_at)].set(largest)


def block_levels(rng, shape, cuts, low, high):
    loudness, own = 1.0, jax.random.fold_in(rng, 6)
    for axis_at, shards_of in cuts:
        draws = jnp.exp(jax.random.uniform(jax.random.fold_in(own, axis_at), (shards_of,), jnp.float32, low / len(cuts), high / len(cuts)))
        loudness = loudness * jnp.repeat(draws, shape[axis_at] // shards_of).reshape([-1 if axis == axis_at else 1 for axis in range(len(shape))])
    return loudness


def bell_draw(key, shape, scale, most, cuts=(), kind=jnp.bfloat16):
    loudness = block_levels(key, shape, cuts, -0.22, 0.18) if cuts else 1.0
    drawn = jax.random.normal(key, shape, jnp.float32) * scale * loudness
    return jnp.minimum(jnp.maximum(drawn, -most), most).astype(kind)


def setup_inputs(seed: int = 0) -> dict:
    key_list = jax.random.split(jax.random.key(seed), 12)
    return {
        "x_in": bell_draw(key_list[0], (TOKENS, HEADS * HEAD_DIM), 1.0, 6.0, ((0, 16), (1, 8))),
        "z_gate": bell_draw(key_list[1], (TOKENS, HEADS * HEAD_DIM), 1.0, 6.0, ((0, 16), (1, 8))),
        "b_proj": bell_draw(key_list[2], (TOKENS, PROJECTION_SETS * STATE), (STATE * SLICE_POSITIONS) ** -0.5, 0.015625, ((0, 128),)),
        "c_proj": bell_draw(key_list[3], (TOKENS, PROJECTION_SETS * STATE), 1.0, 6.0, ((0, 128),)),
        "dt_raw": draw_dt_raw(jax.random.fold_in(key_list[11], 71), 0),
        "dt_bias": jnp.clip(jax.random.uniform(key_list[5], (HEADS,), jnp.float32, -1.0, 1.0) * block_levels(key_list[5], (HEADS,), ((0, 8),), -0.4, 0.0), -1.0, 1.0),
        "a_log": jnp.clip(-10.0 + 6.5 * jax.random.uniform(key_list[6], (HEADS,), jnp.float32) ** block_levels(key_list[6], (HEADS,), ((0, 8),), -0.2, 0.2), -10.0, -3.5),
        "skip": jnp.clip(0.5 + 1.0 * jax.random.uniform(key_list[7], (HEADS,), jnp.float32) ** block_levels(key_list[7], (HEADS,), ((0, 8),), -0.2, 0.2), 0.5, 1.5),
        "norm_weight": jnp.clip(1.0 + 0.15 * jax.random.normal(key_list[8], (HEADS * HEAD_DIM,), jnp.float32), 0.25, 1.75),
        "doc_starts": touch_ends((jax.random.randint(key_list[9], (TOKENS,), 0, 2 * SLICE_POSITIONS) < 1).astype(jnp.int32), jax.random.fold_in(key_list[9], 1), 0, 1),
        "grad_out": draw_grad_out(jax.random.fold_in(key_list[11], 71), 0),
    }


EPSILON = 1e-05
PRECISE = lax.Precision.HIGHEST

def block_step(carried, pieces):
    x_block, b_block, c_block, dt_block, rate_block, start_block = pieces
    length = start_block.shape[0]
    cumulative = jnp.cumsum(rate_block, axis=1)
    segment = jnp.cumsum(start_block, dtype=jnp.int32)
    causal = lax.broadcasted_iota(jnp.int32, (length, length), 0) >= lax.broadcasted_iota(jnp.int32, (length, length), 1)
    masked = causal & (segment[:, None] == segment[None, :])
    spread = jnp.where(masked[None], cumulative[:, :, None] - cumulative[:, None, :], 0.0)
    decays = jnp.where(masked[None], jnp.exp(spread), 0.0)
    weight = jnp.where((segment == 0)[None, :], jnp.exp(cumulative), 0.0)
    through = jnp.where(segment[-1] == 0, jnp.exp(cumulative[:, -1]), 0.0)
    intersection = jnp.dot(c_block, b_block.T, precision=PRECISE, preferred_element_type=jnp.float32)
    score_values = decays * intersection[None] * dt_block[:, None, :]
    output = jnp.einsum('kts,skp->tkp', score_values, x_block, precision=PRECISE)
    output = output + jnp.einsum('tn,kpn->tkp', c_block, carried, precision=PRECISE) * weight.T[:, :, None]
    to_end = decays[:, -1, :] * dt_block
    carried = through[:, None, None] * carried + jnp.einsum('ks,skp,sn->kpn', to_end, x_block, b_block, precision=PRECISE)
    return (carried, output)

def group_forward(x_group, z_group, b_group, c_group, dt_group, bias_group, alog_group, skip_group, gain_group, starts):
    tokens = x_group.shape[0]
    heads = dt_group.shape[0]
    length = min(256, SLICE_POSITIONS)
    blocks = tokens // length
    dt_full = jax.nn.softplus(dt_group + bias_group[:, None])
    rate_full = dt_full * (-jnp.exp(alog_group))[:, None]
    x_heads = x_group.reshape(tokens, heads, HEAD_DIM)
    pieces = (x_heads.reshape(blocks, length, heads, HEAD_DIM), b_group.reshape(blocks, length, STATE), c_group.reshape(blocks, length, STATE), dt_full.reshape(heads, blocks, length).transpose(1, 0, 2), rate_full.reshape(heads, blocks, length).transpose(1, 0, 2), starts.reshape(blocks, length))
    initial = jnp.zeros((heads, HEAD_DIM, STATE), jnp.float32)
    _, outputs = lax.scan(jax.checkpoint(block_step), initial, pieces)
    y_full = outputs.reshape(tokens, heads, HEAD_DIM) + skip_group[None, :, None] * x_heads
    gated = (y_full * jax.nn.silu(z_group.reshape(tokens, heads, HEAD_DIM))).reshape(tokens, heads * HEAD_DIM)
    inv_rms = lax.rsqrt(lax.optimization_barrier(jnp.mean(gated * gated, axis=1, keepdims=True)) + EPSILON)
    return gated * inv_rms * gain_group[None, :]

def reference(x_in, z_gate, b_proj, c_proj, dt_raw, dt_bias, a_log, skip, norm_weight, doc_starts, grad_out):
    per_group = HEADS // PROJECTION_SETS
    width = per_group * HEAD_DIM
    stacked = (x_in.reshape(TOKENS, PROJECTION_SETS, width).transpose(1, 0, 2), z_gate.reshape(TOKENS, PROJECTION_SETS, width).transpose(1, 0, 2), b_proj.reshape(TOKENS, PROJECTION_SETS, STATE).transpose(1, 0, 2), c_proj.reshape(TOKENS, PROJECTION_SETS, STATE).transpose(1, 0, 2), dt_raw.reshape(PROJECTION_SETS, per_group, TOKENS), dt_bias.reshape(PROJECTION_SETS, per_group), a_log.reshape(PROJECTION_SETS, per_group), skip.reshape(PROJECTION_SETS, per_group), norm_weight.reshape(PROJECTION_SETS, width), grad_out.reshape(TOKENS, PROJECTION_SETS, width).transpose(1, 0, 2))

    def one_group(pieces):
        x_group, z_group, b_group, c_group, dt_group, bias_group, alog_group, skip_group, gain_group, cotangent = pieces
        primals = (x_group.astype(jnp.float32), z_group.astype(jnp.float32), b_group.astype(jnp.float32), c_group.astype(jnp.float32), dt_group, bias_group, alog_group, skip_group, gain_group)

        def forward_fn(*values):
            return group_forward(*values, doc_starts)
        _, pullback = jax.vjp(forward_fn, *primals)
        grads = pullback(cotangent.astype(jnp.float32))
        return (grads[0].astype(jnp.bfloat16), grads[1].astype(jnp.bfloat16), grads[2].astype(jnp.bfloat16), grads[3].astype(jnp.bfloat16), grads[4], grads[5], grads[6], grads[7], grads[8])
    grads = lax.map(one_group, stacked)
    grad_x = grads[0].transpose(1, 0, 2).reshape(TOKENS, HEADS * HEAD_DIM)
    grad_z = grads[1].transpose(1, 0, 2).reshape(TOKENS, HEADS * HEAD_DIM)
    grad_b = grads[2].transpose(1, 0, 2).reshape(TOKENS, PROJECTION_SETS * STATE)
    grad_c = grads[3].transpose(1, 0, 2).reshape(TOKENS, PROJECTION_SETS * STATE)
    grad_dt = grads[4].reshape(HEADS, TOKENS)
    grad_bias = grads[5].reshape(HEADS)
    grad_alog = grads[6].reshape(HEADS)
    grad_skip = grads[7].reshape(HEADS)
    grad_gain = grads[8].reshape(HEADS * HEAD_DIM)
    return (grad_x, grad_z, grad_b, grad_c, grad_dt, grad_alog, grad_bias, grad_skip, grad_gain)
```

```python
import jax
import jax.numpy as jnp
import numpy as np
from jax import lax
from jax.experimental import pallas as pl
from jax.experimental.pallas import tpu as pltpu
from jax.sharding import PartitionSpec as P

HEADS = 128
HEAD_DIM = 64
STATE = 128
PROJECTION_SETS = 8
EPSILON = 1e-05

T = 1024
H = 16
W = H * HEAD_DIM
L = 256
C = T // L
SEQ = 16
GRP = 8
ROWS = STATE // SEQ
F32 = jnp.float32
BF16 = jnp.bfloat16
STEP = 16

THR, PRE, SUF, KAP, TABLE = 0, 4, 9, 13, 24

NN = (((1,), (0,)), ((), ()))
NT = (((1,), (1,)), ((), ()))
TN = (((0,), (0,)), ((), ()))


def dot(a, b, dims):
    return lax.dot_general(a, b, dims, preferred_element_type=F32)


def split2(a):
    hi = a.astype(BF16)
    return hi, (a - hi.astype(F32)).astype(BF16)


def split3(a):
    hi, mid = split2(a)
    lo = (a - hi.astype(F32) - mid.astype(F32)).astype(BF16)
    return hi, mid, lo


def dot2(a, b, dims):
    return dot(a, b[0], dims) + dot(a, b[1], dims)


def dot3(a, b, dims):
    return dot(a[0], b[0], dims) + dot(a[0], b[1], dims) + dot(a[1], b[0], dims)


def rows_loop(body):
    def step(i, carry):
        body(pl.ds(pl.multiple_of(i * STEP, STEP), STEP))
        return carry

    lax.fori_loop(0, L // STEP, step, 0)


def prep_kernel(dt_ref, par_ref, st_ref, e3_ref, pk_ref, rf_ref, mask_ref, me_ref, mw_ref, thx_ref):
    bias = par_ref[:, 0:1]
    nega = -jnp.exp(par_ref[:, 1:2])
    row = lax.broadcasted_iota(jnp.int32, (L, L), 0)
    col = lax.broadcasted_iota(jnp.int32, (L, L), 1)
    tri = (row <= col).astype(F32).astype(BF16)
    causal = row >= col
    first = lax.broadcasted_iota(jnp.int32, (H, L), 0) == 0
    lane = lax.broadcasted_iota(jnp.int32, (H, 128), 1)
    ones = jnp.ones((H, L), BF16)
    thr, kap = [], []
    for c in range(C):
        at = slice(c * L, (c + 1) * L)
        pre = dt_ref[:, at] + bias
        dt = jax.nn.softplus(pre)
        rf_ref[0:H, at] = dt
        rf_ref[H : 2 * H, at] = jax.nn.sigmoid(pre)
        rate = dt * nega
        parts = dot(jnp.concatenate(split3(rate), 0), tri, NN)
        cum = parts[0:H] + parts[H : 2 * H] + parts[2 * H : 3 * H]
        starts = jnp.broadcast_to(st_ref[:, at].astype(F32), (H, L))
        seg = dot(starts.astype(BF16), tri, NN)
        cum_end = cum[:, L - 1 : L]
        seg_end = seg[:, L - 1 : L]
        half = 0.5 * cum_end
        alpha = jnp.exp(cum - half)
        beta = jnp.exp(half - cum)
        pk_ref[0:H, at], pk_ref[H : 2 * H, at] = split2(alpha)
        pk_ref[2 * H : 3 * H, at], pk_ref[3 * H : 4 * H, at] = split2(dt * beta)
        seg_first = jnp.where(first, seg, 0.0).astype(BF16)
        seg_col = dot(seg_first, ones, TN)
        mask = causal & (seg_col == seg[0:1, :])
        mask_ref[at, :] = mask.astype(F32).astype(BF16)
        to_end = jnp.where(first & (seg == seg_end), 1.0, 0.0).astype(BF16)
        from_start = jnp.where(first & (seg == 0.0), 1.0, 0.0).astype(BF16)
        me_ref[at, :] = dot(to_end, ones[:, :128], TN).astype(BF16)
        mw_ref[at, :] = dot(from_start, ones[:, :128], TN).astype(BF16)
        thr.append(jnp.where(seg_end == 0.0, jnp.exp(cum_end), 0.0))
        kap.append(jnp.exp(half))
    columns = list(thr)
    passed = jnp.ones((H, 1), F32)
    for c in range(C):
        columns.append(passed)
        passed = passed * thr[c]
    columns.append(passed)
    after = [None] * C
    passed = jnp.ones((H, 1), F32)
    for c in reversed(range(C)):
        after[c] = passed
        passed = passed * thr[c]
    columns += after + kap
    table = jnp.zeros((H, 128), F32)
    for k, v in enumerate(columns):
        table = jnp.where(lane == k, v, table)
    wide = dot(jnp.concatenate(split3(table), 0), e3_ref[...], TN)
    thx_ref[...] = wide[0:TABLE]


def table_row(thx_ref, base):
    return thx_ref[pl.ds(base, 1), :]


def expand_alpha(pk_ref, e3_ref):
    return dot(pk_ref[0 : 2 * H, :], e3_ref[0 : 2 * H, :], TN)


def expand_dtbeta(pk_ref, e3_ref):
    return dot(pk_ref[2 * H : 4 * H, :], e3_ref[0 : 2 * H, :], TN)


def states_kernel(x_ref, bc_ref, me_ref, pk_ref, e3_ref, thx_ref, sloc_ref, pay_ref, acc, ex, hi, lo):
    c = pl.program_id(0)

    @pl.when(c == 0)
    def _():
        acc[...] = jnp.zeros_like(acc)

    ex[...] = expand_dtbeta(pk_ref, e3_ref)

    def scale(at):
        hi[at, :], lo[at, :] = split2(x_ref[at, :].astype(F32) * ex[at, :])

    rows_loop(scale)
    b = bc_ref[:, :STATE] * me_ref[...]
    new = dot2(b, (hi[...], lo[...]), TN)
    acc[...] = table_row(thx_ref, THR + c) * acc[...] + table_row(thx_ref, KAP + c) * new
    sloc_ref[0] = acc[...]

    @pl.when(c == C - 1)
    def _():
        pay_ref[:, :W] = acc[...]
        total = thx_ref[PRE + C : PRE + C + 1, :]
        block = jnp.concatenate([total[:, 128 * r : 128 * (r + 1)] for r in range(ROWS)], 0)
        for d in range(SEQ):
            pay_ref[ROWS * d : ROWS * (d + 1), W:] = block


def through_row(got_ref, j):
    block = got_ref[ROWS * j : ROWS * (j + 1), W:]
    return jnp.concatenate([block[r : r + 1, :] for r in range(ROWS)], 1)


def scan_forward_kernel(got_ref, out_ref):
    acc = jnp.zeros((ROWS, W), F32)
    for j in range(SEQ):
        at = slice(ROWS * j, ROWS * (j + 1))
        out_ref[at, :] = acc
        acc = through_row(got_ref, j) * acc + got_ref[at, :W]


def scan_backward_kernel(got_ref, forward_ref, out_ref):
    acc = jnp.zeros((ROWS, W), F32)
    for j in reversed(range(SEQ)):
        at = slice(ROWS * j, ROWS * (j + 1))
        out_ref[at, :] = acc
        acc = through_row(forward_ref, j) * acc + got_ref[at, :]


def within_kernel(
    x_ref, bc_ref, mask_ref, mw_ref, pk_ref, e3_ref, thx_ref, sloc_ref, ys_ref, al, ex, hi, lo, res
):
    c = pl.program_id(0)
    ex[...] = expand_dtbeta(pk_ref, e3_ref)
    al[...] = expand_alpha(pk_ref, e3_ref)

    def scale(at):
        hi[at, :], lo[at, :] = split2(x_ref[at, :].astype(F32) * ex[at, :])

    rows_loop(scale)
    cc = bc_ref[:, STATE:]
    g = split2(dot(cc, bc_ref[:, :STATE], NT) * mask_ref[...].astype(F32))
    seen = jnp.where(c > 0, 1.0, 0.0) * table_row(thx_ref, KAP + c)
    state = split2(seen * sloc_ref[0])
    res[...] = dot3(g, (hi[...], lo[...]), NN) + dot2(cc * mw_ref[...], state, NN)

    def finish(at):
        ys_ref[at, :] = al[at, :] * res[at, :]

    rows_loop(finish)


def norm_kernel(
    ys_ref, x_ref, z_ref, go_ref, bc_ref, mw_ref, pk_ref, e3_ref, thx_ref, vec_ref, sin_ref,
    gy_ref, gz_ref, dloc_ref, r_ref, pay_ref, sums_ref, acc, gain_acc, skip_acc, al, res, hi, lo, rhi, rlo,
):
    step = pl.program_id(0)
    c = C - 1 - step

    @pl.when(step == 0)
    def _():
        acc[...] = jnp.zeros_like(acc)
        gain_acc[...] = jnp.zeros_like(gain_acc)
        skip_acc[...] = jnp.zeros_like(skip_acc)

    al[...] = expand_alpha(pk_ref, e3_ref)
    cm = bc_ref[:, STATE:] * mw_ref[...]
    kappa = table_row(thx_ref, KAP + c)
    state = split2((kappa * table_row(thx_ref, PRE + c)) * sin_ref[...])
    res[...] = dot2(cm, state, NN)
    gain = vec_ref[0:1, :]
    skip = vec_ref[1:2, :]

    def body(at):
        alpha = al[at, :]
        x = x_ref[at, :].astype(F32)
        z = z_ref[at, :].astype(F32)
        out = go_ref[at, :].astype(F32)
        ys = ys_ref[at, :] + alpha * res[at, :]
        y = ys + skip * x
        logistic = jax.nn.sigmoid(z)
        silu = z * logistic
        gated = y * silu
        inv = lax.rsqrt(jnp.sum(gated * gated, axis=1, keepdims=True) * (1.0 / W) + EPSILON)
        normed = gated * inv
        grad_normed = out * gain
        k = jnp.sum(grad_normed * normed, axis=1, keepdims=True) * (1.0 / W)
        grad_gated = inv * (grad_normed - normed * k)
        gy = grad_gated * silu
        gz = grad_gated * y * (logistic + silu * (1.0 - logistic))
        gz_ref[at, :] = gz.astype(BF16)
        gy_ref[at, :] = gy
        gpart = out * normed
        spart = gy * x
        gain_acc[...] += gpart[0:8] + gpart[8:16]
        skip_acc[...] += spart[0:8] + spart[8:16]
        hi[at, :], lo[at, :] = split2(gy * alpha)
        rhi[at, :], rlo[at, :] = split2(gy * ys)

    rows_loop(body)
    r_ref[...] = dot2(e3_ref[0:H, :], (rhi[...], rlo[...]), NT)
    back = kappa * dot2(cm, (hi[...], lo[...]), TN)
    dloc_ref[0] = acc[...]
    acc[...] = back + table_row(thx_ref, THR + c) * acc[...]

    @pl.when(step == C - 1)
    def _():
        pay_ref[...] = acc[...]
        sums_ref[0:1, :] = jnp.sum(gain_acc[...], axis=0, keepdims=True)
        sums_ref[1:2, :] = jnp.sum(skip_acc[...], axis=0, keepdims=True)
        sums_ref[2:8, :] = jnp.zeros((6, W), F32)


def local_kernel(
    gy_ref, x_ref, bc_ref, mask_ref, me_ref, mw_ref, pk_ref, e3_ref, thx_ref, vec_ref, sloc_ref, sin_ref, dloc_ref,
    gx_ref, u_ref, gbc_ref, al, ex, ghi, glo, xhi, xlo, res, rhi, rlo,
):
    c = pl.program_id(0)
    ex[...] = expand_dtbeta(pk_ref, e3_ref)
    al[...] = expand_alpha(pk_ref, e3_ref)

    def scale(at):
        xhi[at, :], xlo[at, :] = split2(x_ref[at, :].astype(F32) * ex[at, :])
        ghi[at, :], glo[at, :] = split2(gy_ref[at, :] * al[at, :])

    rows_loop(scale)
    b = bc_ref[:, :STATE]
    cc = bc_ref[:, STATE:]
    me = me_ref[...]
    mw = mw_ref[...]
    mask = mask_ref[...].astype(F32)
    gys = (ghi[...], glo[...])
    xs = (xhi[...], xlo[...])
    g = split2(dot(cc, b, NT) * mask)
    q = split2(dot3(gys, xs, NT) * mask)
    kappa = table_row(thx_ref, KAP + c)
    seen = jnp.where(c > 0, 1.0, 0.0) * kappa
    state = split2(seen * sloc_ref[0] + (kappa * table_row(thx_ref, PRE + c)) * sin_ref[...])
    dstate = split2(kappa * dloc_ref[0])
    res[...] = dot3(g, gys, TN) + dot2(b * me, dstate, NN)
    gb = dot(q[0], cc, TN) + dot(q[1], cc, TN) + me.astype(F32) * dot3(xs, dstate, NT)
    gc = dot(q[0], b, NN) + dot(q[1], b, NN) + mw.astype(F32) * dot3(gys, state, NT)
    gbc_ref[:, :STATE] = gb
    gbc_ref[:, STATE:] = gc
    skip = vec_ref[1:2, :]

    def finish(at):
        v = res[at, :]
        scaled = ex[at, :] * v
        gx_ref[at, :] = scaled + skip * gy_ref[at, :]
        rhi[at, :], rlo[at, :] = split2(scaled * x_ref[at, :].astype(F32))

    rows_loop(finish)
    u_ref[...] = dot2(e3_ref[0:H, :], (rhi[...], rlo[...]), NT)


def final_kernel(
    gx_ref, x_ref, bc_ref, me_ref, pk_ref, rf_ref, e3_ref, thx_ref, par_ref, sloc_ref, sin_ref, dloc_ref, din_ref,
    u_ref, r_ref, gbc_ref, sums_ref, gxo_ref, gdt_ref, gbco_ref, par_out_ref, ex, xhi, xlo, res, rhi, rlo, cols,
):
    c = pl.program_id(0)

    @pl.when(c == 0)
    def _():
        cols[...] = jnp.zeros_like(cols)

    ex[...] = expand_dtbeta(pk_ref, e3_ref)
    kappa = table_row(thx_ref, KAP + c)
    suffix = table_row(thx_ref, SUF + c)
    dstate = split2((kappa * suffix) * din_ref[...])
    me = me_ref[...]
    res[...] = dot2(bc_ref[:, :STATE] * me, dstate, NN)

    def body(at):
        xs = x_ref[at, :].astype(F32) * ex[at, :]
        xhi[at, :], xlo[at, :] = split2(xs)
        v = res[at, :]
        gxo_ref[at, :] = (gx_ref[at, :] + ex[at, :] * v).astype(BF16)
        rhi[at, :], rlo[at, :] = split2(xs * v)

    rows_loop(body)
    heads = e3_ref[0:H, :]
    gb = gbc_ref[:, :STATE] + me.astype(F32) * dot3((xhi[...], xlo[...]), dstate, NT)
    gbco_ref[:, :STATE] = gb.astype(BF16)
    gbco_ref[:, STATE:] = gbc_ref[:, STATE:].astype(BF16)
    u = u_ref[...] + dot2(heads, (rhi[...], rlo[...]), NT)
    state = sloc_ref[0] + table_row(thx_ref, PRE + 1 + c) * sin_ref[...]
    grad = dloc_ref[0] + suffix * din_ref[...]
    ends = jnp.broadcast_to(jnp.sum(state * grad, axis=0, keepdims=True), (H, W))
    end = sum(dot(heads, part, NT) for part in split3(ends))[:, 0:1]
    dt = rf_ref[0:H, :]
    grad_cum = r_ref[...] - u
    row = lax.broadcasted_iota(jnp.int32, (L, L), 0)
    col = lax.broadcasted_iota(jnp.int32, (L, L), 1)
    tri = (row >= col).astype(F32).astype(BF16)
    parts = dot(jnp.concatenate(split3(grad_cum), 0), tri, NN)
    grad_rate = parts[0:H] + parts[H : 2 * H] + parts[2 * H : 3 * H] + end
    nega = -jnp.exp(par_ref[:, 1:2])
    grad_dt = (u / dt + grad_rate * nega) * rf_ref[H : 2 * H, :]
    gdt_ref[...] = grad_dt
    alog_part = jnp.sum(grad_rate * dt, axis=1, keepdims=True) * nega
    bias_part = jnp.sum(grad_dt, axis=1, keepdims=True)
    lane = lax.broadcasted_iota(jnp.int32, (H, 128), 1)
    cols[...] += jnp.where(lane == 1, alog_part, 0.0) + jnp.where(lane == 2, bias_part, 0.0)

    @pl.when(c == C - 1)
    def _():
        skips = jnp.broadcast_to(sums_ref[1:2, :], (H, W))
        skip_part = sum(dot(heads, part, NT) for part in split3(skips))[:, 0:1]
        right = cols[...] + jnp.where(lane == 0, skip_part, 0.0)
        gains = sums_ref[0:1, :]
        left = jnp.concatenate([gains[:, 128 * r : 128 * (r + 1)] for r in range(8)], 0)
        left = jnp.concatenate([left, jnp.zeros((8, 128), F32)], 0)
        for d in range(SEQ):
            par_out_ref[H * d : H * (d + 1), :128] = left
            par_out_ref[H * d : H * (d + 1), 128:] = right


def head_matrix():
    one = np.arange(W)[None, :] // HEAD_DIM == np.arange(H)[:, None]
    return jnp.asarray(np.concatenate([one, one, one], 0), BF16)


def whole(shape):
    return pl.BlockSpec(shape, lambda i: (0,) * len(shape))


def shard_body(
    x_in, z_gate, b_proj, c_proj, dt_raw, dt_bias, a_log, skip, norm_weight, doc_starts, grad_out
):
    e3 = head_matrix()
    par = jnp.pad(jnp.stack([dt_bias, a_log], 1), ((0, 0), (0, 126)))
    vec = jnp.pad(
        jnp.stack([norm_weight, jnp.repeat(skip, HEAD_DIM)], 0), ((0, 6), (0, 0))
    )
    starts = doc_starts.reshape(1, T)
    mine = jnp.concatenate(
        [b_proj.reshape(128, GRP, STATE), c_proj.reshape(128, GRP, STATE)], 2
    ).transpose(1, 0, 2)
    bc = lax.all_to_all(mine, "head", split_axis=0, concat_axis=0, tiled=True).reshape(T, 2 * STATE)

    def call(kernel, outs, out_specs, in_specs, scratch, flops, name):
        return pl.pallas_call(
            kernel,
            grid=(C,),
            out_shape=outs,
            in_specs=in_specs,
            out_specs=out_specs,
            scratch_shapes=scratch,
            compiler_params=pltpu.CompilerParams(
                dimension_semantics=("arbitrary",), vmem_limit_bytes=40 * 2**20
            ),
            cost_estimate=pl.CostEstimate(flops=flops, bytes_accessed=8 * 2**20, transcendentals=0),
            name=name,
        )

    sds = jax.ShapeDtypeStruct
    pk, rf, mask, me, mw, thx = pl.pallas_call(
        prep_kernel,
        out_shape=(
            sds((4 * H, T), BF16),
            sds((2 * H, T), F32),
            sds((T, L), BF16),
            sds((T, 128), BF16),
            sds((T, 128), BF16),
            sds((TABLE, W), F32),
        ),
        compiler_params=pltpu.CompilerParams(vmem_limit_bytes=40 * 2**20),
        name="prep",
    )(dt_raw, par, starts, e3)

    def tok(width, flip=False):
        return pl.BlockSpec((L, width), (lambda i: (C - 1 - i, 0)) if flip else (lambda i: (i, 0)))

    def rowf(rows, flip=False):
        return pl.BlockSpec((rows, L), (lambda i: (0, C - 1 - i)) if flip else (lambda i: (0, i)))

    state_at = pl.BlockSpec((1, STATE, W), lambda i: (i, 0, 0))
    state_before = pl.BlockSpec((1, STATE, W), lambda i: (jnp.maximum(i - 1, 0), 0, 0))
    state_flip = pl.BlockSpec((1, STATE, W), lambda i: (C - 1 - i, 0, 0))
    e3_spec = whole((3 * H, W))
    thx_spec = whole((TABLE, W))
    vec_spec = whole((8, W))
    sin_spec = whole((STATE, W))
    big = pltpu.VMEM((L, W), F32)
    half = pltpu.VMEM((L, W), BF16)
    unit = 2 * T * L * W

    sloc, pay = call(
        states_kernel,
        (sds((C, STATE, W), F32), sds((STATE, W + 128), F32)),
        (state_at, whole((STATE, W + 128))),
        [tok(W), tok(2 * STATE), tok(128), rowf(4 * H), e3_spec, thx_spec],
        [pltpu.VMEM((STATE, W), F32), big, half, half],
        2 * unit,
        "states",
    )(x_in, bc, me, pk, e3, thx)

    def exchange(v):
        return lax.all_to_all(v, "seq", split_axis=0, concat_axis=0, tiled=True)

    got = exchange(pay)
    before = pl.pallas_call(
        scan_forward_kernel, out_shape=sds((STATE, W), F32), name="scan_forward"
    )(got)
    sin = exchange(before)

    ys = call(
        within_kernel,
        sds((T, W), F32),
        tok(W),
        [tok(W), tok(2 * STATE), tok(L), tok(128), rowf(4 * H), e3_spec, thx_spec, state_before],
        [big, big, half, half, big],
        6 * unit,
        "within",
    )(x_in, bc, mask, mw, pk, e3, thx, sloc)

    gy, gz, dloc, r, back, sums = call(
        norm_kernel,
        (
            sds((T, W), F32),
            sds((T, W), BF16),
            sds((C, STATE, W), F32),
            sds((H, T), F32),
            sds((STATE, W), F32),
            sds((8, W), F32),
        ),
        (tok(W, True), tok(W, True), state_flip, rowf(H, True), sin_spec, vec_spec),
        [
            tok(W, True), tok(W, True), tok(W, True), tok(W, True), tok(2 * STATE, True), tok(128, True),
            rowf(4 * H, True), e3_spec, thx_spec, vec_spec, sin_spec,
        ],
        [
            pltpu.VMEM((STATE, W), F32), pltpu.VMEM((8, W), F32), pltpu.VMEM((8, W), F32),
            big, big, half, half, half, half,
        ],
        6 * unit,
        "norm",
    )(ys, x_in, z_gate, grad_out, bc, mw, pk, e3, thx, vec, sin)

    got_back = exchange(back)
    behind = pl.pallas_call(
        scan_backward_kernel, out_shape=sds((STATE, W), F32), name="scan_backward"
    )(got_back, got)
    din = exchange(behind)

    gx_local, u, gbc_local = call(
        local_kernel,
        (sds((T, W), F32), sds((H, T), F32), sds((T, 2 * STATE), F32)),
        (tok(W), rowf(H), tok(2 * STATE)),
        [
            tok(W), tok(W), tok(2 * STATE), tok(L), tok(128), tok(128), rowf(4 * H), e3_spec, thx_spec, vec_spec,
            state_before, sin_spec, state_at,
        ],
        [big, big, half, half, half, half, big, half, half],
        12 * unit,
        "local",
    )(gy, x_in, bc, mask, me, mw, pk, e3, thx, vec, sloc, sin, dloc)

    grad_x, grad_dt, gbc, params = call(
        final_kernel,
        (sds((T, W), BF16), sds((H, T), F32), sds((T, 2 * STATE), BF16), sds((SEQ * H, 256), F32)),
        (tok(W), rowf(H), tok(2 * STATE), whole((SEQ * H, 256))),
        [
            tok(W), tok(W), tok(2 * STATE), tok(128), rowf(4 * H), rowf(2 * H), e3_spec, thx_spec, whole((H, 128)),
            state_at, sin_spec, state_at, sin_spec, rowf(H), rowf(H), tok(2 * STATE), vec_spec,
        ],
        [big, half, half, big, half, half, pltpu.VMEM((H, 128), F32)],
        5 * unit,
        "final",
    )(gx_local, x_in, bc, me, pk, rf, e3, thx, par, sloc, sin, dloc, din, u, r, gbc_local, sums)

    back_bc = lax.all_to_all(
        gbc.reshape(GRP, 128, 2 * STATE), "head", split_axis=0, concat_axis=0, tiled=True
    )
    grad_b = back_bc[:, :, :STATE].transpose(1, 0, 2).reshape(128, GRP * STATE)
    grad_c = back_bc[:, :, STATE:].transpose(1, 0, 2).reshape(128, GRP * STATE)
    summed = jnp.sum(exchange(params).reshape(SEQ, H, 256), axis=0)
    grad_gain = summed[:8, :128].reshape(W)
    grad_skip, grad_alog, grad_bias = summed[:, 128], summed[:, 129], summed[:, 130]
    return (grad_x, gz, grad_b, grad_c, grad_dt, grad_alog, grad_bias, grad_skip, grad_gain)


def solution(mesh):
    in_specs = (
        P("seq", "head"),
        P("seq", "head"),
        P(("seq", "head"), None),
        P(("seq", "head"), None),
        P("head", "seq"),
        P("head"),
        P("head"),
        P("head"),
        P("head"),
        P("seq"),
        P("seq", "head"),
    )
    out_specs = (
        P("seq", "head"),
        P("seq", "head"),
        P(("seq", "head"), None),
        P(("seq", "head"), None),
        P("head", "seq"),
        P("head"),
        P("head"),
        P("head"),
        P("head"),
    )
    return jax.shard_map(shard_body, mesh=mesh, in_specs=in_specs, out_specs=out_specs, check_vma=False)
```

```python
import functools

import jax
import jax.numpy as jnp
import numpy as np
from jax import lax
from jax.experimental import pallas as pl
from jax.experimental.pallas import tpu as pltpu
from jax.sharding import PartitionSpec as P

HEADS = 128
HEAD_DIM = 64
STATE = 128
PROJECTION_SETS = 8
EPSILON = 1e-05

T = 1024
H = 16
W = H * HEAD_DIM
L = 256
C = T // L
SEQ = 16
GRP = 8
ROWS = STATE // SEQ
F32 = jnp.float32
BF16 = jnp.bfloat16
STEP = 16

THR, PRE, SUF, KAP, TABLE = 0, 4, 9, 13, 24

NN = (((1,), (0,)), ((), ()))
NT = (((1,), (1,)), ((), ()))
TN = (((0,), (0,)), ((), ()))


def dot(a, b, dims):
    return lax.dot_general(a, b, dims, preferred_element_type=F32)


def split2(a):
    hi = a.astype(BF16)
    return hi, (a - hi.astype(F32)).astype(BF16)


def split3(a):
    hi, mid = split2(a)
    lo = (a - hi.astype(F32) - mid.astype(F32)).astype(BF16)
    return hi, mid, lo


def dot2(a, b, dims):
    return dot(a, b[0], dims) + dot(a, b[1], dims)


def dot3(a, b, dims):
    return dot(a[0], b[0], dims) + dot(a[0], b[1], dims) + dot(a[1], b[0], dims)


def rows_loop(body, unroll=16):
    def step(i, carry):
        body(pl.ds(pl.multiple_of(i * STEP, STEP), STEP))
        return carry

    lax.fori_loop(0, L // STEP, step, 0, unroll=unroll)


def prep_kernel(dt_ref, par_ref, st_ref, e3_ref, pk_ref, rf_ref, mask_ref, me_ref, mw_ref, thx_ref):
    bias = par_ref[:, 0:1]
    nega = -jnp.exp(par_ref[:, 1:2])
    row = lax.broadcasted_iota(jnp.int32, (L, L), 0)
    col = lax.broadcasted_iota(jnp.int32, (L, L), 1)
    tri = (row <= col).astype(F32).astype(BF16)
    causal = row >= col
    first = lax.broadcasted_iota(jnp.int32, (H, L), 0) == 0
    lane = lax.broadcasted_iota(jnp.int32, (H, 128), 1)
    ones = jnp.ones((H, L), BF16)
    thr, kap = [], []
    for c in range(C):
        at = slice(c * L, (c + 1) * L)
        pre = dt_ref[:, at] + bias
        dt = jax.nn.softplus(pre)
        rf_ref[0:H, at] = dt
        rf_ref[H : 2 * H, at] = jax.nn.sigmoid(pre)
        rate = dt * nega
        parts = dot(jnp.concatenate(split3(rate), 0), tri, NN)
        cum = parts[0:H] + parts[H : 2 * H] + parts[2 * H : 3 * H]
        starts = jnp.broadcast_to(st_ref[:, at].astype(F32), (H, L))
        seg = dot(starts.astype(BF16), tri, NN)
        cum_end = cum[:, L - 1 : L]
        seg_end = seg[:, L - 1 : L]
        half = 0.5 * cum_end
        alpha = jnp.exp(cum - half)
        beta = jnp.exp(half - cum)
        pk_ref[0:H, at], pk_ref[H : 2 * H, at] = split2(alpha)
        pk_ref[2 * H : 3 * H, at], pk_ref[3 * H : 4 * H, at] = split2(dt * beta)
        seg_first = jnp.where(first, seg, 0.0).astype(BF16)
        seg_col = dot(seg_first, ones, TN)
        mask = causal & (seg_col == seg[0:1, :])
        mask_ref[at, :] = mask.astype(F32).astype(BF16)
        to_end = jnp.where(first & (seg == seg_end), 1.0, 0.0).astype(BF16)
        from_start = jnp.where(first & (seg == 0.0), 1.0, 0.0).astype(BF16)
        me_ref[at, :] = dot(to_end, ones[:, :128], TN).astype(BF16)
        mw_ref[at, :] = dot(from_start, ones[:, :128], TN).astype(BF16)
        thr.append(jnp.where(seg_end == 0.0, jnp.exp(cum_end), 0.0))
        kap.append(jnp.exp(half))
    columns = list(thr)
    passed = jnp.ones((H, 1), F32)
    for c in range(C):
        columns.append(passed)
        passed = passed * thr[c]
    columns.append(passed)
    after = [None] * C
    passed = jnp.ones((H, 1), F32)
    for c in reversed(range(C)):
        after[c] = passed
        passed = passed * thr[c]
    columns += after + kap
    table = jnp.zeros((H, 128), F32)
    for k, v in enumerate(columns):
        table = jnp.where(lane == k, v, table)
    wide = dot(jnp.concatenate(split3(table), 0), e3_ref[...], TN)
    thx_ref[...] = wide[0:TABLE]


def table_row(thx_ref, base):
    return thx_ref[pl.ds(base, 1), :]


def expand_alpha(pk_ref, e3_ref):
    return dot(pk_ref[0 : 2 * H, :], e3_ref[0 : 2 * H, :], TN)


def expand_dtbeta(pk_ref, e3_ref):
    return dot(pk_ref[2 * H : 4 * H, :], e3_ref[0 : 2 * H, :], TN)


def states_kernel(x_ref, bc_ref, me_ref, pk_ref, e3_ref, thx_ref, sloc_ref, pay_ref, acc, ex, hi, lo):
    c = pl.program_id(0)

    @pl.when(c == 0)
    def _():
        acc[...] = jnp.zeros_like(acc)

    ex[...] = expand_dtbeta(pk_ref, e3_ref)

    def scale(at):
        hi[at, :], lo[at, :] = split2(x_ref[at, :].astype(F32) * ex[at, :])

    rows_loop(scale)
    b = bc_ref[:, :STATE] * me_ref[...]
    new = dot2(b, (hi[...], lo[...]), TN)
    acc[...] = table_row(thx_ref, THR + c) * acc[...] + table_row(thx_ref, KAP + c) * new
    sloc_ref[0] = acc[...]

    @pl.when(c == C - 1)
    def _():
        pay_ref[:, :W] = acc[...]
        total = thx_ref[PRE + C : PRE + C + 1, :]
        block = jnp.concatenate([total[:, 128 * r : 128 * (r + 1)] for r in range(ROWS)], 0)
        for d in range(SEQ):
            pay_ref[ROWS * d : ROWS * (d + 1), W:] = block


def through_row(got_ref, j):
    block = got_ref[ROWS * j : ROWS * (j + 1), W:]
    return jnp.concatenate([block[r : r + 1, :] for r in range(ROWS)], 1)


def scan_forward_kernel(got_ref, out_ref):
    acc = jnp.zeros((ROWS, W), F32)
    for j in range(SEQ):
        at = slice(ROWS * j, ROWS * (j + 1))
        out_ref[at, :] = acc
        acc = through_row(got_ref, j) * acc + got_ref[at, :W]


def scan_backward_kernel(got_ref, forward_ref, out_ref):
    acc = jnp.zeros((ROWS, W), F32)
    for j in reversed(range(SEQ)):
        at = slice(ROWS * j, ROWS * (j + 1))
        out_ref[at, :] = acc
        acc = through_row(forward_ref, j) * acc + got_ref[at, :]


def within_kernel(
    first, x_ref, bc_ref, mask_ref, mw_ref, pk_ref, e3_ref, thx_ref, sloc_ref, *refs
):
    ys_ref, al, ex, hi, lo, res = refs[-6:]
    c = pl.program_id(0) + first
    ex[...] = expand_dtbeta(pk_ref, e3_ref)
    al[...] = expand_alpha(pk_ref, e3_ref)

    def scale(at):
        hi[at, :], lo[at, :] = split2(x_ref[at, :].astype(F32) * ex[at, :])

    rows_loop(scale)
    cc = bc_ref[:, STATE:]
    g = split2(dot(cc, bc_ref[:, :STATE], NT) * mask_ref[...].astype(F32))
    seen = jnp.where(c > 0, 1.0, 0.0) * table_row(thx_ref, KAP + c)
    state = split2(seen * sloc_ref[0])
    res[...] = dot3(g, (hi[...], lo[...]), NN) + dot2(cc * mw_ref[...], state, NN)

    def finish(at):
        ys_ref[at, :] = al[at, :] * res[at, :]

    rows_loop(finish)


def norm_kernel(
    ys_ref, x_ref, z_ref, go_ref, bc_ref, mw_ref, pk_ref, e3_ref, thx_ref, vec_ref, sin_ref,
    gy_ref, gz_ref, dloc_ref, r_ref, pay_ref, sums_ref, acc, gain_acc, skip_acc, al, res, hi, lo, rhi, rlo,
):
    step = pl.program_id(0)
    c = C - 1 - step

    @pl.when(step == 0)
    def _():
        acc[...] = jnp.zeros_like(acc)
        gain_acc[...] = jnp.zeros_like(gain_acc)
        skip_acc[...] = jnp.zeros_like(skip_acc)

    al[...] = expand_alpha(pk_ref, e3_ref)
    cm = bc_ref[:, STATE:] * mw_ref[...]
    kappa = table_row(thx_ref, KAP + c)
    state = split2((kappa * table_row(thx_ref, PRE + c)) * sin_ref[...])
    res[...] = dot2(cm, state, NN)
    gain = vec_ref[0:1, :]
    skip = vec_ref[1:2, :]

    def body(at):
        alpha = al[at, :]
        x = x_ref[at, :].astype(F32)
        z = z_ref[at, :].astype(F32)
        out = go_ref[at, :].astype(F32)
        ys = ys_ref[at, :] + alpha * res[at, :]
        y = ys + skip * x
        logistic = jax.nn.sigmoid(z)
        silu = z * logistic
        gated = y * silu
        grad_normed = out * gain
        square = jnp.sum(gated * gated, axis=1, keepdims=True) * (1.0 / W)
        cross = jnp.sum(grad_normed * gated, axis=1, keepdims=True) * (1.0 / W)
        inv = lax.rsqrt(square + EPSILON)
        normed = gated * inv
        grad_gated = inv * (grad_normed - normed * (inv * cross))
        gy = grad_gated * silu
        gz = grad_gated * y * (logistic + silu * (1.0 - logistic))
        gz_ref[at, :] = gz.astype(BF16)
        gy_ref[at, :] = gy
        gpart = out * normed
        spart = gy * x
        gain_acc[...] += gpart[0:8] + gpart[8:16]
        skip_acc[...] += spart[0:8] + spart[8:16]
        hi[at, :], lo[at, :] = split2(gy * alpha)
        rhi[at, :], rlo[at, :] = split2(gy * ys)

    rows_loop(body)
    r_ref[...] = dot2(e3_ref[0:H, :], (rhi[...], rlo[...]), NT)
    back = kappa * dot2(cm, (hi[...], lo[...]), TN)
    dloc_ref[0] = acc[...]
    acc[...] = back + table_row(thx_ref, THR + c) * acc[...]

    @pl.when(step == C - 1)
    def _():
        pay_ref[...] = acc[...]
        sums_ref[0:1, :] = jnp.sum(gain_acc[...], axis=0, keepdims=True)
        sums_ref[1:2, :] = jnp.sum(skip_acc[...], axis=0, keepdims=True)
        sums_ref[2:8, :] = jnp.zeros((6, W), F32)


def local_kernel(
    first, gy_ref, x_ref, bc_ref, mask_ref, me_ref, mw_ref, pk_ref, e3_ref, thx_ref, vec_ref, sloc_ref, sin_ref,
    dloc_ref, *refs,
):
    gx_ref, u_ref, gbc_ref, al, ex, ghi, glo, xhi, xlo, res, rhi, rlo = refs[-12:]
    c = pl.program_id(0) + first
    ex[...] = expand_dtbeta(pk_ref, e3_ref)
    al[...] = expand_alpha(pk_ref, e3_ref)

    def scale(at):
        xhi[at, :], xlo[at, :] = split2(x_ref[at, :].astype(F32) * ex[at, :])
        ghi[at, :], glo[at, :] = split2(gy_ref[at, :] * al[at, :])

    rows_loop(scale)
    b = bc_ref[:, :STATE]
    cc = bc_ref[:, STATE:]
    me = me_ref[...]
    mw = mw_ref[...]
    mask = mask_ref[...].astype(F32)
    gys = (ghi[...], glo[...])
    xs = (xhi[...], xlo[...])
    g = split2(dot(cc, b, NT) * mask)
    q = split2(dot3(gys, xs, NT) * mask)
    kappa = table_row(thx_ref, KAP + c)
    seen = jnp.where(c > 0, 1.0, 0.0) * kappa
    state = split2(seen * sloc_ref[0] + (kappa * table_row(thx_ref, PRE + c)) * sin_ref[...])
    dstate = split2(kappa * dloc_ref[0])
    res[...] = dot3(g, gys, TN) + dot2(b * me, dstate, NN)
    gb = dot(q[0], cc, TN) + dot(q[1], cc, TN) + me.astype(F32) * dot3(xs, dstate, NT)
    gc = dot(q[0], b, NN) + dot(q[1], b, NN) + mw.astype(F32) * dot3(gys, state, NT)
    gbc_ref[:, :STATE] = gb
    gbc_ref[:, STATE:] = gc
    skip = vec_ref[1:2, :]

    def finish(at):
        v = res[at, :]
        scaled = ex[at, :] * v
        gx_ref[at, :] = scaled + skip * gy_ref[at, :]
        rhi[at, :], rlo[at, :] = split2(scaled * x_ref[at, :].astype(F32))

    rows_loop(finish)
    u_ref[...] = dot2(e3_ref[0:H, :], (rhi[...], rlo[...]), NT)


def steps_kernel(
    x_ref, bc_ref, me_ref, pk_ref, rf_ref, e3_ref, thx_ref, par_ref, sloc_ref, sin_ref, dloc_ref, din_ref,
    u_ref, r_ref, sums_ref, gdt_ref, par_out_ref, ex, res, rhi, rlo, cols,
):
    c = pl.program_id(0)

    @pl.when(c == 0)
    def _():
        cols[...] = jnp.zeros_like(cols)

    ex[...] = expand_dtbeta(pk_ref, e3_ref)
    kappa = table_row(thx_ref, KAP + c)
    suffix = table_row(thx_ref, SUF + c)
    dstate = split2((kappa * suffix) * din_ref[...])
    res[...] = dot2(bc_ref[:, :STATE] * me_ref[...], dstate, NN)

    def body(at):
        xs = x_ref[at, :].astype(F32) * ex[at, :]
        rhi[at, :], rlo[at, :] = split2(xs * res[at, :])

    rows_loop(body)
    heads = e3_ref[0:H, :]
    u = u_ref[...] + dot2(heads, (rhi[...], rlo[...]), NT)
    state = sloc_ref[0] + table_row(thx_ref, PRE + 1 + c) * sin_ref[...]
    grad = dloc_ref[0] + suffix * din_ref[...]
    ends = jnp.broadcast_to(jnp.sum(state * grad, axis=0, keepdims=True), (H, W))
    end = sum(dot(heads, part, NT) for part in split3(ends))[:, 0:1]
    dt = rf_ref[0:H, :]
    grad_cum = r_ref[...] - u
    row = lax.broadcasted_iota(jnp.int32, (L, L), 0)
    col = lax.broadcasted_iota(jnp.int32, (L, L), 1)
    tri = (row >= col).astype(F32).astype(BF16)
    parts = dot(jnp.concatenate(split3(grad_cum), 0), tri, NN)
    grad_rate = parts[0:H] + parts[H : 2 * H] + parts[2 * H : 3 * H] + end
    nega = -jnp.exp(par_ref[:, 1:2])
    grad_dt = (u / dt + grad_rate * nega) * rf_ref[H : 2 * H, :]
    gdt_ref[...] = grad_dt
    alog_part = jnp.sum(grad_rate * dt, axis=1, keepdims=True) * nega
    bias_part = jnp.sum(grad_dt, axis=1, keepdims=True)
    lane = lax.broadcasted_iota(jnp.int32, (H, 128), 1)
    cols[...] += jnp.where(lane == 1, alog_part, 0.0) + jnp.where(lane == 2, bias_part, 0.0)

    @pl.when(c == C - 1)
    def _():
        skips = jnp.broadcast_to(sums_ref[1:2, :], (H, W))
        skip_part = sum(dot(heads, part, NT) for part in split3(skips))[:, 0:1]
        right = cols[...] + jnp.where(lane == 0, skip_part, 0.0)
        gains = sums_ref[0:1, :]
        left = jnp.concatenate([gains[:, 128 * r : 128 * (r + 1)] for r in range(8)], 0)
        left = jnp.concatenate([left, jnp.zeros((8, 128), F32)], 0)
        for d in range(SEQ):
            par_out_ref[H * d : H * (d + 1), :128] = left
            par_out_ref[H * d : H * (d + 1), 128:] = right


def final_kernel(
    gx_ref, x_ref, bc_ref, me_ref, pk_ref, e3_ref, thx_ref, din_ref, gbc_ref,
    gxo_ref, gbco_ref, ex, xhi, xlo, res,
):
    c = pl.program_id(0)
    ex[...] = expand_dtbeta(pk_ref, e3_ref)
    factor = table_row(thx_ref, KAP + c) * table_row(thx_ref, SUF + c)
    dstate = split2(factor * din_ref[...])
    me = me_ref[...]
    res[...] = dot2(bc_ref[:, :STATE] * me, dstate, NN)

    def body(at):
        scale = ex[at, :]
        xhi[at, :], xlo[at, :] = split2(x_ref[at, :].astype(F32) * scale)
        gxo_ref[at, :] = (gx_ref[at, :] + scale * res[at, :]).astype(BF16)

    rows_loop(body)
    gb = gbc_ref[:, :STATE] + me.astype(F32) * dot3((xhi[...], xlo[...]), dstate, NT)
    gbco_ref[:, :STATE] = gb.astype(BF16)
    gbco_ref[:, STATE:] = gbc_ref[:, STATE:].astype(BF16)


def head_matrix():
    one = np.arange(W)[None, :] // HEAD_DIM == np.arange(H)[:, None]
    return jnp.asarray(np.concatenate([one, one, one], 0), BF16)


def whole(shape):
    return pl.BlockSpec(shape, lambda i: (0,) * len(shape))


def shard_body(
    x_in, z_gate, b_proj, c_proj, dt_raw, dt_bias, a_log, skip, norm_weight, doc_starts, grad_out
):
    e3 = head_matrix()
    par = jnp.pad(jnp.stack([dt_bias, a_log], 1), ((0, 0), (0, 126)))
    vec = jnp.pad(
        jnp.stack([norm_weight, jnp.repeat(skip, HEAD_DIM)], 0), ((0, 6), (0, 0))
    )
    starts = doc_starts.reshape(1, T)
    mine = jnp.concatenate(
        [b_proj.reshape(128, GRP, STATE), c_proj.reshape(128, GRP, STATE)], 2
    ).transpose(1, 0, 2)
    bc = lax.all_to_all(mine, "head", split_axis=0, concat_axis=0, tiled=True).reshape(T, 2 * STATE)

    def call(kernel, outs, out_specs, in_specs, scratch, flops, name, steps=C, aliases={}):
        return pl.pallas_call(
            kernel,
            grid=(steps,),
            input_output_aliases=aliases,
            out_shape=outs,
            in_specs=in_specs,
            out_specs=out_specs,
            scratch_shapes=scratch,
            compiler_params=pltpu.CompilerParams(
                dimension_semantics=("arbitrary",), vmem_limit_bytes=60 * 2**20
            ),
            cost_estimate=pl.CostEstimate(flops=flops, bytes_accessed=8 * 2**20, transcendentals=0),
            name=name,
        )

    sds = jax.ShapeDtypeStruct
    pk, rf, mask, me, mw, thx = pl.pallas_call(
        prep_kernel,
        out_shape=(
            sds((4 * H, T), BF16),
            sds((2 * H, T), F32),
            sds((T, L), BF16),
            sds((T, 128), BF16),
            sds((T, 128), BF16),
            sds((TABLE, W), F32),
        ),
        compiler_params=pltpu.CompilerParams(vmem_limit_bytes=60 * 2**20),
        name="prep",
    )(dt_raw, par, starts, e3)

    def at_chunk(shape, axis, order=lambda i: i):
        def index(i):
            return tuple(order(i) if a == axis else 0 for a in range(len(shape)))

        return pl.BlockSpec(shape, index)

    def reverse(i):
        return C - 1 - i

    def tok(width, order=lambda i: i):
        return at_chunk((L, width), 0, order)

    def rowf(rows, order=lambda i: i):
        return at_chunk((rows, L), 1, order)

    def stat(order=lambda i: i):
        return at_chunk((1, STATE, W), 0, order)

    e3_spec = whole((3 * H, W))
    thx_spec = whole((TABLE, W))
    vec_spec = whole((8, W))
    sin_spec = whole((STATE, W))
    big = pltpu.VMEM((L, W), F32)
    half = pltpu.VMEM((L, W), BF16)
    unit = 2 * T * L * W

    sloc, pay = call(
        states_kernel,
        (sds((C, STATE, W), F32), sds((STATE, W + 128), F32)),
        (stat(), whole((STATE, W + 128))),
        [tok(W), tok(2 * STATE), tok(128), rowf(4 * H), e3_spec, thx_spec],
        [pltpu.VMEM((STATE, W), F32), big, half, half],
        2 * unit,
        "states",
    )(x_in, bc, me, pk, e3, thx)

    def exchange(v):
        return lax.all_to_all(v, "seq", split_axis=0, concat_axis=0, tiled=True)

    any_spec = pl.BlockSpec(memory_space=pl.ANY)

    def within(first, *earlier):
        def order(i):
            return i + first

        return call(
            functools.partial(within_kernel, first),
            sds((T, W), F32),
            tok(W, order),
            [
                tok(W, order), tok(2 * STATE, order), tok(L, order), tok(128, order), rowf(4 * H, order),
                e3_spec, thx_spec, stat(lambda i: jnp.maximum(i + first - 1, 0)),
            ]
            + [any_spec] * len(earlier),
            [big, big, half, half, big],
            3 * unit,
            "within",
            C // 2,
            {8: 0} if earlier else {},
        )(x_in, bc, mask, mw, pk, e3, thx, sloc, *earlier)

    got = exchange(pay)
    ys, got = lax.optimization_barrier((within(0), got))
    before = pl.pallas_call(
        scan_forward_kernel, out_shape=sds((STATE, W), F32), name="scan_forward"
    )(got)
    sin = exchange(before)
    ys = within(C // 2, ys)

    gy, gz, dloc, r, back, sums = call(
        norm_kernel,
        (
            sds((T, W), F32),
            sds((T, W), BF16),
            sds((C, STATE, W), F32),
            sds((H, T), F32),
            sds((STATE, W), F32),
            sds((8, W), F32),
        ),
        (tok(W, reverse), tok(W, reverse), stat(reverse), rowf(H, reverse), sin_spec, vec_spec),
        [tok(W, reverse)] * 4
        + [
            tok(2 * STATE, reverse), tok(128, reverse), rowf(4 * H, reverse), e3_spec, thx_spec, vec_spec, sin_spec,
        ],
        [
            pltpu.VMEM((STATE, W), F32), pltpu.VMEM((8, W), F32), pltpu.VMEM((8, W), F32),
            big, big, half, half, half, half,
        ],
        6 * unit,
        "norm",
    )(ys, x_in, z_gate, grad_out, bc, mw, pk, e3, thx, vec, sin)

    def local(first, *earlier):
        def order(i):
            return i + first

        return call(
            functools.partial(local_kernel, first),
            (sds((T, W), F32), sds((H, T), F32), sds((T, 2 * STATE), F32)),
            (tok(W, order), rowf(H, order), tok(2 * STATE, order)),
            [
                tok(W, order), tok(W, order), tok(2 * STATE, order), tok(L, order), tok(128, order), tok(128, order),
                rowf(4 * H, order), e3_spec, thx_spec, vec_spec,
                stat(lambda i: jnp.maximum(i + first - 1, 0)), sin_spec, stat(order),
            ]
            + [any_spec] * len(earlier),
            [big, big, half, half, half, half, big, half, half],
            6 * unit,
            "local",
            C // 2,
            {13 + k: k for k in range(len(earlier))},
        )(gy, x_in, bc, mask, me, mw, pk, e3, thx, vec, sloc, sin, dloc, *earlier)

    got_back = exchange(back)
    partly, got_back = lax.optimization_barrier((local(0), got_back))
    behind = pl.pallas_call(
        scan_backward_kernel, out_shape=sds((STATE, W), F32), name="scan_backward"
    )(got_back, got)
    din = exchange(behind)
    gx_local, u, gbc_local = local(C // 2, *partly)

    grad_dt, params = call(
        steps_kernel,
        (sds((H, T), F32), sds((SEQ * H, 256), F32)),
        (rowf(H), whole((SEQ * H, 256))),
        [
            tok(W), tok(2 * STATE), tok(128), rowf(4 * H), rowf(2 * H), e3_spec, thx_spec, whole((H, 128)),
            stat(), sin_spec, stat(), sin_spec, rowf(H), rowf(H), vec_spec,
        ],
        [big, big, half, half, pltpu.VMEM((H, 128), F32)],
        3 * unit,
        "steps",
    )(x_in, bc, me, pk, rf, e3, thx, par, sloc, sin, dloc, din, u, r, sums)
    params = exchange(params)

    grad_x, gbc = call(
        final_kernel,
        (sds((T, W), BF16), sds((T, 2 * STATE), BF16)),
        (tok(W), tok(2 * STATE)),
        [tok(W), tok(W), tok(2 * STATE), tok(128), rowf(4 * H), e3_spec, thx_spec, sin_spec, tok(2 * STATE)],
        [big, half, half, big],
        4 * unit,
        "final",
    )(gx_local, x_in, bc, me, pk, e3, thx, din, gbc_local)

    back_bc = lax.all_to_all(
        gbc.reshape(GRP, 128, 2 * STATE), "head", split_axis=0, concat_axis=0, tiled=True
    )
    grad_b = back_bc[:, :, :STATE].transpose(1, 0, 2).reshape(128, GRP * STATE)
    grad_c = back_bc[:, :, STATE:].transpose(1, 0, 2).reshape(128, GRP * STATE)
    summed = jnp.sum(params.reshape(SEQ, H, 256), axis=0)
    grad_gain = summed[:8, :128].reshape(W)
    grad_skip, grad_alog, grad_bias = summed[:, 128], summed[:, 129], summed[:, 130]
    return (grad_x, gz, grad_b, grad_c, grad_dt, grad_alog, grad_bias, grad_skip, grad_gain)


def solution(mesh):
    in_specs = (
        P("seq", "head"),
        P("seq", "head"),
        P(("seq", "head"), None),
        P(("seq", "head"), None),
        P("head", "seq"),
        P("head"),
        P("head"),
        P("head"),
        P("head"),
        P("seq"),
        P("seq", "head"),
    )
    out_specs = (
        P("seq", "head"),
        P("seq", "head"),
        P(("seq", "head"), None),
        P(("seq", "head"), None),
        P("head", "seq"),
        P("head"),
        P("head"),
        P("head"),
        P("head"),
    )
    return jax.shard_map(shard_body, mesh=mesh, in_specs=in_specs, out_specs=out_specs, check_vma=False)
```

```python
import jax
import jax.numpy as jnp
import numpy as np
from jax import lax
from jax.experimental import pallas as pl
from jax.experimental.pallas import tpu as pltpu
from jax.sharding import PartitionSpec as P

HEADS = 128
HEAD_DIM = 64
STATE = 128
PROJECTION_SETS = 8
EPSILON = 1e-05

T = 1024
H = 16
W = H * HEAD_DIM
L = 256
C = T // L
SEQ = 16
GRP = 8
ROWS = STATE // SEQ
F32 = jnp.float32
BF16 = jnp.bfloat16
STEP = 16
VMEM_LIMIT = 60 * 2**20
VMEM_NEAR = 48 * 2**20

THR, KAP, PRE, TOTAL, TABLE = 0, 4, 8, 12, 16
ALPHA, DTBETA, TO_END, FROM_START = 0, 1, 2, 3

NN = (((1,), (0,)), ((), ()))
NT = (((1,), (1,)), ((), ()))
TN = (((0,), (0,)), ((), ()))


def dot(a, b, dims):
    return lax.dot_general(a, b, dims, preferred_element_type=F32)


def split2(a):
    hi = a.astype(BF16)
    return hi, (a - hi.astype(F32)).astype(BF16)


def split3(a):
    hi, mid = split2(a)
    lo = (a - hi.astype(F32) - mid.astype(F32)).astype(BF16)
    return hi, mid, lo


def joined(a, b, dims):
    ((ka,), (kb,)), _ = dims
    return dot(jnp.concatenate(a, ka), jnp.concatenate(b, kb), dims)


def dot2(a, b, dims):
    return joined([a, a], b, dims)


def dot3(a, b, dims):
    return joined([a[0], a[0], a[1]], [b[0], b[1], b[0]], dims)


def dot3_wide(a, b):
    both = dot(a[0], jnp.concatenate(b, 0), NT)
    return both[:, :STATE] + both[:, STATE:] + dot(a[1], b[0], NT)


def each_rows(body):
    for i in range(L // STEP):
        body(slice(STEP * i, STEP * (i + 1)))


class Views:
    def __init__(self, buffers, kinds, c):
        for name, ref in buffers.items():
            kind = kinds[name]
            if kind in ("tok", "near_tok"):
                ref = ref.at[pl.ds(pl.multiple_of(c * L, L), L), :]
            elif kind == "row":
                ref = ref.at[:, pl.ds(pl.multiple_of(c * L, L), L)]
            elif kind == "state":
                ref = ref.at[c]
            setattr(self, name, ref)


def staged(body, ins, outs, scratch, name, flops, backward=False, begin=None, end=None):
    kinds = {k: kind for k, (_, kind) in ins.items()}
    kinds.update({k: kind for k, (_, _, kind) in outs.items()})
    kinds.update({k: "row" if s == (H, T) else "all" for k, (s, _) in scratch.items()})
    n, m = len(ins), len(outs)
    moving = ("tok", "state")
    here = [k for k in ins if kinds[k] in ("near", "near_tok")]
    copied = [k for k in outs if kinds[k] == "copy"]
    buffered_in = [k for k in ins if k not in here]
    buffered_out = [k for k in outs if k not in copied]

    def part(ref, kind, c):
        if kind == "tok":
            return ref.at[pl.ds(pl.multiple_of(c * L, L), L), :]
        return ref.at[c]

    def kernel(*refs):
        far_in = dict(zip(ins, refs[:n]))
        far_out = dict(zip(outs, refs[n : n + m]))
        near = dict(zip([*buffered_in, *buffered_out, *scratch], refs[n + m : -1]))
        near.update({k: far_in[k] for k in here})
        sems = refs[-1]
        slot = {k: i for i, k in enumerate([*ins, *outs])}

        def copy_in(k, c):
            return pltpu.make_async_copy(part(far_in[k], kinds[k], c), part(near[k], kinds[k], c), sems.at[slot[k], c])

        def copy_out(k, c):
            return pltpu.make_async_copy(part(near[k], kinds[k], c), part(far_out[k], kinds[k], c), sems.at[slot[k], c])

        once = [
            pltpu.make_async_copy(far_in[k], near[k], sems.at[slot[k], 0])
            for k in buffered_in
            if kinds[k] not in moving
        ]
        passed = [
            pltpu.make_async_copy(near[k.removesuffix("_copy")], far_out[k], sems.at[slot[k], 0]) for k in copied
        ]
        for copy in once:
            copy.start()
        for c in reversed(range(C)) if backward else range(C):
            for k in ins:
                if kinds[k] in moving:
                    copy_in(k, c).start()
        for copy in passed:
            copy.start()
        for copy in once:
            copy.wait()
        whole = Views(near, {k: "all" for k in near}, 0)
        if begin is not None:
            begin(whole)

        def step(i, carry):
            c = C - 1 - i if backward else i
            for k in ins:
                if kinds[k] in moving:
                    copy_in(k, c).wait()
            body(c, Views(near, kinds, c))
            for k in outs:
                if kinds[k] in moving:
                    copy_out(k, c).start()
            return carry

        lax.fori_loop(0, C, step, 0)
        if end is not None:
            end(whole)
        once = [
            pltpu.make_async_copy(near[k], far_out[k], sems.at[slot[k], 0])
            for k in buffered_out
            if kinds[k] not in moving
        ]
        for copy in once:
            copy.start()
        for c in range(C):
            for k in outs:
                if kinds[k] in moving:
                    copy_out(k, c).wait()
        for copy in once + passed:
            copy.wait()

    far = pl.BlockSpec(memory_space=pl.ANY)
    return pl.pallas_call(
        kernel,
        out_shape=tuple(pltpu.HBM(s, d) for s, d, _ in outs.values()),
        in_specs=[pl.BlockSpec(memory_space=pltpu.VMEM) if k in here else far for k in ins],
        out_specs=tuple([far] * m),
        scratch_shapes=[
            *[pltpu.VMEM(ins[k][0].shape, ins[k][0].dtype) for k in buffered_in],
            *[pltpu.VMEM(*outs[k][:2]) for k in buffered_out],
            *[pltpu.VMEM(s, d) for s, d in scratch.values()],
            pltpu.SemaphoreType.DMA((n + m, C)),
        ],
        compiler_params=pltpu.CompilerParams(vmem_limit_bytes=VMEM_NEAR if here else VMEM_LIMIT),
        cost_estimate=pl.CostEstimate(flops=flops, bytes_accessed=8 * 2**20, transcendentals=0),
        name=name,
    )(*[pltpu.with_memory_space_constraint(ins[k][0], pltpu.VMEM if k in here else pltpu.HBM) for k in ins])


def expand(pk, which, e3):
    return dot(pk[2 * H * which : 2 * H * (which + 1), :], e3[0 : 2 * H, :], TN)


def prep_kernel(dt_ref, par_ref, st_ref, e3_ref, pk_ref, rf_ref, mask_ref, me_ref, mw_ref, thx_ref):
    bias = par_ref[:, 0:1]
    nega = -jnp.exp(par_ref[:, 1:2])
    row = lax.broadcasted_iota(jnp.int32, (L, L), 0)
    col = lax.broadcasted_iota(jnp.int32, (L, L), 1)
    tri = (row <= col).astype(F32).astype(BF16)
    causal = row >= col
    first = lax.broadcasted_iota(jnp.int32, (H, L), 0) == 0
    lane = lax.broadcasted_iota(jnp.int32, (H, 128), 1)
    ones = jnp.ones((H, L), BF16)
    thr, kap, leave, enter = [], [], [], []

    def put(which, at, value):
        base = 2 * H * which
        pk_ref[base : base + H, at], pk_ref[base + H : base + 2 * H, at] = split2(value)

    for c in range(C):
        at = slice(c * L, (c + 1) * L)
        pre = dt_ref[:, at] + bias
        dt = jax.nn.softplus(pre)
        rf_ref[0:H, at] = dt
        rf_ref[H : 2 * H, at] = jax.nn.sigmoid(pre)
        rate = dt * nega
        parts = dot(jnp.concatenate(split3(rate), 0), tri, NN)
        cum = parts[0:H] + parts[H : 2 * H] + parts[2 * H : 3 * H]
        starts = jnp.broadcast_to(st_ref[:, at].astype(F32), (H, L))
        seg = dot(starts.astype(BF16), tri, NN)
        cum_end = cum[:, L - 1 : L]
        seg_end = seg[:, L - 1 : L]
        half = 0.5 * cum_end
        put(ALPHA, at, jnp.exp(cum - half))
        put(DTBETA, at, dt * jnp.exp(half - cum))
        leave.append(jnp.where(seg == seg_end, dt * jnp.exp(cum_end - cum), 0.0))
        enter.append(jnp.where(seg == 0.0, jnp.exp(cum), 0.0))
        seg_first = jnp.where(first, seg, 0.0).astype(BF16)
        seg_col = dot(seg_first, ones, TN)
        mask = causal & (seg_col == seg[0:1, :])
        mask_ref[at, :] = mask.astype(F32).astype(BF16)
        to_end = jnp.where(first & (seg == seg_end), 1.0, 0.0).astype(BF16)
        from_start = jnp.where(first & (seg == 0.0), 1.0, 0.0).astype(BF16)
        me_ref[at, :] = dot(to_end, ones[:, :128], TN).astype(BF16)
        mw_ref[at, :] = dot(from_start, ones[:, :128], TN).astype(BF16)
        thr.append(jnp.where(seg_end == 0.0, jnp.exp(cum_end), 0.0))
        kap.append(jnp.exp(half))
    passed = jnp.ones((H, 1), F32)
    before = []
    for c in range(C):
        before.append(passed)
        put(FROM_START, slice(c * L, (c + 1) * L), enter[c] * passed)
        passed = passed * thr[c]
    columns = [*thr, *kap, *before, passed]
    passed = jnp.ones((H, 1), F32)
    for c in reversed(range(C)):
        put(TO_END, slice(c * L, (c + 1) * L), leave[c] * passed)
        passed = passed * thr[c]
    table = jnp.zeros((H, 128), F32)
    for k, v in enumerate(columns):
        table = jnp.where(lane == k, v, table)
    wide = dot(jnp.concatenate(split3(table), 0), e3_ref[...], TN)
    thx_ref[...] = wide[0:TABLE]


def states_body(c, r):
    scale = expand(r.pk, TO_END, r.e3)

    def rows(at):
        r.hi[at, :], r.lo[at, :] = split2(r.x[at, :].astype(F32) * scale[at, :])

    each_rows(rows)
    new = dot2(r.bc[:, :STATE], (r.hi[...], r.lo[...]), TN)
    r.acc[...] += new


def clear(r):
    r.acc[...] = jnp.zeros((STATE, W), F32)


def states_end(r):
    r.pay[:, :W] = r.acc[...]
    total = r.thx[TOTAL : TOTAL + 1, :]
    block = jnp.concatenate([total[:, 128 * k : 128 * (k + 1)] for k in range(ROWS)], 0)
    for d in range(SEQ):
        r.pay[ROWS * d : ROWS * (d + 1), W:] = block


def through_row(got_ref, j):
    block = got_ref[ROWS * j : ROWS * (j + 1), W:]
    return jnp.concatenate([block[k : k + 1, :] for k in range(ROWS)], 1)


def scan_forward_kernel(got_ref, out_ref, through_ref):
    acc = jnp.zeros((ROWS, W), F32)
    for j in range(SEQ):
        at = slice(ROWS * j, ROWS * (j + 1))
        out_ref[at, :] = acc
        through = through_row(got_ref, j)
        through_ref[j : j + 1, :] = through
        acc = through * acc + got_ref[at, :W]


def scan_backward_kernel(got_ref, through_ref, out_ref):
    acc = jnp.zeros((ROWS, W), F32)
    for j in reversed(range(SEQ)):
        at = slice(ROWS * j, ROWS * (j + 1))
        out_ref[at, :] = acc
        acc = through_ref[j : j + 1, :] * acc + got_ref[at, :]


def within_body(c, r):
    ex = expand(r.pk, DTBETA, r.e3)
    al = expand(r.pk, ALPHA, r.e3)
    fin = expand(r.pk, TO_END, r.e3)

    def scale(at):
        x = r.x[at, :].astype(F32)
        r.hi[at, :], r.lo[at, :] = split2(x * ex[at, :])
        r.xhi[at, :], r.xlo[at, :] = split2(x * fin[at, :])

    each_rows(scale)
    b = r.bc[:, :STATE]
    cc = r.bc[:, STATE:]
    g = split2(dot(cc, b, NT) * r.mask[...].astype(F32))
    xs = (r.hi[...], r.lo[...])
    kappa = r.thx[pl.ds(KAP + c, 1), :]
    r.sloc[...] = r.acc[...]
    res = dot3(g, xs, NN) + dot2(cc * r.mw[...], split2(kappa * r.acc[...]), NN)
    r.ys[...] = al * res
    r.acc[...] = r.thx[pl.ds(THR + c, 1), :] * r.acc[...] + kappa * dot2(b * r.me[...], xs, TN)


def norm_begin(r):
    r.shi[...], r.slo[...] = split2(r.sin[...])
    r.gain_acc[...] = jnp.zeros((8, W), F32)
    r.skip_acc[...] = jnp.zeros((8, W), F32)
    r.back[...] = jnp.zeros((STATE, W), F32)


def norm_body(c, r):
    cc = r.bc[:, STATE:]
    win = expand(r.pk, FROM_START, r.e3)
    res = dot2(cc, (r.shi[...], r.slo[...]), NN)
    gain = r.vec[0:1, :]
    skip = r.vec[1:2, :]

    def body(at):
        weight = win[at, :]
        x = r.x[at, :].astype(F32)
        z = r.z[at, :].astype(F32)
        out = r.go[at, :].astype(F32)
        ys = r.ys[at, :] + weight * res[at, :]
        y = ys + skip * x
        logistic = jax.nn.sigmoid(z)
        silu = z * logistic
        gated = y * silu
        grad_normed = out * gain
        square = jnp.sum(gated * gated, axis=1, keepdims=True) * (1.0 / W)
        cross = jnp.sum(grad_normed * gated, axis=1, keepdims=True) * (1.0 / W)
        inv = lax.rsqrt(square + EPSILON)
        normed = gated * inv
        grad_gated = inv * (grad_normed - normed * (inv * cross))
        gy = grad_gated * silu
        gz = grad_gated * y * (logistic + silu * (1.0 - logistic))
        r.gz[at, :] = gz.astype(BF16)
        r.gy[at, :] = gy
        gpart = out * normed
        spart = gy * x
        r.gain_acc[...] += gpart[0:8] + gpart[8:16]
        r.skip_acc[...] += spart[0:8] + spart[8:16]
        r.hi[at, :], r.lo[at, :] = split2(gy * weight)
        r.rhi[at, :], r.rlo[at, :] = split2(gy * ys)

    each_rows(body)
    r.r[...] = dot2(r.e3[0:H, :], (r.rhi[...], r.rlo[...]), NT)
    new = dot2(cc, (r.hi[...], r.lo[...]), TN)
    r.back[...] += new


def norm_end(r):
    r.sums[0:1, :] = jnp.sum(r.gain_acc[...], axis=0, keepdims=True)
    r.sums[1:2, :] = jnp.sum(r.skip_acc[...], axis=0, keepdims=True)
    r.sums[2:8, :] = jnp.zeros((6, W), F32)


def local_x_body(c, r):
    ex = expand(r.pk, DTBETA, r.e3)
    al = expand(r.pk, ALPHA, r.e3)

    def scale(at):
        r.ghi[at, :], r.glo[at, :] = split2(r.gy[at, :] * al[at, :])

    each_rows(scale)
    b = r.bc[:, :STATE]
    cc = r.bc[:, STATE:]
    gys = (r.ghi[...], r.glo[...])
    g = split2(dot(cc, b, NT) * r.mask[...].astype(F32))
    kappa = r.thx[pl.ds(KAP + c, 1), :]
    r.dloc[...] = r.acc[...]
    res = dot3(g, gys, TN) + dot2(b * r.me[...], split2(kappa * r.acc[...]), NN)
    skip = r.vec[1:2, :]

    def finish(at):
        scaled = ex[at, :] * res[at, :]
        r.gx[at, :] = scaled + skip * r.gy[at, :]
        r.rhi[at, :], r.rlo[at, :] = split2(scaled * r.x[at, :].astype(F32))

    each_rows(finish)
    r.u[...] = dot2(r.e3[0:H, :], (r.rhi[...], r.rlo[...]), NT)
    r.acc[...] = r.thx[pl.ds(THR + c, 1), :] * r.acc[...] + kappa * dot2(cc * r.mw[...], gys, TN)


def local_bc_body(c, r):
    ex = expand(r.pk, DTBETA, r.e3)
    al = expand(r.pk, ALPHA, r.e3)

    def scale(at):
        r.xhi[at, :], r.xlo[at, :] = split2(r.x[at, :].astype(F32) * ex[at, :])
        r.ghi[at, :], r.glo[at, :] = split2(r.gy[at, :] * al[at, :])

    each_rows(scale)
    b = r.bc[:, :STATE]
    cc = r.bc[:, STATE:]
    gys = (r.ghi[...], r.glo[...])
    xs = (r.xhi[...], r.xlo[...])
    q = split2(dot3(gys, xs, NT) * r.mask[...].astype(F32))
    kappa = r.thx[pl.ds(KAP + c, 1), :]
    state = split2(kappa * (r.sloc[...] + r.thx[pl.ds(PRE + c, 1), :] * r.sin[...]))
    dstate = split2(kappa * r.dloc[...])
    gb = joined(q, [cc, cc], TN) + r.me[...].astype(F32) * dot3_wide(xs, dstate)
    gc = joined(q, [b, b], NN) + r.mw[...].astype(F32) * dot3_wide(gys, state)
    r.gbc[:, :STATE] = gb
    r.gbc[:, STATE:] = gc


def final_begin(r):
    r.dhi[...], r.dlo[...] = split2(r.din[...])


def final_bc_body(c, r):
    gb = r.gbc[:, :STATE] + dot3_wide((r.xhi[...], r.xlo[...]), (r.dhi[...], r.dlo[...]))
    r.out[:, :STATE] = gb.astype(BF16)
    r.out[:, STATE:] = r.gbc[:, STATE:].astype(BF16)


def final_x_body(c, r):
    fin = expand(r.pk, TO_END, r.e3)
    v = dot2(r.bc[:, :STATE], (r.dhi[...], r.dlo[...]), NN)

    def body(at):
        scaled = fin[at, :] * v[at, :]
        r.gxo[at, :] = (r.gx[at, :] + scaled).astype(BF16)
        r.rhi[at, :], r.rlo[at, :] = split2(scaled * r.x[at, :].astype(F32))

    each_rows(body)
    r.uu[...] = r.u[...] + dot2(r.e3[0:H, :], (r.rhi[...], r.rlo[...]), NT)


def final_x_end(r):
    heads = r.e3[0:H, :]
    state = r.pay[:, :W] + r.thx[TOTAL : TOTAL + 1, :] * r.sin[...]
    ends = jnp.broadcast_to(jnp.sum(state * r.din[...], axis=0, keepdims=True), (H, W))
    carry = sum(dot(heads, part, NT) for part in split3(ends))[:, 0:1]
    row = lax.broadcasted_iota(jnp.int32, (L, L), 0)
    col = lax.broadcasted_iota(jnp.int32, (L, L), 1)
    tri = (row >= col).astype(F32).astype(BF16)
    nega = -jnp.exp(r.par[:, 1:2])
    alog_part = jnp.zeros((H, 1), F32)
    bias_part = jnp.zeros((H, 1), F32)
    for c in reversed(range(C)):
        at = slice(c * L, (c + 1) * L)
        u = r.uu[:, at]
        dt = r.rf[0:H, at]
        parts = dot(jnp.concatenate(split3(r.r[:, at] - u), 0), tri, NN)
        later = parts[0:H] + parts[H : 2 * H] + parts[2 * H : 3 * H]
        grad_rate = later + carry
        carry = carry + later[:, 0:1]
        grad_dt = (u / dt + grad_rate * nega) * r.rf[H : 2 * H, at]
        r.gdt[:, at] = grad_dt
        alog_part += jnp.sum(grad_rate * dt, axis=1, keepdims=True)
        bias_part += jnp.sum(grad_dt, axis=1, keepdims=True)
    skips = jnp.broadcast_to(r.sums[1:2, :], (H, W))
    skip_part = sum(dot(heads, part, NT) for part in split3(skips))[:, 0:1]
    lane = lax.broadcasted_iota(jnp.int32, (H, 128), 1)
    right = jnp.where(
        lane == 0, skip_part, jnp.where(lane == 1, alog_part * nega, jnp.where(lane == 2, bias_part, 0.0))
    )
    gains = r.sums[0:1, :]
    left = jnp.concatenate([gains[:, 128 * k : 128 * (k + 1)] for k in range(8)], 0)
    left = jnp.concatenate([left, jnp.zeros((8, 128), F32)], 0)
    for d in range(SEQ):
        r.params[H * d : H * (d + 1), :128] = left
        r.params[H * d : H * (d + 1), 128:] = right


def head_matrix():
    one = np.arange(W)[None, :] // HEAD_DIM == np.arange(H)[:, None]
    return jnp.asarray(np.concatenate([one, one, one], 0), BF16)


def shard_body(
    x_in, z_gate, b_proj, c_proj, dt_raw, dt_bias, a_log, skip, norm_weight, doc_starts, grad_out
):
    e3 = head_matrix()
    par = jnp.pad(jnp.stack([dt_bias, a_log], 1), ((0, 0), (0, 126)))
    vec = jnp.pad(
        jnp.stack([norm_weight, jnp.repeat(skip, HEAD_DIM)], 0), ((0, 6), (0, 0))
    )
    starts = doc_starts.reshape(1, T)
    mine = jnp.concatenate(
        [b_proj.reshape(128, GRP, STATE), c_proj.reshape(128, GRP, STATE)], 2
    ).transpose(1, 0, 2)
    bc = lax.all_to_all(mine, "head", split_axis=0, concat_axis=0, tiled=True).reshape(T, 2 * STATE)

    sds = pltpu.HBM
    pk, rf, mask, me, mw, thx = pl.pallas_call(
        prep_kernel,
        out_shape=(
            sds((8 * H, T), BF16),
            sds((2 * H, T), F32),
            sds((T, L), BF16),
            sds((T, 128), BF16),
            sds((T, 128), BF16),
            sds((TABLE, W), F32),
        ),
        compiler_params=pltpu.CompilerParams(vmem_limit_bytes=VMEM_LIMIT),
        name="prep",
    )(*[pltpu.with_memory_space_constraint(a, pltpu.HBM) for a in (dt_raw, par, starts, e3)])

    state = ((STATE, W), F32)
    half = ((L, W), BF16)
    unit = 2 * T * L * W
    common = {"e3": (e3, "all"), "pk": (pk, "row"), "thx": (thx, "all")}
    x = {"x": (x_in, "tok")}
    masks = {"mask": (mask, "tok"), "me": (me, "tok"), "mw": (mw, "tok")}

    pay, bc = staged(
        states_body,
        common | {"bc": (bc, "near_tok")} | x,
        {"pay": ((STATE, W + 128), F32, "all"), "bc_copy": ((T, 2 * STATE), BF16, "copy")},
        {"acc": state, "hi": half, "lo": half},
        "states",
        2 * unit,
        begin=clear,
        end=states_end,
    )

    def scan(kernel, name, outs, got, *others):
        return pl.pallas_call(
            kernel,
            out_shape=outs,
            in_specs=[pl.BlockSpec(memory_space=pltpu.VMEM)] * (1 + len(others)),
            compiler_params=pltpu.CompilerParams(vmem_limit_bytes=16 * 2**20),
            name=name,
        )(
            pltpu.with_memory_space_constraint(got, pltpu.VMEM),
            *[pltpu.with_memory_space_constraint(a, pltpu.HBM) for a in others],
        )

    def exchange(v):
        return lax.all_to_all(v, "seq", split_axis=0, concat_axis=0, tiled=True)

    bcs = {"bc": (bc, "tok")}
    got = exchange(pay)
    ys, sloc, xhi, xlo = staged(
        within_body,
        common | bcs | masks | x,
        {
            "ys": ((T, W), F32, "tok"),
            "sloc": ((C, STATE, W), F32, "state"),
            "xhi": ((T, W), BF16, "tok"),
            "xlo": ((T, W), BF16, "tok"),
        },
        {"acc": state, "hi": half, "lo": half},
        "within",
        7 * unit,
        begin=clear,
    )
    (ys, sloc, xhi, xlo), got = lax.optimization_barrier(((ys, sloc, xhi, xlo), got))
    before, through = scan(
        scan_forward_kernel, "scan_forward", (sds((STATE, W), F32), sds((SEQ, W), F32)), got
    )
    sin = exchange(before)

    gy, gz, r, back, sums, sin = staged(
        norm_body,
        common
        | {"vec": (vec, "all"), "sin": (sin, "near")}
        | bcs
        | {"ys": (ys, "tok"), "z": (z_gate, "tok"), "go": (grad_out, "tok")}
        | x,
        {
            "gy": ((T, W), F32, "tok"),
            "gz": ((T, W), BF16, "tok"),
            "r": ((H, T), F32, "row"),
            "back": ((STATE, W), F32, "all"),
            "sums": ((8, W), F32, "all"),
            "sin_copy": ((STATE, W), F32, "copy"),
        },
        {
            "gain_acc": ((8, W), F32),
            "skip_acc": ((8, W), F32),
            "shi": ((STATE, W), BF16),
            "slo": ((STATE, W), BF16),
            "hi": half,
            "lo": half,
            "rhi": half,
            "rlo": half,
        },
        "norm",
        6 * unit,
        begin=norm_begin,
        end=norm_end,
    )

    got_back = exchange(back)
    gx, u, dloc = staged(
        local_x_body,
        common | {"vec": (vec, "all")} | bcs | masks | {"gy": (gy, "tok")} | x,
        {
            "gx": ((T, W), F32, "tok"),
            "u": ((H, T), F32, "row"),
            "dloc": ((C, STATE, W), F32, "state"),
        },
        {"acc": state, "ghi": half, "glo": half, "rhi": half, "rlo": half},
        "local_x",
        7 * unit,
        backward=True,
        begin=clear,
    )
    dloc, got_back = lax.optimization_barrier((dloc, got_back))
    behind = scan(scan_backward_kernel, "scan_backward", sds((STATE, W), F32), got_back, through)
    din = exchange(behind)
    (gbc,) = staged(
        local_bc_body,
        common
        | {"sin": (sin, "all")}
        | bcs
        | masks
        | {"gy": (gy, "tok"), "sloc": (sloc, "state"), "dloc": (dloc, "state")}
        | x,
        {"gbc": ((T, 2 * STATE), F32, "tok")},
        {"ghi": half, "glo": half, "xhi": half, "xlo": half},
        "local_bc",
        7 * unit,
    )

    gbc, din = lax.optimization_barrier((gbc, din))
    gbc, din = staged(
        final_bc_body,
        {"din": (din, "near"), "gbc": (gbc, "tok"), "xhi": (xhi, "tok"), "xlo": (xlo, "tok")},
        {"out": ((T, 2 * STATE), BF16, "tok"), "din_copy": ((STATE, W), F32, "copy")},
        {"dhi": ((STATE, W), BF16), "dlo": ((STATE, W), BF16)},
        "final_bc",
        2 * unit,
        begin=final_begin,
    )
    gbc, gx = lax.optimization_barrier((gbc, gx))
    back_bc = lax.all_to_all(
        gbc.reshape(GRP, 128, 2 * STATE), "head", split_axis=0, concat_axis=0, tiled=True
    )
    grad_x, grad_dt, params = staged(
        final_x_body,
        common
        | {
            "din": (din, "all"),
            "sin": (sin, "all"),
            "pay": (pay, "all"),
            "par": (par, "all"),
            "sums": (sums, "all"),
            "rf": (rf, "row"),
            "r": (r, "row"),
            "u": (u, "row"),
        }
        | bcs
        | {"gx": (gx, "tok")}
        | x,
        {
            "gxo": ((T, W), BF16, "tok"),
            "gdt": ((H, T), F32, "row"),
            "params": ((SEQ * H, 256), F32, "all"),
        },
        {
            "uu": ((H, T), F32),
            "dhi": ((STATE, W), BF16),
            "dlo": ((STATE, W), BF16),
            "rhi": half,
            "rlo": half,
        },
        "final_x",
        3 * unit,
        begin=final_begin,
        end=final_x_end,
    )
    params, back_bc = lax.optimization_barrier((params, back_bc))
    grad_b = back_bc[:, :, :STATE].transpose(1, 0, 2).reshape(128, GRP * STATE)
    grad_c = back_bc[:, :, STATE:].transpose(1, 0, 2).reshape(128, GRP * STATE)
    summed = jnp.sum(exchange(params).reshape(SEQ, H, 256), axis=0)
    grad_gain = summed[:8, :128].reshape(W)
    grad_skip, grad_alog, grad_bias = summed[:, 128], summed[:, 129], summed[:, 130]
    return (grad_x, gz, grad_b, grad_c, grad_dt, grad_alog, grad_bias, grad_skip, grad_gain)


def solution(mesh):
    in_specs = (
        P("seq", "head"),
        P("seq", "head"),
        P(("seq", "head"), None),
        P(("seq", "head"), None),
        P("head", "seq"),
        P("head"),
        P("head"),
        P("head"),
        P("head"),
        P("seq"),
        P("seq", "head"),
    )
    out_specs = (
        P("seq", "head"),
        P("seq", "head"),
        P(("seq", "head"), None),
        P(("seq", "head"), None),
        P("head", "seq"),
        P("head"),
        P("head"),
        P("head"),
        P("head"),
    )
    return jax.shard_map(shard_body, mesh=mesh, in_specs=in_specs, out_specs=out_specs, check_vma=False)
```

```python
import jax
import jax.numpy as jnp
import numpy as np
from jax import lax
from jax.experimental import pallas as pl
from jax.experimental.pallas import tpu as pltpu
from jax.sharding import PartitionSpec as P

HEADS = 128
HEAD_DIM = 64
STATE = 128
PROJECTION_SETS = 8
EPSILON = 1e-05

T = 1024
H = 16
W = H * HEAD_DIM
L = 256
C = T // L
SEQ = 16
GRP = 8
ROWS = STATE // SEQ
F32 = jnp.float32
BF16 = jnp.bfloat16
STEP = 16
VMEM_LIMIT = 60 * 2**20
VMEM_NEAR = 48 * 2**20

THR, KAP, PRE, TOTAL, BY_ALOG, BY_BIAS, TABLE = 0, 4, 8, 12, 13, 14, 16
ALPHA, DTBETA, TO_END, FROM_START, END_ALOG, END_BIAS = 0, 1, 2, 3, 4, 5
SKIPS, ALOGS, BIASES = 0, 2, 4

NN = (((1,), (0,)), ((), ()))
NT = (((1,), (1,)), ((), ()))
TN = (((0,), (0,)), ((), ()))


def dot(a, b, dims):
    return lax.dot_general(a, b, dims, preferred_element_type=F32)


def split2(a):
    hi = a.astype(BF16)
    return hi, (a - hi.astype(F32)).astype(BF16)


def split3(a):
    hi, mid = split2(a)
    lo = (a - hi.astype(F32) - mid.astype(F32)).astype(BF16)
    return hi, mid, lo


def joined(a, b, dims):
    ((ka,), (kb,)), _ = dims
    return dot(jnp.concatenate(a, ka), jnp.concatenate(b, kb), dims)


def dot2(a, b, dims):
    return joined([a, a], b, dims)


def dot3(a, b, dims):
    return joined([a[0], a[0], a[1]], [b[0], b[1], b[0]], dims)


def dot3_wide(a, b):
    both = dot(a[0], jnp.concatenate(b, 0), NT)
    return both[:, :STATE] + both[:, STATE:] + dot(a[1], b[0], NT)


def each_rows(body):
    for i in range(L // STEP):
        body(slice(STEP * i, STEP * (i + 1)))


class Views:
    def __init__(self, buffers, kinds, c):
        for name, ref in buffers.items():
            kind = kinds[name]
            if kind in ("tok", "near_tok"):
                ref = ref.at[pl.ds(pl.multiple_of(c * L, L), L), :]
            elif kind == "row":
                ref = ref.at[:, pl.ds(pl.multiple_of(c * L, L), L)]
            elif kind == "state":
                ref = ref.at[c]
            setattr(self, name, ref)


def staged(body, ins, outs, scratch, name, flops, backward=False, begin=None, end=None):
    kinds = {k: kind for k, (_, kind) in ins.items()}
    kinds.update({k: kind for k, (_, _, kind) in outs.items()})
    kinds.update({k: "row" if shape == (H, T) else "all" for k, (shape, _) in scratch.items()})
    n, m = len(ins), len(outs)
    moving = ("tok", "state")
    here = [k for k in ins if kinds[k] in ("near", "near_tok")]
    copied = [k for k in outs if kinds[k] == "copy"]
    buffered_in = [k for k in ins if k not in here]
    buffered_out = [k for k in outs if k not in copied]

    def part(ref, kind, c):
        if kind == "tok":
            return ref.at[pl.ds(pl.multiple_of(c * L, L), L), :]
        return ref.at[c]

    def kernel(*refs):
        far_in = dict(zip(ins, refs[:n]))
        far_out = dict(zip(outs, refs[n : n + m]))
        near = dict(zip([*buffered_in, *buffered_out, *scratch], refs[n + m : -1]))
        near.update({k: far_in[k] for k in here})
        sems = refs[-1]
        slot = {k: i for i, k in enumerate([*ins, *outs])}

        def copy_in(k, c):
            return pltpu.make_async_copy(part(far_in[k], kinds[k], c), part(near[k], kinds[k], c), sems.at[slot[k], c])

        def copy_out(k, c):
            return pltpu.make_async_copy(part(near[k], kinds[k], c), part(far_out[k], kinds[k], c), sems.at[slot[k], c])

        once = [
            pltpu.make_async_copy(far_in[k], near[k], sems.at[slot[k], 0])
            for k in buffered_in
            if kinds[k] in ("row", "all")
        ]
        late = [pltpu.make_async_copy(far_in[k], near[k], sems.at[slot[k], 0]) for k in ins if kinds[k] == "late"]
        passed = [
            pltpu.make_async_copy(near[k.removesuffix("_copy")], far_out[k], sems.at[slot[k], 0]) for k in copied
        ]
        for copy in once:
            copy.start()
        for c in reversed(range(C)) if backward else range(C):
            for k in ins:
                if kinds[k] in moving:
                    copy_in(k, c).start()
        for copy in late + passed:
            copy.start()
        for copy in once:
            copy.wait()
        whole = Views(near, {k: "all" for k in near}, 0)
        if begin is not None:
            begin(whole)

        def step(i, carry):
            c = C - 1 - i if backward else i
            for k in ins:
                if kinds[k] in moving:
                    copy_in(k, c).wait()
            body(c, Views(near, kinds, c))
            for k in outs:
                if kinds[k] in moving:
                    copy_out(k, c).start()
            return carry

        lax.fori_loop(0, C, step, 0)
        for copy in late:
            copy.wait()
        if end is not None:
            end(whole)
        once = [
            pltpu.make_async_copy(near[k], far_out[k], sems.at[slot[k], 0])
            for k in buffered_out
            if kinds[k] not in moving
        ]
        for copy in once:
            copy.start()
        for c in range(C):
            for k in outs:
                if kinds[k] in moving:
                    copy_out(k, c).wait()
        for copy in once + passed:
            copy.wait()

    far = pl.BlockSpec(memory_space=pl.ANY)
    return pl.pallas_call(
        kernel,
        out_shape=tuple(pltpu.HBM(s, d) for s, d, _ in outs.values()),
        in_specs=[pl.BlockSpec(memory_space=pltpu.VMEM) if k in here else far for k in ins],
        out_specs=tuple([far] * m),
        scratch_shapes=[
            *[pltpu.VMEM(ins[k][0].shape, ins[k][0].dtype) for k in buffered_in],
            *[pltpu.VMEM(*outs[k][:2]) for k in buffered_out],
            *[pltpu.VMEM(s, d) for s, d in scratch.values()],
            pltpu.SemaphoreType.DMA((n + m, C)),
        ],
        compiler_params=pltpu.CompilerParams(vmem_limit_bytes=VMEM_NEAR if here else VMEM_LIMIT),
        cost_estimate=pl.CostEstimate(flops=flops, bytes_accessed=8 * 2**20, transcendentals=0),
        name=name,
    )(*[pltpu.with_memory_space_constraint(ins[k][0], pltpu.VMEM if k in here else pltpu.HBM) for k in ins])


def expand(pk, which, e3):
    return dot(pk[2 * H * which : 2 * H * (which + 1), :], e3[0 : 2 * H, :], TN)


def prep_kernel(dt_ref, par_ref, st_ref, e3_ref, pk_ref, rf_ref, mask_ref, me_ref, mw_ref, thx_ref):
    bias = par_ref[:, 0:1]
    nega = -jnp.exp(par_ref[:, 1:2])
    row = lax.broadcasted_iota(jnp.int32, (L, L), 0)
    col = lax.broadcasted_iota(jnp.int32, (L, L), 1)
    tri = (row <= col).astype(F32).astype(BF16)
    causal = row >= col
    first = lax.broadcasted_iota(jnp.int32, (H, L), 0) == 0
    lane = lax.broadcasted_iota(jnp.int32, (H, 128), 1)
    ones = jnp.ones((H, L), BF16)
    thr, kap, leave, enter, rest, ratio, sig_rest, rate_sum, sig_sum = [], [], [], [], [], [], [], [], []

    def put(which, at, value):
        base = 2 * H * which
        pk_ref[base : base + H, at], pk_ref[base + H : base + 2 * H, at] = split2(value)

    for c in range(C):
        at = slice(c * L, (c + 1) * L)
        pre = dt_ref[:, at] + bias
        dt = jax.nn.softplus(pre)
        rf_ref[0:H, at] = dt
        sig = jax.nn.sigmoid(pre)
        rf_ref[H : 2 * H, at] = sig
        rate = dt * nega
        parts = dot(jnp.concatenate(split3(rate) + split3(sig), 0), tri, NN)
        cum = parts[0:H] + parts[H : 2 * H] + parts[2 * H : 3 * H]
        sig_cum = parts[3 * H : 4 * H] + parts[4 * H : 5 * H] + parts[5 * H : 6 * H]
        starts = jnp.broadcast_to(st_ref[:, at].astype(F32), (H, L))
        seg = dot(starts.astype(BF16), tri, NN)
        cum_end = cum[:, L - 1 : L]
        seg_end = seg[:, L - 1 : L]
        half = 0.5 * cum_end
        put(ALPHA, at, jnp.exp(cum - half))
        put(DTBETA, at, dt * jnp.exp(half - cum))
        leave.append(jnp.where(seg == seg_end, dt * jnp.exp(cum_end - cum), 0.0))
        rest.append(cum_end - cum)
        ratio.append(sig / dt)
        sig_rest.append(sig_cum[:, L - 1 : L] - sig_cum)
        rate_sum.append(cum_end)
        sig_sum.append(sig_cum[:, L - 1 : L])
        enter.append(jnp.where(seg == 0.0, jnp.exp(cum), 0.0))
        seg_first = jnp.where(first, seg, 0.0).astype(BF16)
        seg_col = dot(seg_first, ones, TN)
        mask = causal & (seg_col == seg[0:1, :])
        mask_ref[at, :] = mask.astype(F32).astype(BF16)
        to_end = jnp.where(first & (seg == seg_end), 1.0, 0.0).astype(BF16)
        from_start = jnp.where(first & (seg == 0.0), 1.0, 0.0).astype(BF16)
        me_ref[at, :] = dot(to_end, ones[:, :128], TN).astype(BF16)
        mw_ref[at, :] = dot(from_start, ones[:, :128], TN).astype(BF16)
        thr.append(jnp.where(seg_end == 0.0, jnp.exp(cum_end), 0.0))
        kap.append(jnp.exp(half))
    passed = jnp.ones((H, 1), F32)
    before = []
    for c in range(C):
        before.append(passed)
        put(FROM_START, slice(c * L, (c + 1) * L), enter[c] * passed)
        passed = passed * thr[c]
    columns = [*thr, *kap, *before, passed, passed * sum(rate_sum), passed * nega * sum(sig_sum)]
    passed = jnp.ones((H, 1), F32)
    rate_after = jnp.zeros((H, 1), F32)
    sig_after = jnp.zeros((H, 1), F32)
    for c in reversed(range(C)):
        at = slice(c * L, (c + 1) * L)
        to_shard_end = leave[c] * passed
        put(TO_END, at, to_shard_end)
        put(END_ALOG, at, to_shard_end * (rest[c] + rate_after))
        put(END_BIAS, at, to_shard_end * (ratio[c] + nega * (sig_rest[c] + sig_after)))
        passed = passed * thr[c]
        rate_after += rate_sum[c]
        sig_after += sig_sum[c]
    table = jnp.zeros((H, 128), F32)
    for k, v in enumerate(columns):
        table = jnp.where(lane == k, v, table)
    wide = dot(jnp.concatenate(split3(table), 0), e3_ref[...], TN)
    thx_ref[...] = wide[0:TABLE]


def scale_body(c, r):
    scale = expand(r.pk, TO_END, r.e3)

    def rows(at):
        r.xhi[at, :], r.xlo[at, :] = split2(r.x[at, :].astype(F32) * scale[at, :])

    each_rows(rows)


def states_body(c, r):
    r.acc[...] += dot2(r.bc[:, :STATE], (r.xhi[...], r.xlo[...]), TN)


def clear(r):
    r.acc[...] = jnp.zeros((STATE, W), F32)


def states_end(r):
    r.pay[:, :W] = r.acc[...]
    total = r.thx[TOTAL : TOTAL + 1, :]
    block = jnp.concatenate([total[:, 128 * k : 128 * (k + 1)] for k in range(ROWS)], 0)
    for d in range(SEQ):
        r.pay[ROWS * d : ROWS * (d + 1), W:] = block


def moments_body(c, r):
    by_alog = expand(r.pk, END_ALOG, r.e3)
    by_bias = expand(r.pk, END_BIAS, r.e3)

    def rows(at):
        x = r.x[at, :].astype(F32)
        r.hi[at, :], r.lo[at, :] = split2(x * by_alog[at, :])
        r.hi2[at, :], r.lo2[at, :] = split2(x * by_bias[at, :])

    each_rows(rows)
    b = r.bc[:, :STATE]
    r.moments[:, :W] += dot2(b, (r.hi[...], r.lo[...]), TN)
    r.moments[:, W:] += dot2(b, (r.hi2[...], r.lo2[...]), TN)


def moments_begin(r):
    r.moments[...] = jnp.zeros((STATE, 2 * W), F32)


def through_row(got_ref, j):
    block = got_ref[ROWS * j : ROWS * (j + 1), W:]
    return jnp.concatenate([block[k : k + 1, :] for k in range(ROWS)], 1)


def scan_forward_kernel(got_ref, out_ref, through_ref):
    acc = jnp.zeros((ROWS, W), F32)
    for j in range(SEQ):
        at = slice(ROWS * j, ROWS * (j + 1))
        out_ref[at, :] = acc
        through = through_row(got_ref, j)
        through_ref[j : j + 1, :] = through
        acc = through * acc + got_ref[at, :W]


def scan_backward_kernel(got_ref, through_ref, loc_ref, sums_ref, e3_ref, out_ref):
    acc = jnp.zeros((ROWS, W), F32)
    by_alog = jnp.zeros((ROWS, W), F32)
    by_bias = jnp.zeros((ROWS, W), F32)
    for j in reversed(range(SEQ)):
        at = slice(ROWS * j, ROWS * (j + 1))
        out_ref[at, :W] = acc
        by_alog += acc * got_ref[at, W : 2 * W]
        by_bias += acc * got_ref[at, 2 * W :]
        acc = through_ref[j : j + 1, :] * acc + got_ref[at, :W]
    row = lax.broadcasted_iota(jnp.int32, (H, W), 0)
    vector = jnp.where(
        row == 0,
        jnp.sum(by_alog, axis=0, keepdims=True),
        jnp.where(row == 1, jnp.sum(by_bias, axis=0, keepdims=True), 0.0),
    )
    heads = e3_ref[0:H, :]
    far = sum(dot(heads, part, NT) for part in split3(vector))
    lane = lax.broadcasted_iota(jnp.int32, (ROWS, 128), 1)
    right = jnp.zeros((ROWS, 128), F32)
    for k in range(2):
        at = slice(ROWS * k, ROWS * (k + 1))
        right = jnp.where(lane == SKIPS + k, loc_ref[at, 0:1], right)
        right = jnp.where(lane == ALOGS + k, loc_ref[at, 1:2] + far[at, 0:1], right)
        right = jnp.where(lane == BIASES + k, loc_ref[at, 2:3] + far[at, 1:2], right)
    gains = sums_ref[0:1, :]
    left = jnp.concatenate([gains[:, 128 * k : 128 * (k + 1)] for k in range(8)], 0)
    for d in range(SEQ):
        out_ref[ROWS * d : ROWS * (d + 1), W : W + 128] = left
        out_ref[ROWS * d : ROWS * (d + 1), W + 128 :] = right


def within_body(c, r):
    ex = expand(r.pk, DTBETA, r.e3)
    al = expand(r.pk, ALPHA, r.e3)

    def scale(at):
        r.hi[at, :], r.lo[at, :] = split2(r.x[at, :].astype(F32) * ex[at, :])

    each_rows(scale)
    b = r.bc[:, :STATE]
    cc = r.bc[:, STATE:]
    g = split2(dot(cc, b, NT) * r.mask[...].astype(F32))
    xs = (r.hi[...], r.lo[...])
    kappa = r.thx[pl.ds(KAP + c, 1), :]
    r.sloc[...] = r.acc[...]
    res = dot3(g, xs, NN) + dot2(cc * r.mw[...], split2(kappa * r.acc[...]), NN)
    r.ys[...] = al * res
    r.acc[...] = r.thx[pl.ds(THR + c, 1), :] * r.acc[...] + kappa * dot2(b * r.me[...], xs, TN)


def norm_begin(r):
    r.shi[...], r.slo[...] = split2(r.sin[...])
    r.gain_acc[...] = jnp.zeros((8, W), F32)
    r.skip_acc[...] = jnp.zeros((8, W), F32)
    r.back[:, :W] = jnp.zeros((STATE, W), F32)


def norm_body(c, r):
    cc = r.bc[:, STATE:]
    win = expand(r.pk, FROM_START, r.e3)
    res = dot2(cc, (r.shi[...], r.slo[...]), NN)
    gain = r.vec[0:1, :]
    skip = r.vec[1:2, :]

    def body(at):
        weight = win[at, :]
        x = r.x[at, :].astype(F32)
        z = r.z[at, :].astype(F32)
        out = r.go[at, :].astype(F32)
        ys = r.ys[at, :] + weight * res[at, :]
        y = ys + skip * x
        logistic = jax.nn.sigmoid(z)
        silu = z * logistic
        gated = y * silu
        grad_normed = out * gain
        square = jnp.sum(gated * gated, axis=1, keepdims=True) * (1.0 / W)
        cross = jnp.sum(grad_normed * gated, axis=1, keepdims=True) * (1.0 / W)
        inv = lax.rsqrt(square + EPSILON)
        normed = gated * inv
        grad_gated = inv * (grad_normed - normed * (inv * cross))
        gy = grad_gated * silu
        gz = grad_gated * y * (logistic + silu * (1.0 - logistic))
        r.gz[at, :] = gz.astype(BF16)
        r.gy[at, :] = gy
        gpart = out * normed
        spart = gy * x
        r.gain_acc[...] += gpart[0:8] + gpart[8:16]
        r.skip_acc[...] += spart[0:8] + spart[8:16]
        r.hi[at, :], r.lo[at, :] = split2(gy * weight)
        r.rhi[at, :], r.rlo[at, :] = split2(gy * ys)

    each_rows(body)
    r.r[...] = dot2(r.e3[0:H, :], (r.rhi[...], r.rlo[...]), NT)
    new = dot2(cc, (r.hi[...], r.lo[...]), TN)
    r.back[:, :W] += new


def norm_end(r):
    r.back[:, W : 2 * W] = r.moments[:, :W] + r.thx[BY_ALOG : BY_ALOG + 1, :] * r.sin[...]
    r.back[:, 2 * W :] = r.moments[:, W:] + r.thx[BY_BIAS : BY_BIAS + 1, :] * r.sin[...]
    r.sums[0:1, :] = jnp.sum(r.gain_acc[...], axis=0, keepdims=True)
    r.sums[1:2, :] = jnp.sum(r.skip_acc[...], axis=0, keepdims=True)
    r.sums[2:8, :] = jnp.zeros((6, W), F32)


def local_x_body(c, r):
    ex = expand(r.pk, DTBETA, r.e3)
    al = expand(r.pk, ALPHA, r.e3)

    def scale(at):
        r.ghi[at, :], r.glo[at, :] = split2(r.gy[at, :] * al[at, :])

    each_rows(scale)
    b = r.bc[:, :STATE]
    cc = r.bc[:, STATE:]
    gys = (r.ghi[...], r.glo[...])
    g = split2(dot(cc, b, NT) * r.mask[...].astype(F32))
    kappa = r.thx[pl.ds(KAP + c, 1), :]
    r.dloc[...] = r.acc[...]
    res = dot3(g, gys, TN) + dot2(b * r.me[...], split2(kappa * r.acc[...]), NN)
    skip = r.vec[1:2, :]

    def finish(at):
        scaled = ex[at, :] * res[at, :]
        r.gx[at, :] = scaled + skip * r.gy[at, :]
        r.rhi[at, :], r.rlo[at, :] = split2(scaled * r.x[at, :].astype(F32))

    each_rows(finish)
    r.u[...] = dot2(r.e3[0:H, :], (r.rhi[...], r.rlo[...]), NT)
    state = split2(kappa * (r.sloc[...] + r.thx[pl.ds(PRE + c, 1), :] * r.sin[...]))
    r.gcs[...] = r.mw[...].astype(F32) * dot3_wide(gys, state)
    r.acc[...] = r.thx[pl.ds(THR + c, 1), :] * r.acc[...] + kappa * dot2(cc * r.mw[...], gys, TN)


def local_bc_body(c, r):
    ex = expand(r.pk, DTBETA, r.e3)
    al = expand(r.pk, ALPHA, r.e3)

    def scale(at):
        r.xhi[at, :], r.xlo[at, :] = split2(r.x[at, :].astype(F32) * ex[at, :])
        r.ghi[at, :], r.glo[at, :] = split2(r.gy[at, :] * al[at, :])

    each_rows(scale)
    b = r.bc[:, :STATE]
    cc = r.bc[:, STATE:]
    gys = (r.ghi[...], r.glo[...])
    xs = (r.xhi[...], r.xlo[...])
    q = split2(dot3(gys, xs, NT) * r.mask[...].astype(F32))
    kappa = r.thx[pl.ds(KAP + c, 1), :]
    dstate = split2(kappa * r.dloc[...])
    gb = joined(q, [cc, cc], TN) + r.me[...].astype(F32) * dot3_wide(xs, dstate)
    r.gb[...] = gb
    r.gc[...] = (r.gcs[...] + joined(q, [b, b], NN)).astype(BF16)


def final_begin(r):
    r.dhi[...], r.dlo[...] = split2(r.din[:, :W])


def final_bc_body(c, r):
    gb = r.gb[...] + dot3_wide((r.xhi[...], r.xlo[...]), (r.dhi[...], r.dlo[...]))
    r.out[:, :STATE] = gb.astype(BF16)
    r.out[:, STATE:] = r.gc[...]


def final_bc_end(r):
    total = r.din[0:ROWS, W:]
    for d in range(1, SEQ):
        total += r.din[ROWS * d : ROWS * (d + 1), W:]
    r.params[...] = total


def final_x_body(c, r):
    fin = expand(r.pk, TO_END, r.e3)
    v = dot2(r.bc[:, :STATE], (r.dhi[...], r.dlo[...]), NN)

    def body(at):
        scaled = fin[at, :] * v[at, :]
        r.gxo[at, :] = (r.gx[at, :] + scaled).astype(BF16)
        r.rhi[at, :], r.rlo[at, :] = split2(scaled * r.x[at, :].astype(F32))

    each_rows(body)
    r.uu[...] = r.u[...] + dot2(r.e3[0:H, :], (r.rhi[...], r.rlo[...]), NT)


def time_sums(r, u_ref, carry, write):
    row = lax.broadcasted_iota(jnp.int32, (L, L), 0)
    col = lax.broadcasted_iota(jnp.int32, (L, L), 1)
    tri = (row >= col).astype(F32).astype(BF16)
    nega = -jnp.exp(r.par[:, 1:2])
    for c in reversed(range(C)):
        at = slice(c * L, (c + 1) * L)
        u = u_ref[:, at]
        dt = r.rf[0:H, at]
        parts = dot(jnp.concatenate(split3(r.r[:, at] - u), 0), tri, NN)
        later = parts[0:H] + parts[H : 2 * H] + parts[2 * H : 3 * H]
        grad_rate = later + carry
        carry = carry + later[:, 0:1]
        write(at, (u / dt + grad_rate * nega) * r.rf[H : 2 * H, at], grad_rate * dt * nega)


def local_x_end(r):
    sums = [jnp.zeros((H, 1), F32)] * 2

    def write(at, grad_dt, grad_alog):
        sums[0] += jnp.sum(grad_alog, axis=1, keepdims=True)
        sums[1] += jnp.sum(grad_dt, axis=1, keepdims=True)

    time_sums(r, r.u, jnp.zeros((H, 1), F32), write)
    skips = jnp.broadcast_to(r.sums[1:2, :], (H, W))
    skip_part = sum(dot(r.e3[0:H, :], part, NT) for part in split3(skips))[:, 0:1]
    lane = lax.broadcasted_iota(jnp.int32, (H, 128), 1)
    r.loc[...] = jnp.where(
        lane == 0, skip_part, jnp.where(lane == 1, sums[0], jnp.where(lane == 2, sums[1], 0.0))
    )


def final_x_end(r):
    state = r.pay[:, :W] + r.thx[TOTAL : TOTAL + 1, :] * r.sin[...]
    ends = jnp.broadcast_to(jnp.sum(state * r.din[:, :W], axis=0, keepdims=True), (H, W))
    carry = sum(dot(r.e3[0:H, :], part, NT) for part in split3(ends))[:, 0:1]

    def write(at, grad_dt, grad_alog):
        r.gdt[:, at] = grad_dt

    time_sums(r, r.uu, carry, write)


def pack_kernel(b_ref, c_ref, out_ref):
    for g in range(GRP):
        at = slice(STATE * g, STATE * (g + 1))
        out_ref[g, :, :STATE] = b_ref[:, at]
        out_ref[g, :, STATE:] = c_ref[:, at]


def unpack_kernel(in_ref, b_ref, c_ref, sems):
    copies = []
    for g in range(GRP):
        at = slice(STATE * g, STATE * (g + 1))
        for k, ref in enumerate((b_ref, c_ref)):
            source = in_ref.at[g, :, STATE * k : STATE * (k + 1)]
            copies.append(pltpu.make_async_copy(source, ref.at[:, at], sems.at[k, g]))
    for copy in copies:
        copy.start()
    for copy in copies:
        copy.wait()


def head_matrix():
    one = np.arange(W)[None, :] // HEAD_DIM == np.arange(H)[:, None]
    return jnp.asarray(np.concatenate([one, one, one], 0), BF16)


def shard_body(
    x_in, z_gate, b_proj, c_proj, dt_raw, dt_bias, a_log, skip, norm_weight, doc_starts, grad_out
):
    e3 = head_matrix()
    par = jnp.pad(jnp.stack([dt_bias, a_log], 1), ((0, 0), (0, 126)))
    vec = jnp.pad(
        jnp.stack([norm_weight, jnp.repeat(skip, HEAD_DIM)], 0), ((0, 6), (0, 0))
    )
    starts = doc_starts.reshape(1, T)
    far = pl.BlockSpec(memory_space=pl.ANY)
    mine = pl.pallas_call(
        pack_kernel,
        out_shape=pltpu.HBM((GRP, 128, 2 * STATE), BF16),
        compiler_params=pltpu.CompilerParams(vmem_limit_bytes=VMEM_LIMIT),
        name="pack",
    )(*[pltpu.with_memory_space_constraint(a, pltpu.HBM) for a in (b_proj, c_proj)])
    bc = lax.all_to_all(mine, "head", split_axis=0, concat_axis=0, tiled=True).reshape(T, 2 * STATE)

    sds = pltpu.HBM
    pk, rf, mask, me, mw, thx = pl.pallas_call(
        prep_kernel,
        out_shape=(
            sds((12 * H, T), BF16),
            sds((2 * H, T), F32),
            sds((T, L), BF16),
            sds((T, 128), BF16),
            sds((T, 128), BF16),
            sds((TABLE, W), F32),
        ),
        compiler_params=pltpu.CompilerParams(vmem_limit_bytes=VMEM_LIMIT),
        name="prep",
    )(*[pltpu.with_memory_space_constraint(a, pltpu.HBM) for a in (dt_raw, par, starts, e3)])

    state = ((STATE, W), F32)
    half = ((L, W), BF16)
    unit = 2 * T * L * W
    common = {"e3": (e3, "all"), "pk": (pk, "row"), "thx": (thx, "all")}
    x = {"x": (x_in, "tok")}
    masks = {"mask": (mask, "tok"), "me": (me, "tok"), "mw": (mw, "tok")}

    xhi, xlo = staged(
        scale_body,
        {"e3": (e3, "all"), "pk": (pk, "row")} | x,
        {"xhi": ((T, W), BF16, "tok"), "xlo": ((T, W), BF16, "tok")},
        {},
        "scale",
        unit,
    )
    xhi, xlo, bc = lax.optimization_barrier((xhi, xlo, bc))
    pay, bc = staged(
        states_body,
        {"thx": (thx, "all"), "bc": (bc, "near_tok"), "xhi": (xhi, "tok"), "xlo": (xlo, "tok")},
        {"pay": ((STATE, W + 128), F32, "all"), "bc_copy": ((T, 2 * STATE), BF16, "copy")},
        {"acc": state},
        "states",
        2 * unit,
        begin=clear,
        end=states_end,
    )

    def scan(kernel, name, outs, got, *others):
        return pl.pallas_call(
            kernel,
            out_shape=outs,
            in_specs=[pl.BlockSpec(memory_space=pltpu.VMEM)] * (1 + len(others)),
            compiler_params=pltpu.CompilerParams(vmem_limit_bytes=16 * 2**20),
            name=name,
        )(
            pltpu.with_memory_space_constraint(got, pltpu.VMEM),
            *[pltpu.with_memory_space_constraint(a, pltpu.HBM) for a in others],
        )

    def exchange(v):
        return lax.all_to_all(v, "seq", split_axis=0, concat_axis=0, tiled=True)

    bcs = {"bc": (bc, "tok")}
    got = exchange(pay)
    ys, sloc = staged(
        within_body,
        common | bcs | masks | x,
        {
            "ys": ((T, W), F32, "tok"),
            "sloc": ((C, STATE, W), F32, "state"),
        },
        {"acc": state, "hi": half, "lo": half},
        "within",
        7 * unit,
        begin=clear,
    )
    ys, sloc, got = lax.optimization_barrier((ys, sloc, got))
    before, through = scan(
        scan_forward_kernel, "scan_forward", (sds((STATE, W), F32), sds((SEQ, W), F32)), got
    )
    sin = exchange(before)
    tied, _ = lax.optimization_barrier((x_in, got))
    (moments,) = staged(
        moments_body,
        {"e3": (e3, "all"), "pk": (pk, "row")} | bcs | {"x": (tied, "tok")},
        {"moments": ((STATE, 2 * W), F32, "all")},
        {"hi": half, "lo": half, "hi2": half, "lo2": half},
        "moments",
        4 * unit,
        begin=moments_begin,
    )
    moments, sin = lax.optimization_barrier((moments, sin))

    gy, gz, r, back, sums, sin = staged(
        norm_body,
        common
        | {"vec": (vec, "all"), "sin": (sin, "near")}
        | bcs
        | {"ys": (ys, "tok"), "z": (z_gate, "tok"), "go": (grad_out, "tok")}
        | x
        | {"moments": (moments, "late")},
        {
            "gy": ((T, W), F32, "tok"),
            "gz": ((T, W), BF16, "tok"),
            "r": ((H, T), F32, "row"),
            "back": ((STATE, 3 * W), F32, "all"),
            "sums": ((8, W), F32, "all"),
            "sin_copy": ((STATE, W), F32, "copy"),
        },
        {
            "gain_acc": ((8, W), F32),
            "skip_acc": ((8, W), F32),
            "shi": ((STATE, W), BF16),
            "slo": ((STATE, W), BF16),
            "hi": half,
            "lo": half,
            "rhi": half,
            "rlo": half,
        },
        "norm",
        6 * unit,
        begin=norm_begin,
        end=norm_end,
    )

    got_back = exchange(back)
    gx, u, dloc, gcs, loc = staged(
        local_x_body,
        common
        | {
            "vec": (vec, "all"),
            "sin": (sin, "all"),
            "par": (par, "all"),
            "sums": (sums, "all"),
            "rf": (rf, "row"),
            "r": (r, "row"),
        }
        | bcs
        | masks
        | {"gy": (gy, "tok"), "sloc": (sloc, "state")}
        | x,
        {
            "gx": ((T, W), F32, "tok"),
            "u": ((H, T), F32, "row"),
            "dloc": ((C, STATE, W), F32, "state"),
            "gcs": ((T, STATE), F32, "tok"),
            "loc": ((H, 128), F32, "all"),
        },
        {"acc": state, "ghi": half, "glo": half, "rhi": half, "rlo": half},
        "local_x",
        7 * unit,
        backward=True,
        begin=clear,
        end=local_x_end,
    )
    dloc, got_back = lax.optimization_barrier((dloc, got_back))
    behind = scan(
        scan_backward_kernel, "scan_backward", sds((STATE, W + 256), F32), got_back, through, loc, sums, e3
    )
    din = exchange(behind)
    gb, gc = staged(
        local_bc_body,
        common
        | bcs
        | masks
        | {"gy": (gy, "tok"), "dloc": (dloc, "state"), "gcs": (gcs, "tok")}
        | x,
        {"gb": ((T, STATE), F32, "tok"), "gc": ((T, STATE), BF16, "tok")},
        {"ghi": half, "glo": half, "xhi": half, "xlo": half},
        "local_bc",
        5 * unit,
    )

    gb, din = lax.optimization_barrier((gb, din))
    gbc, din, params = staged(
        final_bc_body,
        {
            "din": (din, "near"),
            "gb": (gb, "tok"),
            "gc": (gc, "tok"),
            "xhi": (xhi, "tok"),
            "xlo": (xlo, "tok"),
        },
        {
            "out": ((T, 2 * STATE), BF16, "tok"),
            "din_copy": ((STATE, W + 256), F32, "copy"),
            "params": ((ROWS, 256), F32, "all"),
        },
        {"dhi": ((STATE, W), BF16), "dlo": ((STATE, W), BF16)},
        "final_bc",
        2 * unit,
        begin=final_begin,
        end=final_bc_end,
    )
    gbc, gx = lax.optimization_barrier((gbc, gx))
    back_bc = lax.all_to_all(
        gbc.reshape(GRP, 128, 2 * STATE), "head", split_axis=0, concat_axis=0, tiled=True
    )
    grad_x, grad_dt = staged(
        final_x_body,
        common
        | {
            "din": (din, "all"),
            "sin": (sin, "all"),
            "pay": (pay, "all"),
            "par": (par, "all"),
            "rf": (rf, "row"),
            "r": (r, "row"),
            "u": (u, "row"),
        }
        | bcs
        | {"gx": (gx, "tok")}
        | x,
        {"gxo": ((T, W), BF16, "tok"), "gdt": ((H, T), F32, "row")},
        {
            "uu": ((H, T), F32),
            "dhi": ((STATE, W), BF16),
            "dlo": ((STATE, W), BF16),
            "rhi": half,
            "rlo": half,
        },
        "final_x",
        3 * unit,
        begin=final_begin,
        end=final_x_end,
    )
    grad_b, grad_c = pl.pallas_call(
        unpack_kernel,
        out_shape=(pltpu.HBM((128, GRP * STATE), BF16), pltpu.HBM((128, GRP * STATE), BF16)),
        in_specs=[pl.BlockSpec(memory_space=pltpu.VMEM)],
        out_specs=(far, far),
        scratch_shapes=[pltpu.SemaphoreType.DMA((2, GRP))],
        compiler_params=pltpu.CompilerParams(vmem_limit_bytes=16 * 2**20),
        name="unpack",
    )(pltpu.with_memory_space_constraint(back_bc, pltpu.VMEM))
    grad_gain = params[:, :128].reshape(W)

    def by_head(at):
        return params[:, 128 + at : 130 + at].T.reshape(H)

    grad_skip, grad_alog, grad_bias = by_head(SKIPS), by_head(ALOGS), by_head(BIASES)
    return (grad_x, gz, grad_b, grad_c, grad_dt, grad_alog, grad_bias, grad_skip, grad_gain)


def solution(mesh):
    in_specs = (
        P("seq", "head"),
        P("seq", "head"),
        P(("seq", "head"), None),
        P(("seq", "head"), None),
        P("head", "seq"),
        P("head"),
        P("head"),
        P("head"),
        P("head"),
        P("seq"),
        P("seq", "head"),
    )
    out_specs = (
        P("seq", "head"),
        P("seq", "head"),
        P(("seq", "head"), None),
        P(("seq", "head"), None),
        P("head", "seq"),
        P("head"),
        P("head"),
        P("head"),
        P("head"),
    )
    return jax.shard_map(shard_body, mesh=mesh, in_specs=in_specs, out_specs=out_specs, check_vma=False)
```

```python
import jax
import jax.numpy as jnp
import numpy as np
from jax import lax
from jax.experimental import pallas as pl
from jax.experimental.pallas import tpu as pltpu
from jax.sharding import PartitionSpec as P

HEADS = 128
HEAD_DIM = 64
STATE = 128
PROJECTION_SETS = 8
EPSILON = 1e-05

T = 1024
H = 16
W = H * HEAD_DIM
L = 256
C = T // L
SEQ = 16
GRP = 8
ROWS = STATE // SEQ
F32 = jnp.float32
BF16 = jnp.bfloat16
STEP = 16
VMEM_LIMIT = 60 * 2**20
VMEM_NEAR = 48 * 2**20

THR, KAP, PRE, TOTAL, BY_ALOG, BY_BIAS, BASE, TABLE = 0, 4, 8, 12, 13, 14, 15, 16
ALPHA, DTBETA, TO_END, FROM_START, END_ALOG, END_BIAS = 0, 1, 2, 3, 4, 5
SKIPS, ALOGS, BIASES = 0, 2, 4

NN = (((1,), (0,)), ((), ()))
NT = (((1,), (1,)), ((), ()))
TN = (((0,), (0,)), ((), ()))


def dot(a, b, dims):
    return lax.dot_general(a, b, dims, preferred_element_type=F32)


def split2(a):
    hi = a.astype(BF16)
    return hi, (a - hi.astype(F32)).astype(BF16)


def split3(a):
    hi, mid = split2(a)
    lo = (a - hi.astype(F32) - mid.astype(F32)).astype(BF16)
    return hi, mid, lo


def joined(a, b, dims):
    ((ka,), (kb,)), _ = dims
    return dot(jnp.concatenate(a, ka), jnp.concatenate(b, kb), dims)


def dot2(a, b, dims):
    return joined([a, a], b, dims)


def dot3(a, b, dims):
    return joined([a[0], a[0], a[1]], [b[0], b[1], b[0]], dims)


def dot3_wide(a, b):
    both = dot(a[0], jnp.concatenate(b, 0), NT)
    return both[:, :STATE] + both[:, STATE:] + dot(a[1], b[0], NT)


def each_rows(body):
    for i in range(L // STEP):
        body(slice(STEP * i, STEP * (i + 1)))


class Views:
    def __init__(self, buffers, kinds, c):
        for name, ref in buffers.items():
            kind = kinds[name]
            if kind in ("tok", "near_tok"):
                ref = ref.at[pl.ds(pl.multiple_of(c * L, L), L), :]
            elif kind == "row":
                ref = ref.at[:, pl.ds(pl.multiple_of(c * L, L), L)]
            elif kind == "state":
                ref = ref.at[c]
            setattr(self, name, ref)


def staged(body, ins, outs, scratch, name, flops, backward=False, begin=None, end=None):
    kinds = {k: kind for k, (_, kind) in ins.items()}
    kinds.update({k: kind for k, (_, _, kind) in outs.items()})
    kinds.update({k: "row" if shape == (H, T) else "all" for k, (shape, _) in scratch.items()})
    n, m = len(ins), len(outs)
    moving = ("tok", "state")
    here = [k for k in ins if kinds[k] in ("near", "near_tok")]
    copied = [k for k in outs if kinds[k] == "copy"]
    buffered_in = [k for k in ins if k not in here]
    buffered_out = [k for k in outs if k not in copied]

    def part(ref, kind, c):
        if kind == "tok":
            return ref.at[pl.ds(pl.multiple_of(c * L, L), L), :]
        return ref.at[c]

    def kernel(*refs):
        far_in = dict(zip(ins, refs[:n]))
        far_out = dict(zip(outs, refs[n : n + m]))
        near = dict(zip([*buffered_in, *buffered_out, *scratch], refs[n + m : -1]))
        near.update({k: far_in[k] for k in here})
        sems = refs[-1]
        slot = {k: i for i, k in enumerate([*ins, *outs])}

        def copy_in(k, c):
            return pltpu.make_async_copy(part(far_in[k], kinds[k], c), part(near[k], kinds[k], c), sems.at[slot[k], c])

        def copy_out(k, c):
            return pltpu.make_async_copy(part(near[k], kinds[k], c), part(far_out[k], kinds[k], c), sems.at[slot[k], c])

        once = [
            pltpu.make_async_copy(far_in[k], near[k], sems.at[slot[k], 0])
            for k in buffered_in
            if kinds[k] in ("row", "all")
        ]
        late = [pltpu.make_async_copy(far_in[k], near[k], sems.at[slot[k], 0]) for k in ins if kinds[k] == "late"]
        passed = [
            pltpu.make_async_copy(near[k.removesuffix("_copy")], far_out[k], sems.at[slot[k], 0]) for k in copied
        ]
        for copy in once:
            copy.start()
        for c in reversed(range(C)) if backward else range(C):
            for k in ins:
                if kinds[k] in moving:
                    copy_in(k, c).start()
        for copy in late + passed:
            copy.start()
        for copy in once:
            copy.wait()
        whole = Views(near, {k: "all" for k in near}, 0)
        if begin is not None:
            begin(whole)

        def step(i, carry):
            c = C - 1 - i if backward else i
            for k in ins:
                if kinds[k] in moving:
                    copy_in(k, c).wait()
            body(c, Views(near, kinds, c))
            for k in outs:
                if kinds[k] in moving:
                    copy_out(k, c).start()
            return carry

        lax.fori_loop(0, C, step, 0)
        for copy in late:
            copy.wait()
        if end is not None:
            end(whole)
        once = [
            pltpu.make_async_copy(near[k], far_out[k], sems.at[slot[k], 0])
            for k in buffered_out
            if kinds[k] not in moving
        ]
        for copy in once:
            copy.start()
        for c in range(C):
            for k in outs:
                if kinds[k] in moving:
                    copy_out(k, c).wait()
        for copy in once + passed:
            copy.wait()

    far = pl.BlockSpec(memory_space=pl.ANY)
    return pl.pallas_call(
        kernel,
        out_shape=tuple(pltpu.HBM(s, d) for s, d, _ in outs.values()),
        in_specs=[pl.BlockSpec(memory_space=pltpu.VMEM) if k in here else far for k in ins],
        out_specs=tuple([far] * m),
        scratch_shapes=[
            *[pltpu.VMEM(ins[k][0].shape, ins[k][0].dtype) for k in buffered_in],
            *[pltpu.VMEM(*outs[k][:2]) for k in buffered_out],
            *[pltpu.VMEM(s, d) for s, d in scratch.values()],
            pltpu.SemaphoreType.DMA((n + m, C)),
        ],
        compiler_params=pltpu.CompilerParams(vmem_limit_bytes=VMEM_NEAR if here else VMEM_LIMIT),
        cost_estimate=pl.CostEstimate(flops=flops, bytes_accessed=8 * 2**20, transcendentals=0),
        name=name,
    )(*[pltpu.with_memory_space_constraint(ins[k][0], pltpu.VMEM if k in here else pltpu.HBM) for k in ins])


def expand(pk, which, e3):
    return dot(pk[2 * H * which : 2 * H * (which + 1), :], e3[0 : 2 * H, :], TN)


def prep_kernel(dt_ref, par_ref, st_ref, e3_ref, pk_ref, rf_ref, mask_ref, me_ref, mw_ref, thx_ref):
    bias = par_ref[:, 0:1]
    nega = -jnp.exp(par_ref[:, 1:2])
    row = lax.broadcasted_iota(jnp.int32, (L, L), 0)
    col = lax.broadcasted_iota(jnp.int32, (L, L), 1)
    tri = (row <= col).astype(F32).astype(BF16)
    causal = row >= col
    first = lax.broadcasted_iota(jnp.int32, (H, L), 0) == 0
    lane = lax.broadcasted_iota(jnp.int32, (H, 128), 1)
    ones = jnp.ones((H, L), BF16)
    thr, kap, leave, enter, rest, ratio, sig_rest, rate_sum, sig_sum = [], [], [], [], [], [], [], [], []

    def put(which, at, value):
        base = 2 * H * which
        pk_ref[base : base + H, at], pk_ref[base + H : base + 2 * H, at] = split2(value)

    for c in range(C):
        at = slice(c * L, (c + 1) * L)
        pre = dt_ref[:, at] + bias
        dt = jax.nn.softplus(pre)
        rf_ref[0:H, at] = dt
        sig = jax.nn.sigmoid(pre)
        rf_ref[H : 2 * H, at] = sig
        rate = dt * nega
        parts = dot(jnp.concatenate(split3(rate) + split3(sig), 0), tri, NN)
        cum = parts[0:H] + parts[H : 2 * H] + parts[2 * H : 3 * H]
        sig_cum = parts[3 * H : 4 * H] + parts[4 * H : 5 * H] + parts[5 * H : 6 * H]
        starts = jnp.broadcast_to(st_ref[:, at].astype(F32), (H, L))
        seg = dot(starts.astype(BF16), tri, NN)
        cum_end = cum[:, L - 1 : L]
        seg_end = seg[:, L - 1 : L]
        half = 0.5 * cum_end
        put(ALPHA, at, jnp.exp(cum - half))
        put(DTBETA, at, dt * jnp.exp(half - cum))
        leave.append(jnp.where(seg == seg_end, dt * jnp.exp(cum_end - cum), 0.0))
        rest.append(cum_end - cum)
        ratio.append(sig / dt)
        sig_rest.append(sig_cum[:, L - 1 : L] - sig_cum)
        rate_sum.append(cum_end)
        sig_sum.append(sig_cum[:, L - 1 : L])
        enter.append(jnp.where(seg == 0.0, jnp.exp(cum), 0.0))
        seg_first = jnp.where(first, seg, 0.0).astype(BF16)
        seg_col = dot(seg_first, ones, TN)
        mask = causal & (seg_col == seg[0:1, :])
        mask_ref[at, :] = mask.astype(F32).astype(BF16)
        to_end = jnp.where(first & (seg == seg_end), 1.0, 0.0).astype(BF16)
        from_start = jnp.where(first & (seg == 0.0), 1.0, 0.0).astype(BF16)
        me_ref[at, :] = dot(to_end, ones[:, :128], TN).astype(BF16)
        mw_ref[at, :] = dot(from_start, ones[:, :128], TN).astype(BF16)
        thr.append(jnp.where(seg_end == 0.0, jnp.exp(cum_end), 0.0))
        kap.append(jnp.exp(half))
    passed = jnp.ones((H, 1), F32)
    before = []
    for c in range(C):
        before.append(passed)
        put(FROM_START, slice(c * L, (c + 1) * L), enter[c] * passed)
        passed = passed * thr[c]
    columns = [*thr, *kap, *before, passed, passed * sum(rate_sum), passed * nega * sum(sig_sum)]
    columns.append(jax.nn.sigmoid(bias) / jax.nn.softplus(bias))
    passed = jnp.ones((H, 1), F32)
    rate_after = jnp.zeros((H, 1), F32)
    sig_after = jnp.zeros((H, 1), F32)
    for c in reversed(range(C)):
        at = slice(c * L, (c + 1) * L)
        to_shard_end = leave[c] * passed
        put(TO_END, at, to_shard_end)
        put(END_ALOG, at, to_shard_end * (rest[c] + rate_after))
        put(END_BIAS, at, to_shard_end * (ratio[c] + nega * (sig_rest[c] + sig_after)))
        passed = passed * thr[c]
        rate_after += rate_sum[c]
        sig_after += sig_sum[c]
    table = jnp.zeros((H, 128), F32)
    for k, v in enumerate(columns):
        table = jnp.where(lane == k, v, table)
    wide = dot(jnp.concatenate(split3(table), 0), e3_ref[...], TN)
    thx_ref[...] = wide[0:TABLE]


def scale_body(c, r):
    scale = expand(r.pk, TO_END, r.e3)

    def rows(at):
        r.xhi[at, :], r.xlo[at, :] = split2(r.x[at, :].astype(F32) * scale[at, :])

    each_rows(rows)


def states_body(c, r):
    r.acc[...] += dot2(r.bc[:, :STATE], (r.xhi[...], r.xlo[...]), TN)


def clear(r):
    r.acc[...] = jnp.zeros((STATE, W), F32)


def states_end(r):
    r.pay[:, :W] = r.acc[...]
    total = r.thx[TOTAL : TOTAL + 1, :]
    block = jnp.concatenate([total[:, 128 * k : 128 * (k + 1)] for k in range(ROWS)], 0)
    for d in range(SEQ):
        r.pay[ROWS * d : ROWS * (d + 1), W:] = block


def moments_body(c, r):
    by_alog = expand(r.pk, END_ALOG, r.e3)
    by_bias = expand(r.pk, END_BIAS, r.e3)

    def rows(at):
        x = r.x[at, :].astype(F32)
        r.hi[at, :], r.lo[at, :] = split2(x * by_alog[at, :])
        r.hi2[at, :], r.lo2[at, :] = split2(x * by_bias[at, :])

    each_rows(rows)
    b = r.bc[:, :STATE]
    r.moments[:, :W] += dot2(b, (r.hi[...], r.lo[...]), TN)
    r.moments[:, W:] += dot2(b, (r.hi2[...], r.lo2[...]), TN)


def moments_begin(r):
    r.moments[...] = jnp.zeros((STATE, 2 * W), F32)


def log_base(through):
    return jnp.where(through > 1e-30, 0.5 * jnp.log(jnp.maximum(through, 1e-30)), 0.0)


def through_row(got_ref, j):
    block = got_ref[ROWS * j : ROWS * (j + 1), W:]
    return jnp.concatenate([block[k : k + 1, :] for k in range(ROWS)], 1)


def scan_forward_kernel(got_ref, out_ref, after_ref, through_ref):
    acc = jnp.zeros((ROWS, W), F32)
    for j in range(SEQ):
        at = slice(ROWS * j, ROWS * (j + 1))
        out_ref[at, :] = acc
        through = through_row(got_ref, j)
        through_ref[j : j + 1, :] = through
        acc = through * acc + got_ref[at, :W]
        after_ref[at, :] = acc


def scan_backward_kernel(got_ref, through_ref, after_ref, loc_ref, sums_ref, e3_ref, thx_ref, out_ref):
    acc = jnp.zeros((ROWS, W), F32)
    by_alog = jnp.zeros((ROWS, W), F32)
    by_bias = jnp.zeros((ROWS, W), F32)
    for j in reversed(range(SEQ)):
        at = slice(ROWS * j, ROWS * (j + 1))
        out_ref[at, :W] = acc
        block = got_ref[2 * ROWS * j : 2 * ROWS * (j + 1), :].astype(F32)
        through = through_ref[j : j + 1, :]
        state = after_ref[at, :]
        rests = block[:ROWS, W:] + 256.0
        back_rest = jnp.floor(rests * (1.0 / 16))
        rests = rests - 16.0 * back_rest
        alog_rest = jnp.floor(rests * 0.25)
        bias_rest = rests - 4.0 * alog_rest
        base = log_base(through)
        bias_base = thx_ref[BASE : BASE + 1, :] * (1.0 + base)
        by_alog += acc * (with_rest(block[ROWS:, :W], alog_rest, 4) + base * state)
        by_bias += acc * (with_rest(block[ROWS:, W:], bias_rest, 4) + bias_base * state)
        acc = through * acc + with_rest(block[:ROWS, :W], back_rest, 32)
    row = lax.broadcasted_iota(jnp.int32, (H, W), 0)
    vector = jnp.where(
        row == 0,
        jnp.sum(by_alog, axis=0, keepdims=True),
        jnp.where(row == 1, jnp.sum(by_bias, axis=0, keepdims=True), 0.0),
    )
    heads = e3_ref[0:H, :]
    far = sum(dot(heads, part, NT) for part in split3(vector))
    lane = lax.broadcasted_iota(jnp.int32, (ROWS, 128), 1)
    right = jnp.zeros((ROWS, 128), F32)
    for k in range(2):
        at = slice(ROWS * k, ROWS * (k + 1))
        right = jnp.where(lane == SKIPS + k, loc_ref[at, 0:1], right)
        right = jnp.where(lane == ALOGS + k, loc_ref[at, 1:2] + far[at, 0:1], right)
        right = jnp.where(lane == BIASES + k, loc_ref[at, 2:3] + far[at, 1:2], right)
    gains = sums_ref[0:1, :]
    left = jnp.concatenate([gains[:, 128 * k : 128 * (k + 1)] for k in range(8)], 0)
    for d in range(SEQ):
        out_ref[ROWS * d : ROWS * (d + 1), W : W + 128] = left
        out_ref[ROWS * d : ROWS * (d + 1), W + 128 :] = right


def within_body(c, r):
    ex = expand(r.pk, DTBETA, r.e3)
    al = expand(r.pk, ALPHA, r.e3)

    def scale(at):
        r.hi[at, :], r.lo[at, :] = split2(r.x[at, :].astype(F32) * ex[at, :])

    each_rows(scale)
    b = r.bc[:, :STATE]
    cc = r.bc[:, STATE:]
    g = split2(dot(cc, b, NT) * r.mask[...].astype(F32))
    xs = (r.hi[...], r.lo[...])
    kappa = r.thx[pl.ds(KAP + c, 1), :]
    r.sloc[...] = r.acc[...]
    res = dot3(g, xs, NN) + dot2(cc * r.mw[...], split2(kappa * r.acc[...]), NN)
    r.ys[...] = al * res
    r.acc[...] = r.thx[pl.ds(THR + c, 1), :] * r.acc[...] + kappa * dot2(b * r.me[...], xs, TN)


def norm_begin(r):
    r.shi[...], r.slo[...] = split2(r.sin[...])
    r.gain_acc[...] = jnp.zeros((8, W), F32)
    r.acc[...] = jnp.zeros((STATE, W), F32)


def norm_body(c, r):
    cc = r.bc[:, STATE:]
    win = expand(r.pk, FROM_START, r.e3)
    res = dot2(cc, (r.shi[...], r.slo[...]), NN)
    gain = r.vec[0:1, :]
    skip = r.vec[1:2, :]

    def body(at):
        weight = win[at, :]
        x = r.x[at, :].astype(F32)
        z = r.z[at, :].astype(F32)
        out = r.go[at, :].astype(F32)
        ys = r.ys[at, :] + weight * res[at, :]
        y = ys + skip * x
        logistic = jax.nn.sigmoid(z)
        silu = z * logistic
        gated = y * silu
        grad_normed = out * gain
        square = jnp.sum(gated * gated, axis=1, keepdims=True) * (1.0 / W)
        cross = jnp.sum(grad_normed * gated, axis=1, keepdims=True) * (1.0 / W)
        inv = lax.rsqrt(square + EPSILON)
        normed = gated * inv
        grad_gated = inv * (grad_normed - normed * (inv * cross))
        gy = grad_gated * silu
        gz = grad_gated * y * (logistic + silu * (1.0 - logistic))
        r.gz[at, :] = gz.astype(BF16)
        r.gy[at, :] = gy
        gpart = out * normed
        r.gain_acc[...] += gpart[0:8] + gpart[8:16]
        r.hi[at, :], r.lo[at, :] = split2(gy * weight)
        r.rhi[at, :], r.rlo[at, :] = split2(gy * ys)

    each_rows(body)
    r.r[...] = dot2(r.e3[0:H, :], (r.rhi[...], r.rlo[...]), NT)
    new = dot2(cc, (r.hi[...], r.lo[...]), TN)
    r.acc[...] += new


def rest_level(value, levels):
    high = value.astype(BF16).astype(F32)
    place = (value - high) / jnp.maximum(jnp.abs(high) * 2.0**-8, 1e-30) + 1.0
    return high, jnp.clip(jnp.floor(place * (levels / 2)), 0.0, levels - 1.0)


def with_rest(high, level, levels):
    return high + jnp.abs(high) * (2.0**-8 * ((level + 0.5) * (2.0 / levels) - 1.0))


def norm_end(r):
    total = r.thx[TOTAL : TOTAL + 1, :]
    base = log_base(total)
    by_alog = r.thx[BY_ALOG : BY_ALOG + 1, :] - base * total
    bias_base = r.thx[BASE : BASE + 1, :] * (1.0 + base)
    by_bias = r.thx[BY_BIAS : BY_BIAS + 1, :] - bias_base * total
    for d in range(SEQ):
        at = slice(ROWS * d, ROWS * (d + 1))
        back, back_rest = rest_level(r.acc[at, :], 32)
        own = r.pay[at, :W]
        sin = r.sin[at, :]
        alog, alog_rest = rest_level(r.moments[at, :W] - base * own + by_alog * sin, 4)
        bias, bias_rest = rest_level(r.moments[at, W:] - bias_base * own + by_bias * sin, 4)
        rests = 16.0 * back_rest + 4.0 * alog_rest + bias_rest - 256.0
        block = jnp.concatenate(
            [jnp.concatenate([back, rests], 1), jnp.concatenate([alog, bias], 1)], 0
        )
        r.back[2 * ROWS * d : 2 * ROWS * (d + 1), :] = block.astype(BF16)
    r.sums[0:1, :] = jnp.sum(r.gain_acc[...], axis=0, keepdims=True)
    r.sums[1:8, :] = jnp.zeros((7, W), F32)


def local_x_begin(r):
    r.acc[...] = jnp.zeros((STATE, W), F32)
    r.skip_acc[...] = jnp.zeros((8, W), F32)


def local_x_body(c, r):
    ex = expand(r.pk, DTBETA, r.e3)
    al = expand(r.pk, ALPHA, r.e3)

    def scale(at):
        r.xhi[at, :], r.xlo[at, :] = split2(r.x[at, :].astype(F32) * ex[at, :])
        r.ghi[at, :], r.glo[at, :] = split2(r.gy[at, :] * al[at, :])

    each_rows(scale)
    b = r.bc[:, :STATE]
    cc = r.bc[:, STATE:]
    gys = (r.ghi[...], r.glo[...])
    g = split2(dot(cc, b, NT) * r.mask[...].astype(F32))
    kappa = r.thx[pl.ds(KAP + c, 1), :]
    dstate = split2(kappa * r.acc[...])
    res = dot3(g, gys, TN) + dot2(b * r.me[...], dstate, NN)
    r.gbs[...] = r.me[...].astype(F32) * dot3_wide((r.xhi[...], r.xlo[...]), dstate)
    skip = r.vec[1:2, :]

    def finish(at):
        x = r.x[at, :].astype(F32)
        gy = r.gy[at, :]
        scaled = ex[at, :] * res[at, :]
        r.gx[at, :] = scaled + skip * gy
        r.rhi[at, :], r.rlo[at, :] = split2(scaled * x)
        spart = gy * x
        r.skip_acc[...] += spart[0:8] + spart[8:16]

    each_rows(finish)
    r.u[...] = dot2(r.e3[0:H, :], (r.rhi[...], r.rlo[...]), NT)
    state = split2(kappa * (r.sloc[...] + r.thx[pl.ds(PRE + c, 1), :] * r.sin[...]))
    r.gcs[...] = r.mw[...].astype(F32) * dot3_wide(gys, state)
    r.acc[...] = r.thx[pl.ds(THR + c, 1), :] * r.acc[...] + kappa * dot2(cc * r.mw[...], gys, TN)


def local_bc_body(c, r):
    ex = expand(r.pk, DTBETA, r.e3)
    al = expand(r.pk, ALPHA, r.e3)

    def scale(at):
        r.xhi[at, :], r.xlo[at, :] = split2(r.x[at, :].astype(F32) * ex[at, :])
        r.ghi[at, :], r.glo[at, :] = split2(r.gy[at, :] * al[at, :])

    each_rows(scale)
    b = r.bc[:, :STATE]
    cc = r.bc[:, STATE:]
    gys = (r.ghi[...], r.glo[...])
    xs = (r.xhi[...], r.xlo[...])
    q = split2(dot3(gys, xs, NT) * r.mask[...].astype(F32))
    r.gb[...] = r.gbs[...] + joined(q, [cc, cc], TN)
    r.gc[...] = (r.gcs[...] + joined(q, [b, b], NN)).astype(BF16)


def final_begin(r):
    r.dhi[...], r.dlo[...] = split2(r.din[:, :W])


def final_bc_body(c, r):
    gb = r.gb[...] + dot3_wide((r.xhi[...], r.xlo[...]), (r.dhi[...], r.dlo[...]))
    r.out[:, :STATE] = gb.astype(BF16)
    r.out[:, STATE:] = r.gc[...]


def final_bc_end(r):
    total = r.din[0:ROWS, W:]
    for d in range(1, SEQ):
        total += r.din[ROWS * d : ROWS * (d + 1), W:]
    r.params[...] = total


def final_x_body(c, r):
    fin = expand(r.pk, TO_END, r.e3)
    v = dot2(r.bc[:, :STATE], (r.dhi[...], r.dlo[...]), NN)

    def body(at):
        scaled = fin[at, :] * v[at, :]
        r.gxo[at, :] = (r.gx[at, :] + scaled).astype(BF16)
        r.rhi[at, :], r.rlo[at, :] = split2(scaled * r.x[at, :].astype(F32))

    each_rows(body)
    r.uu[...] = r.u[...] + dot2(r.e3[0:H, :], (r.rhi[...], r.rlo[...]), NT)


def time_sums(r, u_ref, carry, write):
    row = lax.broadcasted_iota(jnp.int32, (L, L), 0)
    col = lax.broadcasted_iota(jnp.int32, (L, L), 1)
    tri = (row >= col).astype(F32).astype(BF16)
    nega = -jnp.exp(r.par[:, 1:2])
    for c in reversed(range(C)):
        at = slice(c * L, (c + 1) * L)
        u = u_ref[:, at]
        dt = r.rf[0:H, at]
        parts = dot(jnp.concatenate(split3(r.r[:, at] - u), 0), tri, NN)
        later = parts[0:H] + parts[H : 2 * H] + parts[2 * H : 3 * H]
        grad_rate = later + carry
        carry = carry + later[:, 0:1]
        write(at, (u / dt + grad_rate * nega) * r.rf[H : 2 * H, at], grad_rate * dt * nega)


def local_x_end(r):
    sums = [jnp.zeros((H, 1), F32)] * 2

    def write(at, grad_dt, grad_alog):
        sums[0] += jnp.sum(grad_alog, axis=1, keepdims=True)
        sums[1] += jnp.sum(grad_dt, axis=1, keepdims=True)

    time_sums(r, r.u, jnp.zeros((H, 1), F32), write)
    skips = jnp.broadcast_to(jnp.sum(r.skip_acc[...], axis=0, keepdims=True), (H, W))
    skip_part = sum(dot(r.e3[0:H, :], part, NT) for part in split3(skips))[:, 0:1]
    lane = lax.broadcasted_iota(jnp.int32, (H, 128), 1)
    r.loc[...] = jnp.where(
        lane == 0, skip_part, jnp.where(lane == 1, sums[0], jnp.where(lane == 2, sums[1], 0.0))
    )


def final_x_end(r):
    for k in range(8):
        r.gain[:, 128 * k : 128 * (k + 1)] = r.params[k : k + 1, :128]
    row = lax.broadcasted_iota(jnp.int32, (ROWS, ROWS), 0)
    col = lax.broadcasted_iota(jnp.int32, (ROWS, ROWS), 1)
    same = (row == col).astype(F32).astype(BF16)
    turned = sum(dot(part, same, TN) for part in split3(r.params[:, 128:]))
    for ref, at in ((r.gskip, SKIPS), (r.galog, ALOGS), (r.gbias, BIASES)):
        ref[...] = jnp.concatenate([turned[at : at + 1, :], turned[at + 1 : at + 2, :]], 1)
    state = r.pay[:, :W] + r.thx[TOTAL : TOTAL + 1, :] * r.sin[...]
    ends = jnp.broadcast_to(jnp.sum(state * r.din[:, :W], axis=0, keepdims=True), (H, W))
    carry = sum(dot(r.e3[0:H, :], part, NT) for part in split3(ends))[:, 0:1]

    def write(at, grad_dt, grad_alog):
        r.gdt[:, at] = grad_dt

    time_sums(r, r.uu, carry, write)


def pack_kernel(b_ref, c_ref, out_ref):
    for g in range(GRP):
        at = slice(STATE * g, STATE * (g + 1))
        out_ref[g, :, :STATE] = b_ref[:, at]
        out_ref[g, :, STATE:] = c_ref[:, at]


def unpack_kernel(in_ref, b_ref, c_ref, sems):
    copies = []
    for g in range(GRP):
        at = slice(STATE * g, STATE * (g + 1))
        for k, ref in enumerate((b_ref, c_ref)):
            source = in_ref.at[g, :, STATE * k : STATE * (k + 1)]
            copies.append(pltpu.make_async_copy(source, ref.at[:, at], sems.at[k, g]))
    for copy in copies:
        copy.start()
    for copy in copies:
        copy.wait()


def head_matrix():
    one = np.arange(W)[None, :] // HEAD_DIM == np.arange(H)[:, None]
    return jnp.asarray(np.concatenate([one, one, one], 0), BF16)


def shard_body(
    x_in, z_gate, b_proj, c_proj, dt_raw, dt_bias, a_log, skip, norm_weight, doc_starts, grad_out
):
    e3 = head_matrix()
    par = jnp.pad(jnp.stack([dt_bias, a_log], 1), ((0, 0), (0, 126)))
    vec = jnp.pad(
        jnp.stack([norm_weight, jnp.repeat(skip, HEAD_DIM)], 0), ((0, 6), (0, 0))
    )
    starts = doc_starts.reshape(1, T)
    far = pl.BlockSpec(memory_space=pl.ANY)
    mine = pl.pallas_call(
        pack_kernel,
        out_shape=pltpu.HBM((GRP, 128, 2 * STATE), BF16),
        compiler_params=pltpu.CompilerParams(vmem_limit_bytes=VMEM_LIMIT),
        name="pack",
    )(*[pltpu.with_memory_space_constraint(a, pltpu.HBM) for a in (b_proj, c_proj)])
    bc = lax.all_to_all(mine, "head", split_axis=0, concat_axis=0, tiled=True).reshape(T, 2 * STATE)

    sds = pltpu.HBM
    pk, rf, mask, me, mw, thx = pl.pallas_call(
        prep_kernel,
        out_shape=(
            sds((12 * H, T), BF16),
            sds((2 * H, T), F32),
            sds((T, L), BF16),
            sds((T, 128), BF16),
            sds((T, 128), BF16),
            sds((TABLE, W), F32),
        ),
        compiler_params=pltpu.CompilerParams(vmem_limit_bytes=VMEM_LIMIT),
        name="prep",
    )(*[pltpu.with_memory_space_constraint(a, pltpu.HBM) for a in (dt_raw, par, starts, e3)])

    state = ((STATE, W), F32)
    half = ((L, W), BF16)
    unit = 2 * T * L * W
    common = {"e3": (e3, "all"), "pk": (pk, "row"), "thx": (thx, "all")}
    x = {"x": (x_in, "tok")}
    masks = {"mask": (mask, "tok"), "me": (me, "tok"), "mw": (mw, "tok")}

    xhi, xlo = staged(
        scale_body,
        {"e3": (e3, "all"), "pk": (pk, "row")} | x,
        {"xhi": ((T, W), BF16, "tok"), "xlo": ((T, W), BF16, "tok")},
        {},
        "scale",
        unit,
    )
    xhi, xlo, bc = lax.optimization_barrier((xhi, xlo, bc))
    pay, bc = staged(
        states_body,
        {"thx": (thx, "all"), "bc": (bc, "near_tok"), "xhi": (xhi, "tok"), "xlo": (xlo, "tok")},
        {"pay": ((STATE, W + 128), F32, "all"), "bc_copy": ((T, 2 * STATE), BF16, "copy")},
        {"acc": state},
        "states",
        2 * unit,
        begin=clear,
        end=states_end,
    )

    def scan(kernel, name, outs, got, *others):
        return pl.pallas_call(
            kernel,
            out_shape=outs,
            in_specs=[pl.BlockSpec(memory_space=pltpu.VMEM)] * (1 + len(others)),
            compiler_params=pltpu.CompilerParams(vmem_limit_bytes=16 * 2**20),
            name=name,
        )(
            pltpu.with_memory_space_constraint(got, pltpu.VMEM),
            *[pltpu.with_memory_space_constraint(a, pltpu.HBM) for a in others],
        )

    def exchange(v):
        return lax.all_to_all(v, "seq", split_axis=0, concat_axis=0, tiled=True)

    bcs = {"bc": (bc, "tok")}
    got = exchange(pay)
    ys, sloc = staged(
        within_body,
        common | bcs | masks | x,
        {
            "ys": ((T, W), F32, "tok"),
            "sloc": ((C, STATE, W), F32, "state"),
        },
        {"acc": state, "hi": half, "lo": half},
        "within",
        7 * unit,
        begin=clear,
    )
    ys, sloc, got = lax.optimization_barrier((ys, sloc, got))
    before, after, through = scan(
        scan_forward_kernel,
        "scan_forward",
        (sds((STATE, W), F32), sds((STATE, W), F32), sds((SEQ, W), F32)),
        got,
    )
    sin = exchange(before)
    tied, _ = lax.optimization_barrier((x_in, got))
    (moments,) = staged(
        moments_body,
        {"e3": (e3, "all"), "pk": (pk, "row")} | bcs | {"x": (tied, "tok")},
        {"moments": ((STATE, 2 * W), F32, "all")},
        {"hi": half, "lo": half, "hi2": half, "lo2": half},
        "moments",
        4 * unit,
        begin=moments_begin,
    )
    moments, sin = lax.optimization_barrier((moments, sin))

    gy, gz, r, back, sums, sin = staged(
        norm_body,
        common
        | {"vec": (vec, "all"), "sin": (sin, "near")}
        | bcs
        | {"ys": (ys, "tok"), "z": (z_gate, "tok"), "go": (grad_out, "tok")}
        | x
        | {"moments": (moments, "late"), "pay": (pay, "late")},
        {
            "gy": ((T, W), F32, "tok"),
            "gz": ((T, W), BF16, "tok"),
            "r": ((H, T), F32, "row"),
            "back": ((2 * STATE, 2 * W), BF16, "all"),
            "sums": ((8, W), F32, "all"),
            "sin_copy": ((STATE, W), F32, "copy"),
        },
        {
            "gain_acc": ((8, W), F32),
            "acc": state,
            "shi": ((STATE, W), BF16),
            "slo": ((STATE, W), BF16),
            "hi": half,
            "lo": half,
            "rhi": half,
            "rlo": half,
        },
        "norm",
        6 * unit,
        begin=norm_begin,
        end=norm_end,
    )

    got_back = exchange(back)
    gx, u, gbs, gcs, loc = staged(
        local_x_body,
        common
        | {
            "vec": (vec, "all"),
            "sin": (sin, "all"),
            "par": (par, "all"),
            "rf": (rf, "row"),
            "r": (r, "row"),
        }
        | bcs
        | masks
        | {"gy": (gy, "tok"), "sloc": (sloc, "state")}
        | x,
        {
            "gx": ((T, W), F32, "tok"),
            "u": ((H, T), F32, "row"),
            "gbs": ((T, STATE), F32, "tok"),
            "gcs": ((T, STATE), F32, "tok"),
            "loc": ((H, 128), F32, "all"),
        },
        {
            "acc": state,
            "skip_acc": ((8, W), F32),
            "ghi": half,
            "glo": half,
            "xhi": half,
            "xlo": half,
            "rhi": half,
            "rlo": half,
        },
        "local_x",
        7 * unit,
        backward=True,
        begin=local_x_begin,
        end=local_x_end,
    )
    gbs, got_back = lax.optimization_barrier((gbs, got_back))
    behind = scan(
        scan_backward_kernel, "scan_backward", sds((STATE, W + 256), F32), got_back, through, after, loc, sums, e3, thx
    )
    din = exchange(behind)
    gb, gc = staged(
        local_bc_body,
        {"e3": (e3, "all"), "pk": (pk, "row")}
        | bcs
        | {"mask": (mask, "tok"), "gy": (gy, "tok"), "gbs": (gbs, "tok"), "gcs": (gcs, "tok")}
        | x,
        {"gb": ((T, STATE), F32, "tok"), "gc": ((T, STATE), BF16, "tok")},
        {"ghi": half, "glo": half, "xhi": half, "xlo": half},
        "local_bc",
        5 * unit,
    )

    gb, din = lax.optimization_barrier((gb, din))
    gbc, din, params = staged(
        final_bc_body,
        {
            "din": (din, "near"),
            "gb": (gb, "tok"),
            "gc": (gc, "tok"),
            "xhi": (xhi, "tok"),
            "xlo": (xlo, "tok"),
        },
        {
            "out": ((T, 2 * STATE), BF16, "tok"),
            "din_copy": ((STATE, W + 256), F32, "copy"),
            "params": ((ROWS, 256), F32, "all"),
        },
        {"dhi": ((STATE, W), BF16), "dlo": ((STATE, W), BF16)},
        "final_bc",
        2 * unit,
        begin=final_begin,
        end=final_bc_end,
    )
    gbc, gx = lax.optimization_barrier((gbc, gx))
    back_bc = lax.all_to_all(
        gbc.reshape(GRP, 128, 2 * STATE), "head", split_axis=0, concat_axis=0, tiled=True
    )
    grad_x, grad_dt, grad_gain, grad_skip, grad_alog, grad_bias = staged(
        final_x_body,
        common
        | {
            "din": (din, "all"),
            "sin": (sin, "all"),
            "pay": (pay, "all"),
            "par": (par, "all"),
            "rf": (rf, "row"),
            "r": (r, "row"),
            "u": (u, "row"),
            "params": (params, "all"),
        }
        | bcs
        | {"gx": (gx, "tok")}
        | x,
        {
            "gxo": ((T, W), BF16, "tok"),
            "gdt": ((H, T), F32, "row"),
            "gain": ((1, W), F32, "all"),
            "gskip": ((1, H), F32, "all"),
            "galog": ((1, H), F32, "all"),
            "gbias": ((1, H), F32, "all"),
        },
        {
            "uu": ((H, T), F32),
            "dhi": ((STATE, W), BF16),
            "dlo": ((STATE, W), BF16),
            "rhi": half,
            "rlo": half,
        },
        "final_x",
        3 * unit,
        begin=final_begin,
        end=final_x_end,
    )
    grad_b, grad_c = pl.pallas_call(
        unpack_kernel,
        out_shape=(pltpu.HBM((128, GRP * STATE), BF16), pltpu.HBM((128, GRP * STATE), BF16)),
        in_specs=[pl.BlockSpec(memory_space=pltpu.VMEM)],
        out_specs=(far, far),
        scratch_shapes=[pltpu.SemaphoreType.DMA((2, GRP))],
        compiler_params=pltpu.CompilerParams(vmem_limit_bytes=16 * 2**20),
        name="unpack",
    )(pltpu.with_memory_space_constraint(back_bc, pltpu.VMEM))
    grad_gain = grad_gain.reshape(W)
    grad_skip, grad_alog, grad_bias = grad_skip.reshape(H), grad_alog.reshape(H), grad_bias.reshape(H)
    return (grad_x, gz, grad_b, grad_c, grad_dt, grad_alog, grad_bias, grad_skip, grad_gain)


def solution(mesh):
    in_specs = (
        P("seq", "head"),
        P("seq", "head"),
        P(("seq", "head"), None),
        P(("seq", "head"), None),
        P("head", "seq"),
        P("head"),
        P("head"),
        P("head"),
        P("head"),
        P("seq"),
        P("seq", "head"),
    )
    out_specs = (
        P("seq", "head"),
        P("seq", "head"),
        P(("seq", "head"), None),
        P(("seq", "head"), None),
        P("head", "seq"),
        P("head"),
        P("head"),
        P("head"),
        P("head"),
    )
    return jax.shard_map(shard_body, mesh=mesh, in_specs=in_specs, out_specs=out_specs, check_vma=False)
```

```python
import jax
import jax.numpy as jnp
import numpy as np
from jax import lax
from jax.experimental import pallas as pl
from jax.experimental.pallas import tpu as pltpu
from jax.sharding import PartitionSpec as P

HEADS = 128
HEAD_DIM = 64
STATE = 128
PROJECTION_SETS = 8
EPSILON = 1e-05

T = 1024
H = 16
W = H * HEAD_DIM
L = 256
C = T // L
SEQ = 16
GRP = 8
ROWS = STATE // SEQ
F32 = jnp.float32
BF16 = jnp.bfloat16
FLUSHES = 4
STEP = 16
VMEM_LIMIT = 60 * 2**20
VMEM_NEAR = 48 * 2**20

THR, KAP, PRE, TOTAL, BY_ALOG, BY_BIAS, BASE, TABLE = 0, 4, 8, 12, 13, 14, 15, 16
ALPHA, DTBETA, TO_END, FROM_START, END_ALOG, END_BIAS = 0, 1, 2, 3, 4, 5
SKIPS, ALOGS, BIASES = 0, 2, 4

NN = (((1,), (0,)), ((), ()))
NT = (((1,), (1,)), ((), ()))
TN = (((0,), (0,)), ((), ()))


def dot(a, b, dims):
    return lax.dot_general(a, b, dims, preferred_element_type=F32)


def split2(a):
    hi = a.astype(BF16)
    return hi, (a - hi.astype(F32)).astype(BF16)


def split3(a):
    hi, mid = split2(a)
    lo = (a - hi.astype(F32) - mid.astype(F32)).astype(BF16)
    return hi, mid, lo


def joined(a, b, dims):
    ((ka,), (kb,)), _ = dims
    return dot(jnp.concatenate(a, ka), jnp.concatenate(b, kb), dims)


def dot2(a, b, dims):
    return joined([a, a], b, dims)


def dot3(a, b, dims):
    return joined([a[0], a[0], a[1]], [b[0], b[1], b[0]], dims)


def dot3_wide(a, b):
    both = dot(a[0], jnp.concatenate(b, 0), NT)
    return both[:, :STATE] + both[:, STATE:] + dot(a[1], b[0], NT)


def each_rows(body):
    for i in range(L // STEP):
        body(slice(STEP * i, STEP * (i + 1)))


class Views:
    def __init__(self, buffers, kinds, c):
        for name, ref in buffers.items():
            kind = kinds[name]
            if kind in ("tok", "near_tok"):
                ref = ref.at[pl.ds(pl.multiple_of(c * L, L), L), :]
            elif kind == "row":
                ref = ref.at[:, pl.ds(pl.multiple_of(c * L, L), L)]
            elif kind == "state":
                ref = ref.at[c]
            setattr(self, name, ref)


def staged(body, ins, outs, scratch, name, flops, backward=False, begin=None, end=None):
    kinds = {k: kind for k, (_, kind) in ins.items()}
    kinds.update({k: kind for k, (_, _, kind) in outs.items()})
    kinds.update({k: "row" if shape == (H, T) else "all" for k, (shape, _) in scratch.items()})
    n, m = len(ins), len(outs)
    moving = ("tok", "state")
    here = [k for k in ins if kinds[k] in ("near", "near_tok")]
    copied = [k for k in outs if kinds[k] == "copy"]
    steps = C
    slot, count = {}, 0
    for k in [*ins, *outs]:
        slot[k] = count
        count += {"tok": steps, "state": steps, "blocks": FLUSHES, "near": 0, "near_tok": 0}.get(kinds[k], 1)
    buffered_in = [k for k in ins if k not in here]
    buffered_out = [k for k in outs if k not in copied]

    def part(ref, kind, c):
        if kind == "tok":
            return ref.at[pl.ds(pl.multiple_of(c * L, L), L), :]
        return ref.at[c]

    def kernel(*refs):
        far_in = dict(zip(ins, refs[:n]))
        far_out = dict(zip(outs, refs[n : n + m]))
        near = dict(zip([*buffered_in, *buffered_out, *scratch], refs[n + m : -1]))
        near.update({k: far_in[k] for k in here})
        sems = refs[-1]

        def copy_in(k, c):
            return pltpu.make_async_copy(part(far_in[k], kinds[k], c), part(near[k], kinds[k], c), sems.at[slot[k] + c])

        def copy_out(k, c):
            return pltpu.make_async_copy(part(near[k], kinds[k], c), part(far_out[k], kinds[k], c), sems.at[slot[k] + c])

        once = [
            pltpu.make_async_copy(far_in[k], near[k], sems.at[slot[k]])
            for k in buffered_in
            if kinds[k] in ("row", "all")
        ]
        late = [pltpu.make_async_copy(far_in[k], near[k], sems.at[slot[k]]) for k in ins if kinds[k] == "late"]
        passed = [
            pltpu.make_async_copy(near[k.removesuffix("_copy")], far_out[k], sems.at[slot[k]]) for k in copied
        ]
        for copy in once:
            copy.start()
        for c in reversed(range(C)) if backward else range(C):
            for k in ins:
                if kinds[k] in moving:
                    copy_in(k, c).start()
        for copy in late + passed:
            copy.start()
        for copy in once:
            copy.wait()
        whole = Views(near, {k: "all" for k in near}, 0)
        flushed = []

        def flush(k, i, at):
            copy = pltpu.make_async_copy(near[k].at[at, :], far_out[k].at[at, :], sems.at[slot[k] + i])
            copy.start()
            flushed.append(copy)

        whole.flush = flush
        if begin is not None:
            begin(whole)

        def step(i, carry):
            c = C - 1 - i if backward else i
            for k in ins:
                if kinds[k] in moving:
                    copy_in(k, c).wait()
            body(c, Views(near, kinds, c))
            for k in outs:
                if kinds[k] in moving:
                    copy_out(k, c).start()
            return carry

        lax.fori_loop(0, C, step, 0)
        for copy in late:
            copy.wait()
        if end is not None:
            end(whole)
        once = [
            pltpu.make_async_copy(near[k], far_out[k], sems.at[slot[k]])
            for k in buffered_out
            if kinds[k] in ("row", "all")
        ]
        for copy in once:
            copy.start()
        for c in range(C):
            for k in outs:
                if kinds[k] in moving:
                    copy_out(k, c).wait()
        for copy in once + passed + flushed:
            copy.wait()

    far = pl.BlockSpec(memory_space=pl.ANY)
    return pl.pallas_call(
        kernel,
        out_shape=tuple(pltpu.HBM(s, d) for s, d, _ in outs.values()),
        in_specs=[pl.BlockSpec(memory_space=pltpu.VMEM) if k in here else far for k in ins],
        out_specs=tuple([far] * m),
        scratch_shapes=[
            *[pltpu.VMEM(ins[k][0].shape, ins[k][0].dtype) for k in buffered_in],
            *[pltpu.VMEM(*outs[k][:2]) for k in buffered_out],
            *[pltpu.VMEM(s, d) for s, d in scratch.values()],
            pltpu.SemaphoreType.DMA((count,)),
        ],
        compiler_params=pltpu.CompilerParams(vmem_limit_bytes=VMEM_NEAR if here else VMEM_LIMIT),
        cost_estimate=pl.CostEstimate(flops=flops, bytes_accessed=8 * 2**20, transcendentals=0),
        name=name,
    )(*[pltpu.with_memory_space_constraint(ins[k][0], pltpu.VMEM if k in here else pltpu.HBM) for k in ins])


def expand(pk, which, e3):
    return dot(pk[2 * H * which : 2 * H * (which + 1), :], e3[0 : 2 * H, :], TN)


def fold(v):
    lane = lax.broadcasted_iota(jnp.int32, (STEP, 128), 1)
    tiles = []
    for k in range(0, W, 256):
        a, b = v[:, k : k + 128], v[:, k + 128 : k + 256]
        a = a + pltpu.roll(a, 96, 1)
        b = b + pltpu.roll(b, 32, 1)
        tiles.append(jnp.where((lane & 32) == 0, a, b))
    return jnp.concatenate(tiles, 1)


def folded_heads():
    lane = np.arange(W // 2)
    head = 4 * (lane // 128) + (lane % 128 >= 64) + 2 * ((lane & 32) != 0)
    return jnp.asarray(head[None, :] == np.arange(H)[:, None], BF16)


def prep_kernel(dt_ref, par_ref, st_ref, e3_ref, pk_ref, rf_ref, marks_ref, thx_ref):
    bias = par_ref[:, 0:1]
    nega = -jnp.exp(par_ref[:, 1:2])
    row = lax.broadcasted_iota(jnp.int32, (L, L), 0)
    col = lax.broadcasted_iota(jnp.int32, (L, L), 1)
    tri = (row <= col).astype(F32).astype(BF16)
    causal = row >= col
    first = lax.broadcasted_iota(jnp.int32, (H, L), 0) == 0
    lane = lax.broadcasted_iota(jnp.int32, (H, 128), 1)
    ones = jnp.ones((H, L), BF16)
    thr, kap, leave, enter, rest, ratio, sig_rest, rate_sum, sig_sum = [], [], [], [], [], [], [], [], []

    def put(which, at, value):
        base = 2 * H * which
        pk_ref[base : base + H, at], pk_ref[base + H : base + 2 * H, at] = split2(value)

    for c in range(C):
        at = slice(c * L, (c + 1) * L)
        pre = dt_ref[:, at] + bias
        dt = jax.nn.softplus(pre)
        rf_ref[0:H, at] = dt
        sig = jax.nn.sigmoid(pre)
        rf_ref[H : 2 * H, at] = sig
        rate = dt * nega
        parts = dot(jnp.concatenate(split3(rate) + split3(sig), 0), tri, NN)
        cum = parts[0:H] + parts[H : 2 * H] + parts[2 * H : 3 * H]
        sig_cum = parts[3 * H : 4 * H] + parts[4 * H : 5 * H] + parts[5 * H : 6 * H]
        starts = jnp.broadcast_to(st_ref[:, at].astype(F32), (H, L))
        seg = dot(starts.astype(BF16), tri, NN)
        cum_end = cum[:, L - 1 : L]
        seg_end = seg[:, L - 1 : L]
        half = 0.5 * cum_end
        put(ALPHA, at, jnp.exp(cum - half))
        put(DTBETA, at, dt * jnp.exp(half - cum))
        leave.append(jnp.where(seg == seg_end, dt * jnp.exp(cum_end - cum), 0.0))
        rest.append(cum_end - cum)
        ratio.append(sig / dt)
        sig_rest.append(sig_cum[:, L - 1 : L] - sig_cum)
        rate_sum.append(cum_end)
        sig_sum.append(sig_cum[:, L - 1 : L])
        enter.append(jnp.where(seg == 0.0, jnp.exp(cum), 0.0))
        seg_first = jnp.where(first, seg, 0.0).astype(BF16)
        seg_col = dot(seg_first, ones, TN)
        mask = causal & (seg_col == seg[0:1, :])
        marks_ref[at, :L] = mask.astype(F32).astype(BF16)
        to_end = jnp.where(first & (seg == seg_end), 1.0, 0.0).astype(BF16)
        from_start = jnp.where(first & (seg == 0.0), 1.0, 0.0).astype(BF16)
        marks_ref[at, L : L + 128] = dot(to_end, ones[:, :128], TN).astype(BF16)
        marks_ref[at, L + 128 :] = dot(from_start, ones[:, :128], TN).astype(BF16)
        thr.append(jnp.where(seg_end == 0.0, jnp.exp(cum_end), 0.0))
        kap.append(jnp.exp(half))
    passed = jnp.ones((H, 1), F32)
    before = []
    for c in range(C):
        before.append(passed)
        put(FROM_START, slice(c * L, (c + 1) * L), enter[c] * passed)
        passed = passed * thr[c]
    columns = [*thr, *kap, *before, passed, passed * sum(rate_sum), passed * nega * sum(sig_sum)]
    columns.append(jax.nn.sigmoid(bias) / jax.nn.softplus(bias))
    passed = jnp.ones((H, 1), F32)
    rate_after = jnp.zeros((H, 1), F32)
    sig_after = jnp.zeros((H, 1), F32)
    for c in reversed(range(C)):
        at = slice(c * L, (c + 1) * L)
        to_shard_end = leave[c] * passed
        put(TO_END, at, to_shard_end)
        put(END_ALOG, at, to_shard_end * (rest[c] + rate_after))
        put(END_BIAS, at, to_shard_end * (ratio[c] + nega * (sig_rest[c] + sig_after)))
        passed = passed * thr[c]
        rate_after += rate_sum[c]
        sig_after += sig_sum[c]
    table = jnp.zeros((H, 128), F32)
    for k, v in enumerate(columns):
        table = jnp.where(lane == k, v, table)
    wide = dot(jnp.concatenate(split3(table), 0), e3_ref[...], TN)
    thx_ref[...] = wide[0:TABLE]


def scale_body(c, r):
    scale = expand(r.pk, TO_END, r.e3)

    def rows(at):
        r.xhi[at, :], r.xlo[at, :] = split2(r.x[at, :].astype(F32) * scale[at, :])

    each_rows(rows)


def states_body(c, r):
    r.acc[...] += dot2(r.bc[:, :STATE], (r.xhi[...], r.xlo[...]), TN)


def clear(r):
    r.acc[...] = jnp.zeros((STATE, W), F32)


def states_end(r):
    r.pay[:, :W] = r.acc[...]
    total = r.thx[TOTAL : TOTAL + 1, :]
    block = jnp.concatenate([total[:, 128 * k : 128 * (k + 1)] for k in range(ROWS)], 0)
    for d in range(SEQ):
        r.pay[ROWS * d : ROWS * (d + 1), W:] = block


def log_base(through):
    return jnp.where(through > 1e-30, 0.5 * jnp.log(jnp.maximum(through, 1e-30)), 0.0)


def moments_body(c, r):
    by_alog = expand(r.pk, END_ALOG, r.e3)
    by_bias = expand(r.pk, END_BIAS, r.e3)

    def rows(at):
        x = r.x[at, :].astype(F32)
        r.hi[at, :], r.lo[at, :] = split2(x * by_alog[at, :])
        r.hi2[at, :], r.lo2[at, :] = split2(x * by_bias[at, :])

    each_rows(rows)
    b = r.bc[:, :STATE]
    r.moments[:, :W] += dot2(b, (r.hi[...], r.lo[...]), TN)
    r.moments[:, W:] += dot2(b, (r.hi2[...], r.lo2[...]), TN)


def moments_begin(r):
    r.moments[...] = jnp.zeros((STATE, 2 * W), F32)


def moments_end(r):
    base = log_base(r.thx[TOTAL : TOTAL + 1, :])
    own = r.pay[:, :W]
    r.moments[:, :W] -= base * own
    r.moments[:, W:] -= (r.thx[BASE : BASE + 1, :] * (1.0 + base)) * own


def through_row(got_ref, j):
    block = got_ref[ROWS * j : ROWS * (j + 1), W:]
    return jnp.concatenate([block[k : k + 1, :] for k in range(ROWS)], 1)


def scan_forward_kernel(got_ref, out_ref, after_ref, through_ref):
    acc = jnp.zeros((ROWS, W), F32)
    for j in range(SEQ):
        at = slice(ROWS * j, ROWS * (j + 1))
        out_ref[at, :] = acc
        through = through_row(got_ref, j)
        through_ref[j : j + 1, :] = through
        acc = through * acc + got_ref[at, :W]
        after_ref[at, :] = acc


def scan_backward_kernel(got_ref, through_ref, after_ref, loc_ref, sums_ref, e3_ref, thx_ref, far_ref, out_ref, sems):
    acc = jnp.zeros((ROWS, W), F32)
    by_alog = jnp.zeros((ROWS, W), F32)
    by_bias = jnp.zeros((ROWS, W), F32)
    through_all = through_ref[...]
    base_all = log_base(through_all)
    bias_base_all = thx_ref[BASE : BASE + 1, :] * (1.0 + base_all)
    copies = []

    def send(j, lanes, k):
        at = slice(ROWS * j, ROWS * (j + 1))
        copy = pltpu.make_async_copy(out_ref.at[at, lanes], far_ref.at[at, lanes], sems.at[k, j])
        copy.start()
        copies.append(copy)

    for j in reversed(range(SEQ)):
        at = slice(ROWS * j, ROWS * (j + 1))
        out_ref[at, :W] = acc
        send(j, slice(0, W), 0)
        block = got_ref[2 * ROWS * j : 2 * ROWS * (j + 1), :].astype(F32)
        through = through_all[j : j + 1, :]
        state = after_ref[at, :]
        rests = block[:ROWS, W:] + 256.0
        back_rest = jnp.floor(rests * (1.0 / 16))
        rests = rests - 16.0 * back_rest
        alog_rest = jnp.floor(rests * 0.25)
        bias_rest = rests - 4.0 * alog_rest
        base = base_all[j : j + 1, :]
        bias_base = bias_base_all[j : j + 1, :]
        by_alog += acc * (with_rest(block[ROWS:, :W], alog_rest, 4) + base * state)
        by_bias += acc * (with_rest(block[ROWS:, W:], bias_rest, 4) + bias_base * state)
        acc = through * acc + with_rest(block[:ROWS, :W], back_rest, 32)
    row = lax.broadcasted_iota(jnp.int32, (H, W), 0)
    vector = jnp.where(
        row == 0,
        jnp.sum(by_alog, axis=0, keepdims=True),
        jnp.where(row == 1, jnp.sum(by_bias, axis=0, keepdims=True), 0.0),
    )
    heads = e3_ref[0:H, :]
    far = sum(dot(heads, part, NT) for part in split3(vector))
    lane = lax.broadcasted_iota(jnp.int32, (ROWS, 128), 1)
    right = jnp.zeros((ROWS, 128), F32)
    for k in range(2):
        at = slice(ROWS * k, ROWS * (k + 1))
        right = jnp.where(lane == SKIPS + k, loc_ref[at, 0:1], right)
        right = jnp.where(lane == ALOGS + k, loc_ref[at, 1:2] + far[at, 0:1], right)
        right = jnp.where(lane == BIASES + k, loc_ref[at, 2:3] + far[at, 1:2], right)
    gains = sums_ref[0:1, :]
    left = jnp.concatenate([gains[:, 128 * k : 128 * (k + 1)] for k in range(8)], 0)
    for d in range(SEQ):
        out_ref[ROWS * d : ROWS * (d + 1), W : W + 128] = left
        out_ref[ROWS * d : ROWS * (d + 1), W + 128 :] = right
        send(d, slice(W, W + 256), 1)
    for copy in copies:
        copy.wait()


def within_body(c, r):
    ex = expand(r.pk, DTBETA, r.e3)
    al = expand(r.pk, ALPHA, r.e3)

    def scale(at):
        r.hi[at, :], r.lo[at, :] = split2(r.x[at, :].astype(F32) * ex[at, :])

    each_rows(scale)
    b = r.bc[:, :STATE]
    cc = r.bc[:, STATE:]
    g = split2(dot(cc, b, NT) * r.marks[:, :L].astype(F32))
    r.g[:, :L], r.g[:, L:] = g
    xs = (r.hi[...], r.lo[...])
    kappa = r.thx[pl.ds(KAP + c, 1), :]
    r.sloc[...] = r.acc[...]
    res = dot3(g, xs, NN) + dot2(cc * r.marks[:, L + 128 :], split2(kappa * r.acc[...]), NN)
    r.y[...] = al * res + r.vec[1:2, :] * r.x[...].astype(F32)
    r.acc[...] = r.thx[pl.ds(THR + c, 1), :] * r.acc[...] + kappa * dot2(b * r.marks[:, L : L + 128], xs, TN)


def norm_begin(r):
    r.shi[...], r.slo[...] = split2(r.sin[...])
    r.gain_acc[...] = jnp.zeros((8, W), F32)
    r.acc[...] = jnp.zeros((STATE, W), F32)


def norm_body(c, r):
    cc = r.bc[:, STATE:]
    win = expand(r.pk, FROM_START, r.e3)
    res = dot2(cc, (r.shi[...], r.slo[...]), NN)
    gain = r.vec[0:1, :]

    def body(at):
        weight = win[at, :]
        z = r.z[at, :].astype(F32)
        out = r.go[at, :].astype(F32)
        y = r.y[at, :] + weight * res[at, :]
        logistic = jax.nn.sigmoid(z)
        silu = z * logistic
        gated = y * silu
        grad_normed = out * gain
        square = jnp.sum(gated * gated, axis=1, keepdims=True) * (1.0 / W)
        cross = jnp.sum(grad_normed * gated, axis=1, keepdims=True) * (1.0 / W)
        inv = lax.rsqrt(square + EPSILON)
        normed = gated * inv
        grad_gated = inv * (grad_normed - normed * (inv * cross))
        gy = grad_gated * silu
        gz = grad_gated * y * (logistic + silu * (1.0 - logistic))
        r.gz[at, :] = gz.astype(BF16)
        r.gy[at, :] = gy
        gpart = out * normed
        r.gain_acc[...] += gpart[0:8] + gpart[8:16]
        r.hi[at, :], r.lo[at, :] = split2(gy * weight)
        r.rhi[at, :], r.rlo[at, :] = split2(gy * y)

    each_rows(body)
    r.r[...] = dot2(r.e3[0:H, :], (r.rhi[...], r.rlo[...]), NT)
    new = dot2(cc, (r.hi[...], r.lo[...]), TN)
    r.acc[...] += new


def rest_level(value, levels):
    high = value.astype(BF16).astype(F32)
    place = (value - high) * pl.reciprocal(jnp.maximum(jnp.abs(high) * 2.0**-8, 1e-30), approx=True) + 1.0
    return high, jnp.clip(jnp.floor(place * (levels / 2)), 0.0, levels - 1.0)


def with_rest(high, level, levels):
    return high + jnp.abs(high) * (2.0**-8 * ((level + 0.5) * (2.0 / levels) - 1.0))


def norm_end(r):
    total = r.thx[TOTAL : TOTAL + 1, :]
    base = log_base(total)
    by_alog = r.thx[BY_ALOG : BY_ALOG + 1, :] - base * total
    bias_base = r.thx[BASE : BASE + 1, :] * (1.0 + base)
    by_bias = r.thx[BY_BIAS : BY_BIAS + 1, :] - bias_base * total
    for d in range(SEQ):
        at = slice(ROWS * d, ROWS * (d + 1))
        back, back_rest = rest_level(r.acc[at, :], 32)
        sin = r.sin[at, :]
        alog, alog_rest = rest_level(r.moments[at, :W] + by_alog * sin, 4)
        bias, bias_rest = rest_level(r.moments[at, W:] + by_bias * sin, 4)
        rests = 16.0 * back_rest + 4.0 * alog_rest + bias_rest - 256.0
        block = jnp.concatenate(
            [jnp.concatenate([back, rests], 1), jnp.concatenate([alog, bias], 1)], 0
        )
        to = slice(2 * ROWS * d, 2 * ROWS * (d + 1))
        r.back[to, :] = block.astype(BF16)
        if (d + 1) % (SEQ // FLUSHES) == 0:
            rows = 2 * STATE // FLUSHES
            piece = d * FLUSHES // SEQ
            r.flush("back", piece, slice(rows * piece, rows * (piece + 1)))
    r.sums[0:1, :] = jnp.sum(r.gain_acc[...], axis=0, keepdims=True)
    r.sums[1:8, :] = jnp.zeros((7, W), F32)


def local_x_begin(r):
    r.acc[...] = jnp.zeros((STATE, W), F32)


def local_x_body(c, r):
    ex = expand(r.pk, DTBETA, r.e3)
    al = expand(r.pk, ALPHA, r.e3)

    def scale(at):
        r.xhi[at, :], r.xlo[at, :] = split2(r.x[at, :].astype(F32) * ex[at, :])
        r.ghi[at, :], r.glo[at, :] = split2(r.gy[at, :] * al[at, :])

    each_rows(scale)
    b = r.bc[:, :STATE]
    cc = r.bc[:, STATE:]
    gys = (r.ghi[...], r.glo[...])
    g = (r.g[:, :L], r.g[:, L:])
    kappa = r.thx[pl.ds(KAP + c, 1), :]
    dstate = split2(kappa * r.acc[...])
    res = dot3(g, gys, TN) + dot2(b * r.marks[:, L : L + 128], dstate, NN)
    r.gs[:, :STATE] = r.marks[:, L : L + 128].astype(F32) * dot3_wide((r.xhi[...], r.xlo[...]), dstate)
    skip = r.vec[1:2, :]

    def finish(at):
        x = r.x[at, :].astype(F32)
        gy = r.gy[at, :]
        scaled = ex[at, :] * res[at, :]
        r.gx[at, :] = scaled + skip * gy
        r.rhi[at, :], r.rlo[at, :] = split2(fold(scaled * x))
        r.shi[at, :], r.slo[at, :] = split2(fold(gy * x))

    each_rows(finish)
    r.u[...] = dot2(r.eh[...], (r.rhi[...], r.rlo[...]), NT)
    r.sx[...] = dot2(r.eh[...], (r.shi[...], r.slo[...]), NT)
    r.rr[...] = r.r[...] - r.par[:, 2:3] * r.sx[...]
    state = split2(kappa * (r.sloc[...] + r.thx[pl.ds(PRE + c, 1), :] * r.sin[...]))
    r.gs[:, STATE:] = r.marks[:, L + 128 :].astype(F32) * dot3_wide(gys, state)
    r.acc[...] = r.thx[pl.ds(THR + c, 1), :] * r.acc[...] + kappa * dot2(cc * r.marks[:, L + 128 :], gys, TN)


def local_bc_body(c, r):
    al = expand(r.pk, ALPHA, r.e3)

    def scale(at):
        r.ghi[at, :], r.glo[at, :] = split2(r.gy[at, :] * al[at, :])

    each_rows(scale)
    b = r.bc[:, :STATE]
    cc = r.bc[:, STATE:]
    gys = (r.ghi[...], r.glo[...])
    xs = (r.xhi[...], r.xlo[...])
    q = split2(dot3(gys, xs, NT) * r.marks[:, :L].astype(F32))
    r.gb[...] = r.gs[:, :STATE] + joined(q, [cc, cc], TN)
    r.gc[...] = (r.gs[:, STATE:] + joined(q, [b, b], NN)).astype(BF16)


def final_begin(r):
    r.dhi[...], r.dlo[...] = split2(r.din[:, :W])


def final_bc_body(c, r):
    gb = r.gb[...] + dot3_wide((r.xhi[...], r.xlo[...]), (r.dhi[...], r.dlo[...]))
    r.out[:, :STATE] = gb.astype(BF16)
    r.out[:, STATE:] = r.gc[...]


def final_bc_end(r):
    total = r.din[0:ROWS, W:]
    for d in range(1, SEQ):
        total += r.din[ROWS * d : ROWS * (d + 1), W:]
    r.params[...] = total


def final_x_body(c, r):
    fin = expand(r.pk, TO_END, r.e3)
    v = dot2(r.bc[:, :STATE], (r.dhi[...], r.dlo[...]), NN)

    def body(at):
        scaled = fin[at, :] * v[at, :]
        r.gxo[at, :] = (r.gx[at, :] + scaled).astype(BF16)
        r.rhi[at, :], r.rlo[at, :] = split2(fold(scaled * r.x[at, :].astype(F32)))

    each_rows(body)
    r.uu[...] = r.u[...] + dot2(r.eh[...], (r.rhi[...], r.rlo[...]), NT)


def time_sums(r, r_ref, u_ref, carry, write):
    row = lax.broadcasted_iota(jnp.int32, (L, L), 0)
    col = lax.broadcasted_iota(jnp.int32, (L, L), 1)
    tri = (row >= col).astype(F32).astype(BF16)
    nega = -jnp.exp(r.par[:, 1:2])
    chunks = [slice(c * L, (c + 1) * L) for c in range(C)]
    parts = dot(jnp.concatenate([part for at in chunks for part in split3(r_ref[:, at] - u_ref[:, at])], 0), tri, NN)
    for c in reversed(range(C)):
        at = chunks[c]
        u = u_ref[:, at]
        dt = r.rf[0:H, at]
        base = 3 * H * c
        later = parts[base : base + H] + parts[base + H : base + 2 * H] + parts[base + 2 * H : base + 3 * H]
        grad_rate = later + carry
        carry = carry + later[:, 0:1]
        write(at, (u / dt + grad_rate * nega) * r.rf[H : 2 * H, at], grad_rate * dt * nega)


def local_x_end(r):
    sums = [jnp.zeros((H, 1), F32)] * 2

    def write(at, grad_dt, grad_alog):
        sums[0] += jnp.sum(grad_alog, axis=1, keepdims=True)
        sums[1] += jnp.sum(grad_dt, axis=1, keepdims=True)

    time_sums(r, r.rr, r.u, jnp.zeros((H, 1), F32), write)
    skip_part = jnp.sum(r.sx[...], axis=1, keepdims=True)
    lane = lax.broadcasted_iota(jnp.int32, (H, 128), 1)
    r.loc[...] = jnp.where(
        lane == 0, skip_part, jnp.where(lane == 1, sums[0], jnp.where(lane == 2, sums[1], 0.0))
    )


def final_x_end(r):
    for k in range(8):
        r.gain[:, 128 * k : 128 * (k + 1)] = r.params[k : k + 1, :128]
    row = lax.broadcasted_iota(jnp.int32, (ROWS, ROWS), 0)
    col = lax.broadcasted_iota(jnp.int32, (ROWS, ROWS), 1)
    same = (row == col).astype(F32).astype(BF16)
    turned = sum(dot(part, same, TN) for part in split3(r.params[:, 128:]))
    for ref, at in ((r.gskip, SKIPS), (r.galog, ALOGS), (r.gbias, BIASES)):
        ref[...] = jnp.concatenate([turned[at : at + 1, :], turned[at + 1 : at + 2, :]], 1)
    state = r.pay[:, :W] + r.thx[TOTAL : TOTAL + 1, :] * r.sin[...]
    ends = jnp.broadcast_to(jnp.sum(state * r.din[:, :W], axis=0, keepdims=True), (H, W))
    carry = sum(dot(r.e3[0:H, :], part, NT) for part in split3(ends))[:, 0:1]

    def write(at, grad_dt, grad_alog):
        r.gdt[:, at] = grad_dt

    time_sums(r, r.r, r.uu, carry, write)


def pack_kernel(b_ref, c_ref, out_ref, sems):
    copies = []
    for k, ref in enumerate((b_ref, c_ref)):
        for g in range(GRP):
            source = ref.at[:, STATE * g : STATE * (g + 1)]
            copies.append(pltpu.make_async_copy(source, out_ref.at[g, :, STATE * k : STATE * (k + 1)], sems.at[k, g]))
    for copy in copies:
        copy.start()
    for copy in copies:
        copy.wait()


def unpack_kernel(in_ref, b_ref, c_ref, sems):
    copies = []
    for g in range(GRP):
        at = slice(STATE * g, STATE * (g + 1))
        for k, ref in enumerate((b_ref, c_ref)):
            source = in_ref.at[g, :, STATE * k : STATE * (k + 1)]
            copies.append(pltpu.make_async_copy(source, ref.at[:, at], sems.at[k, g]))
    for copy in copies:
        copy.start()
    for copy in copies:
        copy.wait()


def head_matrix():
    one = np.arange(W)[None, :] // HEAD_DIM == np.arange(H)[:, None]
    return jnp.asarray(np.concatenate([one, one, one], 0), BF16)


def shard_body(
    x_in, z_gate, b_proj, c_proj, dt_raw, dt_bias, a_log, skip, norm_weight, doc_starts, grad_out
):
    e3 = head_matrix()
    par = jnp.pad(jnp.stack([dt_bias, a_log, skip], 1), ((0, 0), (0, 125)))
    vec = jnp.pad(
        jnp.stack([norm_weight, jnp.repeat(skip, HEAD_DIM)], 0), ((0, 6), (0, 0))
    )
    starts = doc_starts.reshape(1, T)
    far = pl.BlockSpec(memory_space=pl.ANY)
    mine = pl.pallas_call(
        pack_kernel,
        out_shape=pltpu.HBM((GRP, 128, 2 * STATE), BF16),
        out_specs=far,
        scratch_shapes=[pltpu.SemaphoreType.DMA((2, GRP))],
        compiler_params=pltpu.CompilerParams(vmem_limit_bytes=VMEM_LIMIT),
        name="pack",
    )(*[pltpu.with_memory_space_constraint(a, pltpu.HBM) for a in (b_proj, c_proj)])
    bc = lax.all_to_all(mine, "head", split_axis=0, concat_axis=0, tiled=True).reshape(T, 2 * STATE)

    sds = pltpu.HBM
    pk, rf, marks, thx = pl.pallas_call(
        prep_kernel,
        out_shape=(
            sds((12 * H, T), BF16),
            sds((2 * H, T), F32),
            sds((T, L + 256), BF16),
            sds((TABLE, W), F32),
        ),
        compiler_params=pltpu.CompilerParams(vmem_limit_bytes=VMEM_LIMIT),
        name="prep",
    )(*[pltpu.with_memory_space_constraint(a, pltpu.HBM) for a in (dt_raw, par, starts, e3)])

    pk, vec = lax.optimization_barrier((pk, vec))
    state = ((STATE, W), F32)
    half = ((L, W), BF16)
    folded = ((L, W // 2), BF16)
    eh = {"eh": (folded_heads(), "all")}
    unit = 2 * T * L * W
    common = {"e3": (e3, "all"), "pk": (pk, "row"), "thx": (thx, "all")}
    x = {"x": (x_in, "tok")}
    masks = {"marks": (marks, "tok")}

    xhi, xlo = staged(
        scale_body,
        {"e3": (e3, "all"), "pk": (pk, "row")} | x,
        {"xhi": ((T, W), BF16, "tok"), "xlo": ((T, W), BF16, "tok")},
        {},
        "scale",
        unit,
    )
    xhi, xlo, bc = lax.optimization_barrier((xhi, xlo, bc))
    pay, bc = staged(
        states_body,
        {"thx": (thx, "all"), "bc": (bc, "near_tok"), "xhi": (xhi, "tok"), "xlo": (xlo, "tok")},
        {"pay": ((STATE, W + 128), F32, "all"), "bc_copy": ((T, 2 * STATE), BF16, "copy")},
        {"acc": state},
        "states",
        2 * unit,
        begin=clear,
        end=states_end,
    )

    def scan(kernel, name, outs, got, *others, **more):
        return pl.pallas_call(
            kernel,
            out_shape=outs,
            **more,
            in_specs=[pl.BlockSpec(memory_space=pltpu.VMEM)] * (1 + len(others)),
            compiler_params=pltpu.CompilerParams(vmem_limit_bytes=16 * 2**20),
            name=name,
        )(
            pltpu.with_memory_space_constraint(got, pltpu.VMEM),
            *[pltpu.with_memory_space_constraint(a, pltpu.HBM) for a in others],
        )

    def exchange(v):
        return lax.all_to_all(v, "seq", split_axis=0, concat_axis=0, tiled=True)

    bcs = {"bc": (bc, "tok")}
    got = exchange(pay)
    y, sloc, wxhi, wxlo, g = staged(
        within_body,
        common | {"vec": (vec, "all")} | bcs | masks | x,
        {
            "y": ((T, W), F32, "tok"),
            "sloc": ((C, STATE, W), F32, "state"),
            "hi": ((T, W), BF16, "tok"),
            "lo": ((T, W), BF16, "tok"),
            "g": ((T, 2 * L), BF16, "tok"),
        },
        {"acc": state},
        "within",
        7 * unit,
        begin=clear,
    )
    y, sloc, got = lax.optimization_barrier((y, sloc, got))
    before, after, through = scan(
        scan_forward_kernel,
        "scan_forward",
        (sds((STATE, W), F32), sds((STATE, W), F32), sds((SEQ, W), F32)),
        got,
    )
    sin = exchange(before)
    tied, _ = lax.optimization_barrier((x_in, got))
    (moments,) = staged(
        moments_body,
        common | bcs | {"x": (tied, "tok"), "pay": (pay, "late")},
        {"moments": ((STATE, 2 * W), F32, "all")},
        {"hi": half, "lo": half, "hi2": half, "lo2": half},
        "moments",
        4 * unit,
        begin=moments_begin,
        end=moments_end,
    )
    moments, sin = lax.optimization_barrier((moments, sin))

    gy, gz, r, back, sums, sin = staged(
        norm_body,
        common
        | {"vec": (vec, "all"), "sin": (sin, "near")}
        | bcs
        | {"y": (y, "tok"), "z": (z_gate, "tok"), "go": (grad_out, "tok")}
        | {"moments": (moments, "late")},
        {
            "gy": ((T, W), F32, "tok"),
            "gz": ((T, W), BF16, "tok"),
            "r": ((H, T), F32, "row"),
            "back": ((2 * STATE, 2 * W), BF16, "blocks"),
            "sums": ((8, W), F32, "all"),
            "sin_copy": ((STATE, W), F32, "copy"),
        },
        {
            "gain_acc": ((8, W), F32),
            "acc": state,
            "shi": ((STATE, W), BF16),
            "slo": ((STATE, W), BF16),
            "hi": half,
            "lo": half,
            "rhi": half,
            "rlo": half,
        },
        "norm",
        6 * unit,
        begin=norm_begin,
        end=norm_end,
    )

    got_back = exchange(back)
    gx, u, r, gs, loc = staged(
        local_x_body,
        common
        | eh
        | {
            "vec": (vec, "all"),
            "sin": (sin, "all"),
            "par": (par, "all"),
            "rf": (rf, "row"),
            "r": (r, "row"),
        }
        | bcs
        | masks
        | {"g": (g, "tok"), "gy": (gy, "tok"), "sloc": (sloc, "state")}
        | x,
        {
            "gx": ((T, W), F32, "tok"),
            "u": ((H, T), F32, "row"),
            "rr": ((H, T), F32, "row"),
            "gs": ((T, 2 * STATE), F32, "tok"),
            "loc": ((H, 128), F32, "all"),
        },
        {
            "acc": state,
            "sx": ((H, T), F32),
            "shi": folded,
            "slo": folded,
            "ghi": half,
            "glo": half,
            "xhi": half,
            "xlo": half,
            "rhi": folded,
            "rlo": folded,
        },
        "local_x",
        7 * unit,
        backward=True,
        begin=local_x_begin,
        end=local_x_end,
    )
    gs, got_back = lax.optimization_barrier((gs, got_back))
    behind = scan(
        scan_backward_kernel,
        "scan_backward",
        sds((STATE, W + 256), F32),
        got_back,
        *(through, after, loc, sums, e3, thx),
        out_specs=far,
        scratch_shapes=[pltpu.VMEM((STATE, W + 256), F32), pltpu.SemaphoreType.DMA((2, SEQ))],
    )
    din = exchange(behind)
    gb, gc = staged(
        local_bc_body,
        {"e3": (e3, "all"), "pk": (pk, "row")}
        | bcs
        | masks | {"gy": (gy, "tok"), "xhi": (wxhi, "tok"), "xlo": (wxlo, "tok")}
        | {"gs": (gs, "tok")},
        {"gb": ((T, STATE), F32, "tok"), "gc": ((T, STATE), BF16, "tok")},
        {"ghi": half, "glo": half},
        "local_bc",
        5 * unit,
    )

    gb, din = lax.optimization_barrier((gb, din))
    gbc, din, params = staged(
        final_bc_body,
        {
            "din": (din, "near"),
            "gb": (gb, "tok"),
            "gc": (gc, "tok"),
            "xhi": (xhi, "tok"),
            "xlo": (xlo, "tok"),
        },
        {
            "out": ((T, 2 * STATE), BF16, "tok"),
            "din_copy": ((STATE, W + 256), F32, "copy"),
            "params": ((ROWS, 256), F32, "all"),
        },
        {"dhi": ((STATE, W), BF16), "dlo": ((STATE, W), BF16)},
        "final_bc",
        2 * unit,
        begin=final_begin,
        end=final_bc_end,
    )
    gbc, gx = lax.optimization_barrier((gbc, gx))
    back_bc = lax.all_to_all(
        gbc.reshape(GRP, 128, 2 * STATE), "head", split_axis=0, concat_axis=0, tiled=True
    )
    grad_x, grad_dt, grad_gain, grad_skip, grad_alog, grad_bias = staged(
        final_x_body,
        common
        | eh
        | {
            "din": (din, "all"),
            "sin": (sin, "all"),
            "pay": (pay, "all"),
            "par": (par, "all"),
            "rf": (rf, "row"),
            "r": (r, "row"),
            "u": (u, "row"),
            "params": (params, "all"),
        }
        | bcs
        | {"gx": (gx, "tok")}
        | x,
        {
            "gxo": ((T, W), BF16, "tok"),
            "gdt": ((H, T), F32, "row"),
            "gain": ((1, W), F32, "all"),
            "gskip": ((1, H), F32, "all"),
            "galog": ((1, H), F32, "all"),
            "gbias": ((1, H), F32, "all"),
        },
        {
            "uu": ((H, T), F32),
            "dhi": ((STATE, W), BF16),
            "dlo": ((STATE, W), BF16),
            "rhi": folded,
            "rlo": folded,
        },
        "final_x",
        3 * unit,
        begin=final_begin,
        end=final_x_end,
    )
    grad_b, grad_c = pl.pallas_call(
        unpack_kernel,
        out_shape=(pltpu.HBM((128, GRP * STATE), BF16), pltpu.HBM((128, GRP * STATE), BF16)),
        in_specs=[pl.BlockSpec(memory_space=pltpu.VMEM)],
        out_specs=(far, far),
        scratch_shapes=[pltpu.SemaphoreType.DMA((2, GRP))],
        compiler_params=pltpu.CompilerParams(vmem_limit_bytes=16 * 2**20),
        name="unpack",
    )(pltpu.with_memory_space_constraint(back_bc, pltpu.VMEM))
    grad_gain = grad_gain.reshape(W)
    grad_skip, grad_alog, grad_bias = grad_skip.reshape(H), grad_alog.reshape(H), grad_bias.reshape(H)
    return (grad_x, gz, grad_b, grad_c, grad_dt, grad_alog, grad_bias, grad_skip, grad_gain)


def solution(mesh):
    in_specs = (
        P("seq", "head"),
        P("seq", "head"),
        P(("seq", "head"), None),
        P(("seq", "head"), None),
        P("head", "seq"),
        P("head"),
        P("head"),
        P("head"),
        P("head"),
        P("seq"),
        P("seq", "head"),
    )
    out_specs = (
        P("seq", "head"),
        P("seq", "head"),
        P(("seq", "head"), None),
        P(("seq", "head"), None),
        P("head", "seq"),
        P("head"),
        P("head"),
        P("head"),
        P("head"),
    )
    return jax.shard_map(shard_body, mesh=mesh, in_specs=in_specs, out_specs=out_specs, check_vma=False)
```

```python
import jax
import jax.numpy as jnp
import numpy as np
from jax import lax
from jax.experimental import pallas as pl
from jax.experimental.pallas import tpu as pltpu
from jax.sharding import PartitionSpec as P

HEADS = 128
HEAD_DIM = 64
STATE = 128
PROJECTION_SETS = 8
EPSILON = 1e-05

T = 1024
H = 16
W = H * HEAD_DIM
L = 256
C = T // L
SEQ = 16
GRP = 8
ROWS = STATE // SEQ
F32 = jnp.float32
BF16 = jnp.bfloat16
FLUSHES = 4
BACK_LEVELS, ALOG_LEVELS, BIAS_LEVELS = 16, 2, 16
STEP = 16
VMEM_LIMIT = 60 * 2**20
VMEM_NEAR = 48 * 2**20

THR, KAP, PRE, TOTAL, BY_ALOG, BY_BIAS, BASE, TABLE = 0, 4, 8, 12, 13, 14, 15, 16
ALPHA, DTBETA, TO_END, FROM_START, END_ALOG, END_BIAS = 0, 1, 2, 3, 4, 5
SKIPS, ALOGS, BIASES = 0, 2, 4

NN = (((1,), (0,)), ((), ()))
NT = (((1,), (1,)), ((), ()))
TN = (((0,), (0,)), ((), ()))


def dot(a, b, dims):
    return lax.dot_general(a, b, dims, preferred_element_type=F32)


def split2(a):
    hi = a.astype(BF16)
    return hi, (a - hi.astype(F32)).astype(BF16)


def split3(a):
    hi, mid = split2(a)
    lo = (a - hi.astype(F32) - mid.astype(F32)).astype(BF16)
    return hi, mid, lo


def joined(a, b, dims):
    ((ka,), (kb,)), _ = dims
    return dot(jnp.concatenate(a, ka), jnp.concatenate(b, kb), dims)


def dot2(a, b, dims):
    return joined([a, a], b, dims)


def dot3(a, b, dims):
    return joined([a[0], a[0], a[1]], [b[0], b[1], b[0]], dims)


def dot3_wide(a, b):
    both = dot(a[0], jnp.concatenate(b, 0), NT)
    return both[:, :STATE] + both[:, STATE:] + dot(a[1], b[0], NT)


def each_rows(body):
    for i in range(L // STEP):
        body(slice(STEP * i, STEP * (i + 1)))


class Views:
    def __init__(self, buffers, kinds, c):
        for name, ref in buffers.items():
            kind = kinds[name]
            if kind in ("tok", "near_tok"):
                ref = ref.at[pl.ds(pl.multiple_of(c * L, L), L), :]
            elif kind == "row":
                ref = ref.at[:, pl.ds(pl.multiple_of(c * L, L), L)]
            elif kind == "state":
                ref = ref.at[c]
            setattr(self, name, ref)


def staged(body, ins, outs, scratch, name, flops, backward=False, begin=None, end=None):
    kinds = {k: kind for k, (_, kind) in ins.items()}
    kinds.update({k: kind for k, (_, _, kind) in outs.items()})
    kinds.update({k: "row" if shape == (H, T) else "all" for k, (shape, _) in scratch.items()})
    n, m = len(ins), len(outs)
    moving = ("tok", "state")
    here = [k for k in ins if kinds[k] in ("near", "near_tok")]
    copied = [k for k in outs if kinds[k] == "copy"]
    steps = C
    slot, count = {}, 0
    for k in [*ins, *outs]:
        slot[k] = count
        count += {"tok": steps, "state": steps, "blocks": FLUSHES, "near": 0, "near_tok": 0}.get(kinds[k], 1)
    buffered_in = [k for k in ins if k not in here]
    buffered_out = [k for k in outs if k not in copied]

    def part(ref, kind, c):
        if kind == "tok":
            return ref.at[pl.ds(pl.multiple_of(c * L, L), L), :]
        return ref.at[c]

    def kernel(*refs):
        far_in = dict(zip(ins, refs[:n]))
        far_out = dict(zip(outs, refs[n : n + m]))
        near = dict(zip([*buffered_in, *buffered_out, *scratch], refs[n + m : -1]))
        near.update({k: far_in[k] for k in here})
        sems = refs[-1]

        def copy_in(k, c):
            return pltpu.make_async_copy(part(far_in[k], kinds[k], c), part(near[k], kinds[k], c), sems.at[slot[k] + c])

        def copy_out(k, c):
            return pltpu.make_async_copy(part(near[k], kinds[k], c), part(far_out[k], kinds[k], c), sems.at[slot[k] + c])

        once = [
            pltpu.make_async_copy(far_in[k], near[k], sems.at[slot[k]])
            for k in buffered_in
            if kinds[k] in ("row", "all")
        ]
        late = [pltpu.make_async_copy(far_in[k], near[k], sems.at[slot[k]]) for k in ins if kinds[k] == "late"]
        passed = [
            pltpu.make_async_copy(near[k.removesuffix("_copy")], far_out[k], sems.at[slot[k]]) for k in copied
        ]
        for copy in once:
            copy.start()
        for c in reversed(range(C)) if backward else range(C):
            for k in ins:
                if kinds[k] in moving:
                    copy_in(k, c).start()
        for copy in late + passed:
            copy.start()
        for copy in once:
            copy.wait()
        whole = Views(near, {k: "all" for k in near}, 0)
        flushed = []

        def flush(k, i, at):
            copy = pltpu.make_async_copy(near[k].at[at, :], far_out[k].at[at, :], sems.at[slot[k] + i])
            copy.start()
            flushed.append(copy)

        whole.flush = flush
        if begin is not None:
            begin(whole)

        def step(i, carry):
            c = C - 1 - i if backward else i
            for k in ins:
                if kinds[k] in moving:
                    copy_in(k, c).wait()
            body(c, Views(near, kinds, c))
            for k in outs:
                if kinds[k] in moving:
                    copy_out(k, c).start()
            return carry

        lax.fori_loop(0, C, step, 0)
        for copy in late:
            copy.wait()
        if end is not None:
            end(whole)
        once = [
            pltpu.make_async_copy(near[k], far_out[k], sems.at[slot[k]])
            for k in buffered_out
            if kinds[k] in ("row", "all")
        ]
        for copy in once:
            copy.start()
        for c in range(C):
            for k in outs:
                if kinds[k] in moving:
                    copy_out(k, c).wait()
        for copy in once + passed + flushed:
            copy.wait()

    far = pl.BlockSpec(memory_space=pl.ANY)
    return pl.pallas_call(
        kernel,
        out_shape=tuple(pltpu.HBM(s, d) for s, d, _ in outs.values()),
        in_specs=[pl.BlockSpec(memory_space=pltpu.VMEM) if k in here else far for k in ins],
        out_specs=tuple([far] * m),
        scratch_shapes=[
            *[pltpu.VMEM(ins[k][0].shape, ins[k][0].dtype) for k in buffered_in],
            *[pltpu.VMEM(*outs[k][:2]) for k in buffered_out],
            *[pltpu.VMEM(s, d) for s, d in scratch.values()],
            pltpu.SemaphoreType.DMA((count,)),
        ],
        compiler_params=pltpu.CompilerParams(vmem_limit_bytes=VMEM_NEAR if here else VMEM_LIMIT),
        cost_estimate=pl.CostEstimate(flops=flops, bytes_accessed=8 * 2**20, transcendentals=0),
        name=name,
    )(*[pltpu.with_memory_space_constraint(ins[k][0], pltpu.VMEM if k in here else pltpu.HBM) for k in ins])


def expand(pk, which, e3):
    return dot(pk[2 * H * which : 2 * H * (which + 1), :], e3[0 : 2 * H, :], TN)


def fold(v):
    lane = lax.broadcasted_iota(jnp.int32, (STEP, 128), 1)
    tiles = []
    for k in range(0, W, 256):
        a, b = v[:, k : k + 128], v[:, k + 128 : k + 256]
        a = a + pltpu.roll(a, 96, 1)
        b = b + pltpu.roll(b, 32, 1)
        tiles.append(jnp.where((lane & 32) == 0, a, b))
    return jnp.concatenate(tiles, 1)


def folded_heads():
    lane = np.arange(W // 2)
    head = 4 * (lane // 128) + (lane % 128 >= 64) + 2 * ((lane & 32) != 0)
    return jnp.asarray(head[None, :] == np.arange(H)[:, None], BF16)


def prep_kernel(dt_ref, par_ref, st_ref, e3_ref, pk_ref, rf_ref, marks_ref, thx_ref):
    bias = par_ref[:, 0:1]
    nega = -jnp.exp(par_ref[:, 1:2])
    row = lax.broadcasted_iota(jnp.int32, (L, L), 0)
    col = lax.broadcasted_iota(jnp.int32, (L, L), 1)
    tri = (row <= col).astype(F32).astype(BF16)
    causal = row >= col
    first = lax.broadcasted_iota(jnp.int32, (H, L), 0) == 0
    lane = lax.broadcasted_iota(jnp.int32, (H, 128), 1)
    ones = jnp.ones((H, L), BF16)
    thr, kap, leave, enter, rest, ratio, sig_rest, rate_sum, sig_sum = [], [], [], [], [], [], [], [], []

    def put(which, at, value):
        base = 2 * H * which
        pk_ref[base : base + H, at], pk_ref[base + H : base + 2 * H, at] = split2(value)

    for c in range(C):
        at = slice(c * L, (c + 1) * L)
        pre = dt_ref[:, at] + bias
        dt = jax.nn.softplus(pre)
        rf_ref[0:H, at] = dt
        sig = jax.nn.sigmoid(pre)
        rf_ref[H : 2 * H, at] = sig
        rate = dt * nega
        parts = dot(jnp.concatenate(split3(rate) + split3(sig), 0), tri, NN)
        cum = parts[0:H] + parts[H : 2 * H] + parts[2 * H : 3 * H]
        sig_cum = parts[3 * H : 4 * H] + parts[4 * H : 5 * H] + parts[5 * H : 6 * H]
        starts = jnp.broadcast_to(st_ref[:, at].astype(F32), (H, L))
        seg = dot(starts.astype(BF16), tri, NN)
        cum_end = cum[:, L - 1 : L]
        seg_end = seg[:, L - 1 : L]
        half = 0.5 * cum_end
        put(ALPHA, at, jnp.exp(cum - half))
        put(DTBETA, at, dt * jnp.exp(half - cum))
        leave.append(jnp.where(seg == seg_end, dt * jnp.exp(cum_end - cum), 0.0))
        rest.append(cum_end - cum)
        ratio.append(sig / dt)
        sig_rest.append(sig_cum[:, L - 1 : L] - sig_cum)
        rate_sum.append(cum_end)
        sig_sum.append(sig_cum[:, L - 1 : L])
        enter.append(jnp.where(seg == 0.0, jnp.exp(cum), 0.0))
        seg_first = jnp.where(first, seg, 0.0).astype(BF16)
        seg_col = dot(seg_first, ones, TN)
        mask = causal & (seg_col == seg[0:1, :])
        marks_ref[at, :L] = mask.astype(F32).astype(BF16)
        to_end = jnp.where(first & (seg == seg_end), 1.0, 0.0).astype(BF16)
        from_start = jnp.where(first & (seg == 0.0), 1.0, 0.0).astype(BF16)
        marks_ref[at, L : L + 128] = dot(to_end, ones[:, :128], TN).astype(BF16)
        marks_ref[at, L + 128 :] = dot(from_start, ones[:, :128], TN).astype(BF16)
        thr.append(jnp.where(seg_end == 0.0, jnp.exp(cum_end), 0.0))
        kap.append(jnp.exp(half))
    passed = jnp.ones((H, 1), F32)
    before = []
    for c in range(C):
        before.append(passed)
        put(FROM_START, slice(c * L, (c + 1) * L), enter[c] * passed)
        passed = passed * thr[c]
    columns = [*thr, *kap, *before, passed, passed * sum(rate_sum), passed * nega * sum(sig_sum)]
    columns.append(jax.nn.sigmoid(bias) / jax.nn.softplus(bias))
    passed = jnp.ones((H, 1), F32)
    rate_after = jnp.zeros((H, 1), F32)
    sig_after = jnp.zeros((H, 1), F32)
    for c in reversed(range(C)):
        at = slice(c * L, (c + 1) * L)
        to_shard_end = leave[c] * passed
        put(TO_END, at, to_shard_end)
        put(END_ALOG, at, to_shard_end * (rest[c] + rate_after))
        put(END_BIAS, at, to_shard_end * (ratio[c] + nega * (sig_rest[c] + sig_after)))
        passed = passed * thr[c]
        rate_after += rate_sum[c]
        sig_after += sig_sum[c]
    table = jnp.zeros((H, 128), F32)
    for k, v in enumerate(columns):
        table = jnp.where(lane == k, v, table)
    wide = dot(jnp.concatenate(split3(table), 0), e3_ref[...], TN)
    thx_ref[...] = wide[0:TABLE]


def scale_body(c, r):
    scale = expand(r.pk, TO_END, r.e3)

    def rows(at):
        r.xhi[at, :], r.xlo[at, :] = split2(r.x[at, :].astype(F32) * scale[at, :])

    each_rows(rows)


def states_body(c, r):
    r.acc[...] += dot2(r.bc[:, :STATE], (r.xhi[...], r.xlo[...]), TN)


def clear(r):
    r.acc[...] = jnp.zeros((STATE, W), F32)


def states_end(r):
    r.pay[:, :W] = r.acc[...]
    total = r.thx[TOTAL : TOTAL + 1, :]
    block = jnp.concatenate([total[:, 128 * k : 128 * (k + 1)] for k in range(ROWS)], 0)
    for d in range(SEQ):
        r.pay[ROWS * d : ROWS * (d + 1), W:] = block


def log_base(through):
    return jnp.where(through > 1e-30, 0.5 * jnp.log(jnp.maximum(through, 1e-30)), 0.0)


def moments_body(c, r):
    by_alog = expand(r.pk, END_ALOG, r.e3)
    by_bias = expand(r.pk, END_BIAS, r.e3)

    def rows(at):
        x = r.x[at, :].astype(F32)
        r.hi[at, :], r.lo[at, :] = split2(x * by_alog[at, :])
        r.hi2[at, :], r.lo2[at, :] = split2(x * by_bias[at, :])

    each_rows(rows)
    b = r.bc[:, :STATE]
    r.moments[:, :W] += dot2(b, (r.hi[...], r.lo[...]), TN)
    r.moments[:, W:] += dot2(b, (r.hi2[...], r.lo2[...]), TN)


def moments_begin(r):
    r.moments[...] = jnp.zeros((STATE, 2 * W), F32)


def moments_end(r):
    base = log_base(r.thx[TOTAL : TOTAL + 1, :])
    own = r.pay[:, :W]
    r.moments[:, :W] -= base * own
    r.moments[:, W:] -= (r.thx[BASE : BASE + 1, :] * (1.0 + base)) * own


def through_row(got_ref, j):
    block = got_ref[ROWS * j : ROWS * (j + 1), W:]
    return jnp.concatenate([block[k : k + 1, :] for k in range(ROWS)], 1)


def scan_forward_kernel(got_ref, out_ref, after_ref, through_ref):
    acc = jnp.zeros((ROWS, W), F32)
    for j in range(SEQ):
        at = slice(ROWS * j, ROWS * (j + 1))
        out_ref[at, :] = acc
        through = through_row(got_ref, j)
        through_ref[j : j + 1, :] = through
        acc = through * acc + got_ref[at, :W]
        after_ref[at, :] = acc


def scan_backward_kernel(got_ref, through_ref, after_ref, loc_ref, sums_ref, e3_ref, thx_ref, far_ref, out_ref, sems):
    acc = jnp.zeros((ROWS, W), F32)
    by_alog = jnp.zeros((ROWS, W), F32)
    by_bias = jnp.zeros((ROWS, W), F32)
    through_all = through_ref[...]
    base_all = log_base(through_all)
    bias_base_all = thx_ref[BASE : BASE + 1, :] * (1.0 + base_all)
    copies = []

    def send(j, lanes, k):
        at = slice(ROWS * j, ROWS * (j + 1))
        copy = pltpu.make_async_copy(out_ref.at[at, lanes], far_ref.at[at, lanes], sems.at[k, j])
        copy.start()
        copies.append(copy)

    for j in reversed(range(SEQ)):
        at = slice(ROWS * j, ROWS * (j + 1))
        out_ref[at, :W] = acc
        send(j, slice(0, W), 0)
        block = got_ref[2 * ROWS * j : 2 * ROWS * (j + 1), :].astype(F32)
        through = through_all[j : j + 1, :]
        state = after_ref[at, :]
        rests = block[:ROWS, W:] + 256.0
        upper = jnp.floor(rests * (1.0 / BIAS_LEVELS))
        bias_rest = rests - BIAS_LEVELS * upper
        back_rest = jnp.floor(upper * (1.0 / ALOG_LEVELS))
        alog_rest = upper - ALOG_LEVELS * back_rest
        base = base_all[j : j + 1, :]
        bias_base = bias_base_all[j : j + 1, :]
        by_alog += acc * (with_rest(block[ROWS:, :W], alog_rest, ALOG_LEVELS) + base * state)
        by_bias += acc * (with_rest(block[ROWS:, W:], bias_rest, BIAS_LEVELS) + bias_base * state)
        acc = through * acc + with_rest(block[:ROWS, :W], back_rest, BACK_LEVELS)
    row = lax.broadcasted_iota(jnp.int32, (H, W), 0)
    vector = jnp.where(
        row == 0,
        jnp.sum(by_alog, axis=0, keepdims=True),
        jnp.where(row == 1, jnp.sum(by_bias, axis=0, keepdims=True), 0.0),
    )
    heads = e3_ref[0:H, :]
    far = sum(dot(heads, part, NT) for part in split3(vector))
    lane = lax.broadcasted_iota(jnp.int32, (ROWS, 128), 1)
    right = jnp.zeros((ROWS, 128), F32)
    for k in range(2):
        at = slice(ROWS * k, ROWS * (k + 1))
        right = jnp.where(lane == SKIPS + k, loc_ref[at, 0:1], right)
        right = jnp.where(lane == ALOGS + k, loc_ref[at, 1:2] + far[at, 0:1], right)
        right = jnp.where(lane == BIASES + k, loc_ref[at, 2:3] + far[at, 1:2], right)
    gains = sums_ref[0:1, :]
    left = jnp.concatenate([gains[:, 128 * k : 128 * (k + 1)] for k in range(8)], 0)
    for d in range(SEQ):
        out_ref[ROWS * d : ROWS * (d + 1), W : W + 128] = left
        out_ref[ROWS * d : ROWS * (d + 1), W + 128 :] = right
        send(d, slice(W, W + 256), 1)
    for copy in copies:
        copy.wait()


def within_body(c, r):
    ex = expand(r.pk, DTBETA, r.e3)
    al = expand(r.pk, ALPHA, r.e3)

    def scale(at):
        r.hi[at, :], r.lo[at, :] = split2(r.x[at, :].astype(F32) * ex[at, :])

    each_rows(scale)
    b = r.bc[:, :STATE]
    cc = r.bc[:, STATE:]
    g = split2(dot(cc, b, NT) * r.marks[:, :L].astype(F32))
    r.g[:, :L], r.g[:, L:] = g
    xs = (r.hi[...], r.lo[...])
    kappa = r.thx[pl.ds(KAP + c, 1), :]
    r.sloc[...] = r.acc[...]
    res = dot3(g, xs, NN) + dot2(cc * r.marks[:, L + 128 :], split2(kappa * r.acc[...]), NN)
    r.y[...] = al * res + r.vec[1:2, :] * r.x[...].astype(F32)
    r.acc[...] = r.thx[pl.ds(THR + c, 1), :] * r.acc[...] + kappa * dot2(b * r.marks[:, L : L + 128], xs, TN)


def norm_begin(r):
    r.shi[...], r.slo[...] = split2(r.sin[...])
    r.gain_acc[...] = jnp.zeros((8, W), F32)
    r.acc[...] = jnp.zeros((STATE, W), F32)


def norm_body(c, r):
    cc = r.bc[:, STATE:]
    win = expand(r.pk, FROM_START, r.e3)
    res = dot2(cc, (r.shi[...], r.slo[...]), NN)
    gain = r.vec[0:1, :]

    def body(at):
        weight = win[at, :]
        z = r.z[at, :].astype(F32)
        out = r.go[at, :].astype(F32)
        y = r.y[at, :] + weight * res[at, :]
        logistic = jax.nn.sigmoid(z)
        silu = z * logistic
        gated = y * silu
        grad_normed = out * gain
        square = jnp.sum(gated * gated, axis=1, keepdims=True) * (1.0 / W)
        cross = jnp.sum(grad_normed * gated, axis=1, keepdims=True) * (1.0 / W)
        inv = lax.rsqrt(square + EPSILON)
        normed = gated * inv
        grad_gated = inv * (grad_normed - normed * (inv * cross))
        gy = grad_gated * silu
        gz = grad_gated * y * (logistic + silu * (1.0 - logistic))
        r.gz[at, :] = gz.astype(BF16)
        r.gy[at, :] = gy
        gpart = out * normed
        r.gain_acc[...] += gpart[0:8] + gpart[8:16]
        r.hi[at, :], r.lo[at, :] = split2(gy * weight)
        r.rhi[at, :], r.rlo[at, :] = split2(gy * y)

    each_rows(body)
    r.r[...] = dot2(r.e3[0:H, :], (r.rhi[...], r.rlo[...]), NT)
    new = dot2(cc, (r.hi[...], r.lo[...]), TN)
    r.acc[...] += new


def rest_level(value, levels):
    high = value.astype(BF16).astype(F32)
    place = (value - high) * pl.reciprocal(jnp.maximum(jnp.abs(high) * 2.0**-8, 1e-30), approx=True) + 1.0
    return high, jnp.clip(jnp.floor(place * (levels / 2)), 0.0, levels - 1.0)


def with_rest(high, level, levels):
    return high + jnp.abs(high) * (2.0**-8 * ((level + 0.5) * (2.0 / levels) - 1.0))


def norm_end(r):
    total = r.thx[TOTAL : TOTAL + 1, :]
    base = log_base(total)
    by_alog = r.thx[BY_ALOG : BY_ALOG + 1, :] - base * total
    bias_base = r.thx[BASE : BASE + 1, :] * (1.0 + base)
    by_bias = r.thx[BY_BIAS : BY_BIAS + 1, :] - bias_base * total
    for d in range(SEQ):
        at = slice(ROWS * d, ROWS * (d + 1))
        back, back_rest = rest_level(r.acc[at, :], BACK_LEVELS)
        sin = r.sin[at, :]
        alog, alog_rest = rest_level(r.moments[at, :W] + by_alog * sin, ALOG_LEVELS)
        bias, bias_rest = rest_level(r.moments[at, W:] + by_bias * sin, BIAS_LEVELS)
        rests = (back_rest * ALOG_LEVELS + alog_rest) * BIAS_LEVELS + bias_rest - 256.0
        block = jnp.concatenate(
            [jnp.concatenate([back, rests], 1), jnp.concatenate([alog, bias], 1)], 0
        )
        to = slice(2 * ROWS * d, 2 * ROWS * (d + 1))
        r.back[to, :] = block.astype(BF16)
        if (d + 1) % (SEQ // FLUSHES) == 0:
            rows = 2 * STATE // FLUSHES
            piece = d * FLUSHES // SEQ
            r.flush("back", piece, slice(rows * piece, rows * (piece + 1)))
    r.sums[0:1, :] = jnp.sum(r.gain_acc[...], axis=0, keepdims=True)
    r.sums[1:8, :] = jnp.zeros((7, W), F32)


def local_x_begin(r):
    r.acc[...] = jnp.zeros((STATE, W), F32)


def local_x_body(c, r):
    ex = expand(r.pk, DTBETA, r.e3)
    al = expand(r.pk, ALPHA, r.e3)

    def scale(at):
        r.xhi[at, :], r.xlo[at, :] = split2(r.x[at, :].astype(F32) * ex[at, :])
        r.ghi[at, :], r.glo[at, :] = split2(r.gy[at, :] * al[at, :])

    each_rows(scale)
    b = r.bc[:, :STATE]
    cc = r.bc[:, STATE:]
    gys = (r.ghi[...], r.glo[...])
    g = (r.g[:, :L], r.g[:, L:])
    kappa = r.thx[pl.ds(KAP + c, 1), :]
    dstate = split2(kappa * r.acc[...])
    res = dot3(g, gys, TN) + dot2(b * r.marks[:, L : L + 128], dstate, NN)
    r.gs[:, :STATE] = r.marks[:, L : L + 128].astype(F32) * dot3_wide((r.xhi[...], r.xlo[...]), dstate)
    skip = r.vec[1:2, :]

    def finish(at):
        x = r.x[at, :].astype(F32)
        gy = r.gy[at, :]
        scaled = ex[at, :] * res[at, :]
        r.gx[at, :] = scaled + skip * gy
        r.rhi[at, :], r.rlo[at, :] = split2(fold(scaled * x))
        r.shi[at, :], r.slo[at, :] = split2(fold(gy * x))

    each_rows(finish)
    r.u[...] = dot2(r.eh[...], (r.rhi[...], r.rlo[...]), NT)
    r.sx[...] = dot2(r.eh[...], (r.shi[...], r.slo[...]), NT)
    r.rr[...] = r.r[...] - r.par[:, 2:3] * r.sx[...]
    state = split2(kappa * (r.sloc[...] + r.thx[pl.ds(PRE + c, 1), :] * r.sin[...]))
    r.gs[:, STATE:] = r.marks[:, L + 128 :].astype(F32) * dot3_wide(gys, state)
    r.acc[...] = r.thx[pl.ds(THR + c, 1), :] * r.acc[...] + kappa * dot2(cc * r.marks[:, L + 128 :], gys, TN)


def local_bc_body(c, r):
    al = expand(r.pk, ALPHA, r.e3)

    def scale(at):
        r.ghi[at, :], r.glo[at, :] = split2(r.gy[at, :] * al[at, :])

    each_rows(scale)
    b = r.bc[:, :STATE]
    cc = r.bc[:, STATE:]
    gys = (r.ghi[...], r.glo[...])
    xs = (r.xhi[...], r.xlo[...])
    q = split2(dot3(gys, xs, NT) * r.marks[:, :L].astype(F32))
    r.gb[...] = r.gs[:, :STATE] + joined(q, [cc, cc], TN)
    r.gc[...] = (r.gs[:, STATE:] + joined(q, [b, b], NN)).astype(BF16)


def final_begin(r):
    r.dhi[...], r.dlo[...] = split2(r.din[:, :W])


def final_bc_body(c, r):
    gb = r.gb[...] + dot3_wide((r.xhi[...], r.xlo[...]), (r.dhi[...], r.dlo[...]))
    r.out[:, :STATE] = gb.astype(BF16)
    r.out[:, STATE:] = r.gc[...]


def final_bc_end(r):
    total = r.din[0:ROWS, W:]
    for d in range(1, SEQ):
        total += r.din[ROWS * d : ROWS * (d + 1), W:]
    r.params[...] = total


def final_x_body(c, r):
    fin = expand(r.pk, TO_END, r.e3)
    v = dot2(r.bc[:, :STATE], (r.dhi[...], r.dlo[...]), NN)

    def body(at):
        scaled = fin[at, :] * v[at, :]
        r.gxo[at, :] = (r.gx[at, :] + scaled).astype(BF16)
        r.rhi[at, :], r.rlo[at, :] = split2(fold(scaled * r.x[at, :].astype(F32)))

    each_rows(body)
    r.uu[...] = r.u[...] + dot2(r.eh[...], (r.rhi[...], r.rlo[...]), NT)


def time_sums(r, r_ref, u_ref, carry, write):
    row = lax.broadcasted_iota(jnp.int32, (L, L), 0)
    col = lax.broadcasted_iota(jnp.int32, (L, L), 1)
    tri = (row >= col).astype(F32).astype(BF16)
    nega = -jnp.exp(r.par[:, 1:2])
    chunks = [slice(c * L, (c + 1) * L) for c in range(C)]
    parts = dot(jnp.concatenate([part for at in chunks for part in split3(r_ref[:, at] - u_ref[:, at])], 0), tri, NN)
    for c in reversed(range(C)):
        at = chunks[c]
        u = u_ref[:, at]
        dt = r.rf[0:H, at]
        base = 3 * H * c
        later = parts[base : base + H] + parts[base + H : base + 2 * H] + parts[base + 2 * H : base + 3 * H]
        grad_rate = later + carry
        carry = carry + later[:, 0:1]
        write(at, (u / dt + grad_rate * nega) * r.rf[H : 2 * H, at], grad_rate * dt * nega)


def local_x_end(r):
    sums = [jnp.zeros((H, 1), F32)] * 2

    def write(at, grad_dt, grad_alog):
        sums[0] += jnp.sum(grad_alog, axis=1, keepdims=True)
        sums[1] += jnp.sum(grad_dt, axis=1, keepdims=True)

    time_sums(r, r.rr, r.u, jnp.zeros((H, 1), F32), write)
    skip_part = jnp.sum(r.sx[...], axis=1, keepdims=True)
    lane = lax.broadcasted_iota(jnp.int32, (H, 128), 1)
    r.loc[...] = jnp.where(
        lane == 0, skip_part, jnp.where(lane == 1, sums[0], jnp.where(lane == 2, sums[1], 0.0))
    )


def final_x_end(r):
    for k in range(8):
        r.gain[:, 128 * k : 128 * (k + 1)] = r.params[k : k + 1, :128]
    row = lax.broadcasted_iota(jnp.int32, (ROWS, ROWS), 0)
    col = lax.broadcasted_iota(jnp.int32, (ROWS, ROWS), 1)
    same = (row == col).astype(F32).astype(BF16)
    turned = sum(dot(part, same, TN) for part in split3(r.params[:, 128:]))
    for ref, at in ((r.gskip, SKIPS), (r.galog, ALOGS), (r.gbias, BIASES)):
        ref[...] = jnp.concatenate([turned[at : at + 1, :], turned[at + 1 : at + 2, :]], 1)
    state = r.pay[:, :W] + r.thx[TOTAL : TOTAL + 1, :] * r.sin[...]
    ends = jnp.broadcast_to(jnp.sum(state * r.din[:, :W], axis=0, keepdims=True), (H, W))
    carry = sum(dot(r.e3[0:H, :], part, NT) for part in split3(ends))[:, 0:1]

    def write(at, grad_dt, grad_alog):
        r.gdt[:, at] = grad_dt

    time_sums(r, r.r, r.uu, carry, write)


def pack_kernel(b_ref, c_ref, out_ref, sems):
    copies = []
    for k, ref in enumerate((b_ref, c_ref)):
        for g in range(GRP):
            source = ref.at[:, STATE * g : STATE * (g + 1)]
            copies.append(pltpu.make_async_copy(source, out_ref.at[g, :, STATE * k : STATE * (k + 1)], sems.at[k, g]))
    for copy in copies:
        copy.start()
    for copy in copies:
        copy.wait()


def unpack_kernel(in_ref, b_ref, c_ref, sems):
    copies = []
    for g in range(GRP):
        at = slice(STATE * g, STATE * (g + 1))
        for k, ref in enumerate((b_ref, c_ref)):
            source = in_ref.at[g, :, STATE * k : STATE * (k + 1)]
            copies.append(pltpu.make_async_copy(source, ref.at[:, at], sems.at[k, g]))
    for copy in copies:
        copy.start()
    for copy in copies:
        copy.wait()


def head_matrix():
    one = np.arange(W)[None, :] // HEAD_DIM == np.arange(H)[:, None]
    return jnp.asarray(np.concatenate([one, one, one], 0), BF16)


def shard_body(
    x_in, z_gate, b_proj, c_proj, dt_raw, dt_bias, a_log, skip, norm_weight, doc_starts, grad_out
):
    e3 = head_matrix()
    par = jnp.pad(jnp.stack([dt_bias, a_log, skip], 1), ((0, 0), (0, 125)))
    vec = jnp.pad(
        jnp.stack([norm_weight, jnp.repeat(skip, HEAD_DIM)], 0), ((0, 6), (0, 0))
    )
    starts = doc_starts.reshape(1, T)
    far = pl.BlockSpec(memory_space=pl.ANY)
    mine = pl.pallas_call(
        pack_kernel,
        out_shape=pltpu.HBM((GRP, 128, 2 * STATE), BF16),
        out_specs=far,
        scratch_shapes=[pltpu.SemaphoreType.DMA((2, GRP))],
        compiler_params=pltpu.CompilerParams(vmem_limit_bytes=VMEM_LIMIT),
        name="pack",
    )(*[pltpu.with_memory_space_constraint(a, pltpu.HBM) for a in (b_proj, c_proj)])
    bc = lax.all_to_all(mine, "head", split_axis=0, concat_axis=0, tiled=True).reshape(T, 2 * STATE)

    sds = pltpu.HBM
    pk, rf, marks, thx = pl.pallas_call(
        prep_kernel,
        out_shape=(
            sds((12 * H, T), BF16),
            sds((2 * H, T), F32),
            sds((T, L + 256), BF16),
            sds((TABLE, W), F32),
        ),
        compiler_params=pltpu.CompilerParams(vmem_limit_bytes=VMEM_LIMIT),
        name="prep",
    )(*[pltpu.with_memory_space_constraint(a, pltpu.HBM) for a in (dt_raw, par, starts, e3)])

    pk, vec = lax.optimization_barrier((pk, vec))
    state = ((STATE, W), F32)
    half = ((L, W), BF16)
    folded = ((L, W // 2), BF16)
    eh = {"eh": (folded_heads(), "all")}
    unit = 2 * T * L * W
    common = {"e3": (e3, "all"), "pk": (pk, "row"), "thx": (thx, "all")}
    x = {"x": (x_in, "tok")}
    masks = {"marks": (marks, "tok")}

    xhi, xlo = staged(
        scale_body,
        {"e3": (e3, "all"), "pk": (pk, "row")} | x,
        {"xhi": ((T, W), BF16, "tok"), "xlo": ((T, W), BF16, "tok")},
        {},
        "scale",
        unit,
    )
    xhi, xlo, bc = lax.optimization_barrier((xhi, xlo, bc))
    pay, bc = staged(
        states_body,
        {"thx": (thx, "all"), "bc": (bc, "near_tok"), "xhi": (xhi, "tok"), "xlo": (xlo, "tok")},
        {"pay": ((STATE, W + 128), F32, "all"), "bc_copy": ((T, 2 * STATE), BF16, "copy")},
        {"acc": state},
        "states",
        2 * unit,
        begin=clear,
        end=states_end,
    )

    def scan(kernel, name, outs, got, *others, **more):
        return pl.pallas_call(
            kernel,
            out_shape=outs,
            **more,
            in_specs=[pl.BlockSpec(memory_space=pltpu.VMEM)] * (1 + len(others)),
            compiler_params=pltpu.CompilerParams(vmem_limit_bytes=16 * 2**20),
            name=name,
        )(
            pltpu.with_memory_space_constraint(got, pltpu.VMEM),
            *[pltpu.with_memory_space_constraint(a, pltpu.HBM) for a in others],
        )

    def exchange(v):
        return lax.all_to_all(v, "seq", split_axis=0, concat_axis=0, tiled=True)

    bcs = {"bc": (bc, "tok")}
    got = exchange(pay)
    y, sloc, wxhi, wxlo, g = staged(
        within_body,
        common | {"vec": (vec, "all")} | bcs | masks | x,
        {
            "y": ((T, W), F32, "tok"),
            "sloc": ((C, STATE, W), F32, "state"),
            "hi": ((T, W), BF16, "tok"),
            "lo": ((T, W), BF16, "tok"),
            "g": ((T, 2 * L), BF16, "tok"),
        },
        {"acc": state},
        "within",
        7 * unit,
        begin=clear,
    )
    y, sloc, got = lax.optimization_barrier((y, sloc, got))
    before, after, through = scan(
        scan_forward_kernel,
        "scan_forward",
        (sds((STATE, W), F32), sds((STATE, W), F32), sds((SEQ, W), F32)),
        got,
    )
    sin = exchange(before)
    tied, _ = lax.optimization_barrier((x_in, got))
    (moments,) = staged(
        moments_body,
        common | bcs | {"x": (tied, "tok"), "pay": (pay, "late")},
        {"moments": ((STATE, 2 * W), F32, "all")},
        {"hi": half, "lo": half, "hi2": half, "lo2": half},
        "moments",
        4 * unit,
        begin=moments_begin,
        end=moments_end,
    )
    moments, sin = lax.optimization_barrier((moments, sin))

    gy, gz, r, back, sums, sin = staged(
        norm_body,
        common
        | {"vec": (vec, "all"), "sin": (sin, "near")}
        | bcs
        | {"y": (y, "tok"), "z": (z_gate, "tok"), "go": (grad_out, "tok")}
        | {"moments": (moments, "late")},
        {
            "gy": ((T, W), F32, "tok"),
            "gz": ((T, W), BF16, "tok"),
            "r": ((H, T), F32, "row"),
            "back": ((2 * STATE, 2 * W), BF16, "blocks"),
            "sums": ((8, W), F32, "all"),
            "sin_copy": ((STATE, W), F32, "copy"),
        },
        {
            "gain_acc": ((8, W), F32),
            "acc": state,
            "shi": ((STATE, W), BF16),
            "slo": ((STATE, W), BF16),
            "hi": half,
            "lo": half,
            "rhi": half,
            "rlo": half,
        },
        "norm",
        6 * unit,
        begin=norm_begin,
        end=norm_end,
    )

    got_back = exchange(back)
    gx, u, r, gs, loc = staged(
        local_x_body,
        common
        | eh
        | {
            "vec": (vec, "all"),
            "sin": (sin, "all"),
            "par": (par, "all"),
            "rf": (rf, "row"),
            "r": (r, "row"),
        }
        | bcs
        | masks
        | {"g": (g, "tok"), "gy": (gy, "tok"), "sloc": (sloc, "state")}
        | x,
        {
            "gx": ((T, W), F32, "tok"),
            "u": ((H, T), F32, "row"),
            "rr": ((H, T), F32, "row"),
            "gs": ((T, 2 * STATE), F32, "tok"),
            "loc": ((H, 128), F32, "all"),
        },
        {
            "acc": state,
            "sx": ((H, T), F32),
            "shi": folded,
            "slo": folded,
            "ghi": half,
            "glo": half,
            "xhi": half,
            "xlo": half,
            "rhi": folded,
            "rlo": folded,
        },
        "local_x",
        7 * unit,
        backward=True,
        begin=local_x_begin,
        end=local_x_end,
    )
    gs, got_back = lax.optimization_barrier((gs, got_back))
    behind = scan(
        scan_backward_kernel,
        "scan_backward",
        sds((STATE, W + 256), F32),
        got_back,
        *(through, after, loc, sums, e3, thx),
        out_specs=far,
        scratch_shapes=[pltpu.VMEM((STATE, W + 256), F32), pltpu.SemaphoreType.DMA((2, SEQ))],
    )
    din = exchange(behind)
    gb, gc = staged(
        local_bc_body,
        {"e3": (e3, "all"), "pk": (pk, "row")}
        | bcs
        | masks | {"gy": (gy, "tok"), "xhi": (wxhi, "tok"), "xlo": (wxlo, "tok")}
        | {"gs": (gs, "tok")},
        {"gb": ((T, STATE), F32, "tok"), "gc": ((T, STATE), BF16, "tok")},
        {"ghi": half, "glo": half},
        "local_bc",
        5 * unit,
    )

    gb, din = lax.optimization_barrier((gb, din))
    gbc, din, params = staged(
        final_bc_body,
        {
            "din": (din, "near"),
            "gb": (gb, "tok"),
            "gc": (gc, "tok"),
            "xhi": (xhi, "tok"),
            "xlo": (xlo, "tok"),
        },
        {
            "out": ((T, 2 * STATE), BF16, "tok"),
            "din_copy": ((STATE, W + 256), F32, "copy"),
            "params": ((ROWS, 256), F32, "all"),
        },
        {"dhi": ((STATE, W), BF16), "dlo": ((STATE, W), BF16)},
        "final_bc",
        2 * unit,
        begin=final_begin,
        end=final_bc_end,
    )
    gbc, gx = lax.optimization_barrier((gbc, gx))
    back_bc = lax.all_to_all(
        gbc.reshape(GRP, 128, 2 * STATE), "head", split_axis=0, concat_axis=0, tiled=True
    )
    grad_x, grad_dt, grad_gain, grad_skip, grad_alog, grad_bias = staged(
        final_x_body,
        common
        | eh
        | {
            "din": (din, "all"),
            "sin": (sin, "all"),
            "pay": (pay, "all"),
            "par": (par, "all"),
            "rf": (rf, "row"),
            "r": (r, "row"),
            "u": (u, "row"),
            "params": (params, "all"),
        }
        | bcs
        | {"gx": (gx, "tok")}
        | x,
        {
            "gxo": ((T, W), BF16, "tok"),
            "gdt": ((H, T), F32, "row"),
            "gain": ((1, W), F32, "all"),
            "gskip": ((1, H), F32, "all"),
            "galog": ((1, H), F32, "all"),
            "gbias": ((1, H), F32, "all"),
        },
        {
            "uu": ((H, T), F32),
            "dhi": ((STATE, W), BF16),
            "dlo": ((STATE, W), BF16),
            "rhi": folded,
            "rlo": folded,
        },
        "final_x",
        3 * unit,
        begin=final_begin,
        end=final_x_end,
    )
    grad_b, grad_c = pl.pallas_call(
        unpack_kernel,
        out_shape=(pltpu.HBM((128, GRP * STATE), BF16), pltpu.HBM((128, GRP * STATE), BF16)),
        in_specs=[pl.BlockSpec(memory_space=pltpu.VMEM)],
        out_specs=(far, far),
        scratch_shapes=[pltpu.SemaphoreType.DMA((2, GRP))],
        compiler_params=pltpu.CompilerParams(vmem_limit_bytes=16 * 2**20),
        name="unpack",
    )(pltpu.with_memory_space_constraint(back_bc, pltpu.VMEM))
    grad_gain = grad_gain.reshape(W)
    grad_skip, grad_alog, grad_bias = grad_skip.reshape(H), grad_alog.reshape(H), grad_bias.reshape(H)
    return (grad_x, gz, grad_b, grad_c, grad_dt, grad_alog, grad_bias, grad_skip, grad_gain)


def solution(mesh):
    in_specs = (
        P("seq", "head"),
        P("seq", "head"),
        P(("seq", "head"), None),
        P(("seq", "head"), None),
        P("head", "seq"),
        P("head"),
        P("head"),
        P("head"),
        P("head"),
        P("seq"),
        P("seq", "head"),
    )
    out_specs = (
        P("seq", "head"),
        P("seq", "head"),
        P(("seq", "head"), None),
        P(("seq", "head"), None),
        P("head", "seq"),
        P("head"),
        P("head"),
        P("head"),
        P("head"),
    )
    return jax.shard_map(shard_body, mesh=mesh, in_specs=in_specs, out_specs=out_specs, check_vma=False)
```
